512 devices in a mesh: seq: 16 (over z), etp: 8 (over x, core), exp: 4 (over y).
Axes of the slice: x: 4, y: 4, z: 16, core: 2. Of those that a mesh axis runs over, the one named last changes fastest.
Arguments:
- tokens: bfloat16 [2048, 6144], P('seq', 'etp'), may hold values from -6 to 6
- cotangent: bfloat16 [2048, 6144], P('seq', 'etp'), may hold values from -6 to 6
- experts: int32 [2048, 2], P('seq'), may hold values from 0 to 7, as said below
- route_weight: int32 [2048, 2], P('seq'), may hold values from 4096 to 61440, as said below
- gate_weight: bfloat16 [4, 6144, 8192], P('exp', 'etp', 'seq'), may hold values from -0.078125 to 0.078125
- up_weight: bfloat16 [4, 6144, 8192], P('exp', 'etp', 'seq'), may hold values from -0.078125 to 0.078125
- down_weight: bfloat16 [4, 8192, 6144], P('exp', 'seq', 'etp'), may hold values from -0.0625 to 0.0625
Outputs:
- input_grad: bfloat16 [2048, 6144], P('seq', ('etp', 'exp'))
The draws below stay inside these ranges and needn't reach their ends.
Inputs may be any that keep to these rules, and one draw needn't show every extreme that they name: `experts`: the two entries of a row differ. In each aligned block of 128 rows (the tokens of one index of seq) no expert is named by more than 64 rows. `route_weight`: the two entries of a row sum to 65536.
All inputs are finite; a program needn't handle non-finite values.
Results may differ from the reference program's by a relative error of at most 0.0057.
Values may be sent and summed in bfloat16 or wider, within the bound.
No kernel may reach another device: no remote copies, remote signals or barrier semaphores. Data moves between devices by JAX's collectives and lax.ppermute only.
A program may use at most 64 MiB of HBM per device.

```python
import jax
import jax.numpy as jnp
import numpy as np
from jax import lax

D = 6144
EXPERTS = 8
HIDDEN_SIZE = 8192
TOK_DEV = 128
CAP = 64
TOKENS = 2048
ROWS = 1024
EXP_WIN = 4
N_SEQ = 16


def draw_experts(key, part):
    key = jax.random.fold_in(key, 11)
    block_count = TOKENS // TOK_DEV
    unit_rows = TOK_DEV // 16
    load_tables = jnp.asarray(np.array([[8, 6, 5, 4, 3, 2, 2, 2], [8, 7, 4, 4, 3, 2, 2, 2]]) * unit_rows, dtype=jnp.int32)
    bound_tables = jnp.cumsum(load_tables, axis=1)
    leader_key, rest_key = jax.random.split(key)
    leader = jax.random.randint(leader_key, (), 0, EXP_WIN)
    position = jnp.arange(2 * TOK_DEV, dtype=jnp.int32)

    def one_block(block_key):
        perm_key, order_key, table_key = jax.random.split(block_key, 3)
        shuffled = jax.random.permutation(perm_key, EXPERTS).astype(jnp.int32)
        first_expert = shuffled[0]
        shuffled = jnp.where(shuffled == leader, first_expert, shuffled)
        shuffled = shuffled.at[0].set(leader)
        table_pick = jax.random.randint(table_key, (), 0, 2)
        load_bounds = bound_tables[table_pick]
        load_index = jnp.sum((position[:, None] >= load_bounds[None, :7]).astype(jnp.int32), axis=1)
        listed = shuffled[load_index]
        shuffle = jax.random.permutation(order_key, TOK_DEV).astype(jnp.int32)
        return jnp.stack([listed[shuffle], listed[shuffle + TOK_DEV]], axis=1)
    block_keys = jax.random.split(rest_key, block_count)
    return jax.vmap(one_block)(block_keys).reshape(TOKENS, 2).astype(jnp.int32)


def draw_route_weight(key, part):
    key = jax.random.fold_in(key, 23)
    first_share = jax.random.randint(key, (TOKENS,), 4096, 61441).astype(jnp.int32)
    first_share = first_share.at[0].set(4096)
    return jnp.stack([first_share, 65536 - first_share], axis=1).astype(jnp.int32)


def shard_levels(key, dims, pieces, smallest, largest):
    level = 1.0
    for dim, blocks in pieces:
        draws = jax.random.uniform(jax.random.fold_in(jax.random.fold_in(key, 6), dim), (blocks,), jnp.float32, smallest / len(pieces), largest / len(pieces))
        level = level * jnp.repeat(jnp.exp(draws), dims[dim] // blocks).reshape((-1,) + (1,) * (len(dims) - 1 - dim))
    return level


def gaussian(own_key, extent, scale, reach, shards=(), held_as=jnp.bfloat16):
    result = scale * jax.random.normal(own_key, extent, jnp.float32)
    if shards:
        result = result * shard_levels(own_key, extent, shards, -0.22, 0.18)
    return jnp.clip(result, -reach, reach).astype(held_as)


def setup_inputs(seed: int = 0) -> dict:
    key_of = jax.random.split(jax.random.key(seed), 8)
    return {
        "tokens": gaussian(key_of[0], (TOKENS, D), 1.0, 6.0, ((0, 16), (1, 8))),
        "cotangent": gaussian(key_of[1], (TOKENS, D), 1.0, 6.0, ((0, 16), (1, 8))),
        "experts": draw_experts(jax.random.fold_in(key_of[7], 71), 0),
        "route_weight": draw_route_weight(jax.random.fold_in(key_of[7], 71), 0),
        "gate_weight": gaussian(key_of[4], (EXP_WIN, D, HIDDEN_SIZE), D ** -0.5, 0.078125, ((0, 4), (1, 8), (2, 16))),
        "up_weight": gaussian(key_of[5], (EXP_WIN, D, HIDDEN_SIZE), D ** -0.5, 0.078125, ((0, 4), (1, 8), (2, 16))),
        "down_weight": gaussian(key_of[6], (EXP_WIN, HIDDEN_SIZE, D), HIDDEN_SIZE ** -0.5, 0.0625, ((0, 4), (1, 16), (2, 8))),
    }


unit_scale = 1.0 / 65536.0


def round_half(values):
    rounded = values.astype(jnp.bfloat16)
    rounded = lax.optimization_barrier(rounded)
    return rounded.astype(jnp.float32)


def swiglu_back(gate_sum, up_sum, back_sum):
    sigmoid_gate = jax.nn.sigmoid(gate_sum)
    silu_gate = gate_sum * sigmoid_gate
    grad_up = (back_sum * silu_gate).astype(jnp.bfloat16)
    grad_gate = (back_sum * up_sum * sigmoid_gate * (1.0 + gate_sum * (1.0 - sigmoid_gate))).astype(jnp.bfloat16)
    return grad_gate, grad_up


def reference(tokens, cotangent, experts, route_weight, gate_weight, up_weight, down_weight):
    block_experts = experts.reshape(N_SEQ, TOK_DEV, 2)
    block_weights = route_weight.reshape(N_SEQ, TOK_DEV, 2)
    block_tokens = tokens.astype(jnp.float32).reshape(N_SEQ, TOK_DEV, D)
    block_grads = cotangent.astype(jnp.float32).reshape(N_SEQ, TOK_DEV, D)
    slot_ids = lax.broadcasted_iota(jnp.int32, (N_SEQ, CAP, TOK_DEV), 1)
    total = jnp.zeros((N_SEQ, TOK_DEV, D), jnp.float32)
    highest = lax.Precision.HIGHEST
    for expert_id in range(EXP_WIN):
        named_hit = block_experts == expert_id
        chosen = jnp.any(named_hit, axis=2)
        route_share = jnp.sum(jnp.where(named_hit, block_weights, 0), axis=2).astype(jnp.float32) * unit_scale
        slot_order = (jnp.cumsum(chosen.astype(jnp.int32), axis=1) - 1).astype(jnp.int32)
        slot_table = jnp.where((slot_order[:, None, :] == slot_ids) & chosen[:, None, :], 1.0, 0.0).astype(jnp.float32)
        scaled = round_half(route_share[:, :, None] * block_grads)
        rows_in = jnp.einsum("bct,btd->bcd", slot_table, block_tokens, precision=highest).reshape(ROWS, D)
        rows_grad = jnp.einsum("bct,btd->bcd", slot_table, scaled, precision=highest).reshape(ROWS, D)
        gate_full = gate_weight[expert_id].astype(jnp.float32)
        up_full = up_weight[expert_id].astype(jnp.float32)
        down_full = down_weight[expert_id].astype(jnp.float32)
        gate_sum = jnp.dot(rows_in, gate_full, precision=highest)
        up_sum = jnp.dot(rows_in, up_full, precision=highest)
        back_sum = jnp.einsum("rd,hd->rh", rows_grad, down_full, precision=highest)
        grad_gate, grad_up = swiglu_back(gate_sum, up_sum, back_sum)
        row_grads = jnp.dot(grad_gate, gate_weight[expert_id].T, preferred_element_type=jnp.float32)
        row_grads = row_grads + jnp.dot(grad_up, up_weight[expert_id].T, preferred_element_type=jnp.float32)
        total = total + jnp.einsum("bct,bcd->btd", slot_table, row_grads.reshape(N_SEQ, CAP, D), precision=highest)
    return total.reshape(TOKENS, D).astype(jnp.bfloat16)
```

```python
import jax
import jax.numpy as jnp
from jax import lax
from jax.experimental import pallas as pl
from jax.experimental.pallas import tpu as pltpu
from jax.sharding import Mesh
from jax.sharding import PartitionSpec as P

unit_scale = 1.0 / 65536.0
window = 4
table_rows = 16
bf16 = jnp.bfloat16
f32 = jnp.float32
contract_last = (((1,), (1,)), ((), ()))
contract_first = (((0,), (0,)), ((), ()))
swap_cores = [(0, 1), (1, 0)]
vmem_bytes = 48 * 1024 * 1024


def kernel_call(body, out_shape, n_in, scalars=0):
    vmem = pl.BlockSpec(memory_space=pltpu.VMEM)
    smem = pl.BlockSpec(memory_space=pltpu.SMEM)
    return pl.pallas_call(
        body,
        out_shape=out_shape,
        in_specs=[smem] * scalars + [vmem] * n_in,
        out_specs=vmem,
        compiler_params=pltpu.CompilerParams(vmem_limit_bytes=vmem_bytes),
    )


def slot_map(experts):
    count = experts.shape[0]
    ids = lax.broadcasted_iota(jnp.int32, (window, count), 0)
    named = (experts[:, 0][None, :] == ids) | (experts[:, 1][None, :] == ids)
    before = lax.broadcasted_iota(jnp.int32, (count, count), 0) <= lax.broadcasted_iota(
        jnp.int32, (count, count), 1
    )
    order = jnp.dot(named.astype(bf16), before.astype(bf16), preferred_element_type=f32)
    return jnp.where(named, order - 1.0, -1.0)


def pick_kernel(pay_ref, out_ref):
    blocks, _, cols = pay_ref.shape
    count = pay_ref.shape[1] - table_rows
    part = out_ref.shape[4]
    slot_ids = lax.broadcasted_iota(jnp.int32, (2 * part, count), 0).astype(f32)
    for b in range(blocks):
        table = pay_ref[b, count:, :count].astype(f32)
        select = jnp.concatenate(
            [jnp.where(table[e : e + 1] == slot_ids, 1.0, 0.0) for e in range(window)], axis=0
        ).astype(bf16)
        rows = jnp.dot(select, pay_ref[b, :count, :], preferred_element_type=f32).astype(bf16)
        for e in range(window):
            for core in range(2):
                begin = (2 * e + core) * part
                piece = rows[begin : begin + part]
                for pair in range(2):
                    out_ref[core, e, pair, b] = piece


def joined_kernel(core_ref, x_ref, gate_ref, up_ref, gate_far_ref, up_far_ref, out_ref):
    core = core_ref[0]
    quarter = x_ref.shape[-1]
    hidden = gate_ref.shape[1]
    blocks, _, part, _ = out_ref.shape
    for pair in range(2):
        for m, (near, far) in enumerate(((gate_ref, gate_far_ref), (up_ref, up_far_ref))):
            total = None
            for side, weight in ((core, near), (1 - core, far)):
                for q in range(window):
                    term = jnp.dot(
                        x_ref[side, q, pair],
                        weight[q * quarter : (q + 1) * quarter, :],
                        preferred_element_type=f32,
                    )
                    total = term if total is None else total + term
            out_ref[:, pair, :, m * hidden : (m + 1) * hidden] = total.astype(bf16).reshape(
                blocks, part, hidden
            )


def result_kernel(core_ref, g_ref, gate_ref, up_ref, gate_far_ref, up_far_ref, out_ref):
    core = core_ref[0]
    hidden = gate_ref.shape[1]
    quarter = out_ref.shape[-1]
    blocks, _, part, _ = g_ref.shape
    for pair in range(2):
        grad_gate = g_ref[:, pair, :, :hidden].reshape(blocks * part, hidden)
        grad_up = g_ref[:, pair, :, hidden:].reshape(blocks * part, hidden)
        for side, gate, up in ((core, gate_ref, up_ref), (1 - core, gate_far_ref, up_far_ref)):
            for q in range(window):
                span = slice(q * quarter, (q + 1) * quarter)
                rows = lax.dot_general(
                    grad_gate, gate[span, :], contract_last, preferred_element_type=f32
                ) + lax.dot_general(
                    grad_up, up[span, :], contract_last, preferred_element_type=f32
                )
                out_ref[side, q, pair] = rows.astype(bf16)


def combine_kernel(pay_ref, rows_ref, out_ref):
    blocks, count, cols = out_ref.shape
    part = rows_ref.shape[4]
    slot_ids = lax.broadcasted_iota(jnp.int32, (part, count), 0).astype(f32)
    for b in range(blocks):
        table = pay_ref[b, count:, :count].astype(f32)
        pieces, values = [], []
        for core in range(2):
            for e in range(window):
                hit = jnp.where(table[e : e + 1] == slot_ids + float(core * part), 1.0, 0.0)
                for pair in range(2):
                    pieces.append(hit)
                    values.append(rows_ref[core, e, pair, b])
        select = jnp.concatenate(pieces, axis=0).astype(bf16)
        dense = lax.dot_general(
            select, jnp.concatenate(values, axis=0), contract_first, preferred_element_type=f32
        )
        out_ref[b] = dense.astype(bf16)


def per_device(tokens, cotangent, experts, route_weight, gate_weight, up_weight, down_weight):
    core, expert_id = lax.axis_index("c"), lax.axis_index("y")
    n_high, n_x = lax.axis_size("zh"), lax.axis_size("x")
    group = ("c", "y", "zl")
    count, feats = tokens.shape
    quarter = feats // window
    part = count // 4
    gate, up, down = gate_weight[0], up_weight[0], down_weight[0]
    hidden = gate.shape[1]
    core_id = core.reshape(1).astype(jnp.int32)

    cot_far = lax.ppermute(cotangent, "c", swap_cores)

    table = slot_map(experts)
    own_quarter = lax.dynamic_slice_in_dim(tokens, expert_id * quarter, quarter, axis=1)
    table_pad = jnp.pad(table.astype(bf16), ((0, table_rows - window), (0, quarter - count)))
    pay = jnp.concatenate([own_quarter, table_pad], axis=0)
    pay = lax.all_to_all(
        jnp.broadcast_to(pay[None], (n_high, *pay.shape)), "zh", 0, 0, tiled=True
    )

    share = (
        jnp.sum(jnp.where(experts == expert_id, route_weight, 0), axis=1).astype(f32) * unit_scale
    )
    own_slots = lax.dynamic_slice_in_dim(table, expert_id, 1, axis=0)
    slot_ids = lax.broadcasted_iota(jnp.int32, (part, count), 0) + core * part
    select_half = jnp.where(own_slots == slot_ids.astype(f32), 1.0, 0.0).astype(bf16)
    both = jnp.concatenate([cotangent, cot_far], axis=1)
    scaled = (share[:, None] * both.astype(f32)).astype(bf16)
    picked = jnp.dot(select_half, scaled, preferred_element_type=f32).astype(bf16)
    rows_grad = lax.all_gather(picked, ("zh", "zl"), axis=0, tiled=True)

    gate_far = lax.ppermute(gate, "c", swap_cores)
    up_far = lax.ppermute(up, "c", swap_cores)
    down_far = lax.ppermute(down, "c", swap_cores)

    picks = kernel_call(
        pick_kernel, jax.ShapeDtypeStruct((2, window, 2, n_high, part, quarter), bf16), 1
    )(pay)
    rows_in = lax.all_to_all(
        picks.reshape(4 * window, n_high * part, quarter), group, 0, 0, tiled=True
    ).reshape(2, window, 2, n_high * part, quarter)
    joined = kernel_call(
        joined_kernel, jax.ShapeDtypeStruct((n_high, 2, part, 2 * hidden), bf16), 5, 1
    )(core_id, rows_in, gate, up, gate_far, up_far)
    rows = 2 * n_high * part
    joined = lax.all_to_all(joined.reshape(rows, 2 * hidden), "x", 0, 0, tiled=True)

    back = lax.dot_general(
        rows_grad[:, :feats], down, contract_last, preferred_element_type=f32
    ) + lax.dot_general(rows_grad[:, feats:], down_far, contract_last, preferred_element_type=f32)
    back = lax.all_to_all(back.astype(bf16), "x", 0, 0, tiled=True)

    joined_sum = jnp.sum(joined.reshape(n_x, rows // n_x, 2 * hidden).astype(f32), axis=0)
    back_sum = jnp.sum(back.reshape(n_x, rows // n_x, hidden).astype(f32), axis=0)
    gate_sum, up_sum = joined_sum[:, :hidden], joined_sum[:, hidden:]
    sigmoid_gate = jax.nn.sigmoid(gate_sum)
    grad_up = (back_sum * (gate_sum * sigmoid_gate)).astype(bf16)
    grad_gate = (
        back_sum * up_sum * sigmoid_gate * (1.0 + gate_sum * (1.0 - sigmoid_gate))
    ).astype(bf16)
    grads = jnp.concatenate([grad_gate, grad_up], axis=1)
    grads = lax.all_to_all(
        jnp.broadcast_to(grads[None], (n_x, *grads.shape)), "x", 0, 0, tiled=True
    )

    result = kernel_call(
        result_kernel, jax.ShapeDtypeStruct((2, window, 2, n_high * part, quarter), bf16), 5, 1
    )(core_id, grads.reshape(n_high, 2, part, 2 * hidden), gate, up, gate_far, up_far)
    result = lax.all_to_all(
        result.reshape(4 * window, n_high * part, quarter), group, 0, 0, tiled=True
    )
    dense = kernel_call(
        combine_kernel, jax.ShapeDtypeStruct((n_high, count, quarter), bf16), 2
    )(pay, result.reshape(2, window, 2, n_high, part, quarter))
    dense = lax.all_to_all(dense, "zh", 0, 0, tiled=True)
    return jnp.sum(dense.astype(f32), axis=0).astype(bf16)


def solution(mesh):
    split = Mesh(
        mesh.devices.reshape(mesh.shape["seq"] // 2, 2, mesh.shape["etp"] // 2, 2, -1),
        ("zh", "zl", "x", "c", "y"),
    )
    seq, etp = ("zh", "zl"), ("x", "c")
    placed = (
        P(seq, etp),
        P(seq, etp),
        P(seq, None),
        P(seq, None),
        P("y", etp, seq),
        P("y", etp, seq),
        P("y", seq, etp),
    )
    return jax.shard_map(
        per_device, mesh=split, in_specs=placed, out_specs=P(seq, ("x", "c", "y")), check_vma=False
    )
```

```python
import functools

import jax
import jax.numpy as jnp
from jax import lax
from jax.experimental import pallas as pl
from jax.experimental.pallas import tpu as pltpu
from jax.sharding import Mesh
from jax.sharding import PartitionSpec as P

unit_scale = 1.0 / 65536.0
window = 4
table_rows = 16
block_step = 1024
bf16 = jnp.bfloat16
f32 = jnp.float32
contract_last = (((1,), (1,)), ((), ()))
swap_cores = [(0, 1), (1, 0)]
group = ("c", "zl", "y")
vmem_bytes = 48 * 1024 * 1024


def kernel_call(body, out_shape, n_in, scalars=0):
    vmem = pl.BlockSpec(memory_space=pltpu.VMEM)
    smem = pl.BlockSpec(memory_space=pltpu.SMEM)
    return pl.pallas_call(
        body,
        out_shape=out_shape,
        in_specs=[smem] * scalars + [vmem] * n_in,
        out_specs=jax.tree.map(lambda _: vmem, out_shape),
        compiler_params=pltpu.CompilerParams(vmem_limit_bytes=vmem_bytes),
    )


def slot_map(experts):
    count = experts.shape[0]
    ids = lax.broadcasted_iota(jnp.int32, (window, count), 0)
    named = (experts[:, 0][None, :] == ids) | (experts[:, 1][None, :] == ids)
    before = lax.broadcasted_iota(jnp.int32, (count, count), 0) <= lax.broadcasted_iota(
        jnp.int32, (count, count), 1
    )
    order = jnp.dot(named.astype(bf16), before.astype(bf16), preferred_element_type=f32)
    return jnp.where(named, order - 1.0, -1.0)


def selects(pay_ref, first, blocks, part):
    count = pay_ref.shape[2]
    top = pay_ref.shape[1] - table_rows
    table = jnp.concatenate(
        [
            pay_ref[first + i, top:, :].astype(f32)[:window] + float(i * block_step)
            for i in range(blocks)
        ],
        axis=1,
    )
    row = lax.broadcasted_iota(jnp.int32, (blocks * part, blocks * count), 0)
    slot = (row // part * block_step + row % part).astype(f32)
    return [
        [
            jnp.where(table[e : e + 1] == slot + float(core * part), 1.0, 0.0).astype(bf16)
            for core in range(2)
        ]
        for e in range(window)
    ]


def pick_kernel(pay_ref, out_ref):
    n_blocks, rows, count = pay_ref.shape
    top = rows - table_rows
    part = out_ref.shape[-1] // n_blocks
    blocks = 128 // part
    for first in range(0, n_blocks, blocks):
        dense = jnp.concatenate([pay_ref[first + i, :top, :] for i in range(blocks)], axis=1)
        span = slice(first * part, (first + blocks) * part)
        for e, select in enumerate(selects(pay_ref, first, blocks, part)):
            for core in range(2):
                picked = lax.dot_general(
                    dense, select[core], contract_last, preferred_element_type=f32
                ).astype(bf16)
                out_ref[core, 0, e, :, span] = picked
                out_ref[core, 1, e, :, span] = picked


def pair_kernel(n_x, gate_ref, up_ref, out_ref, flip_ref):
    share = gate_ref.shape[1] // n_x
    for i in range(2 * n_x):
        ref, begin = (gate_ref, up_ref)[i % 2], i // 2 * share
        piece = ref[:, begin : begin + share]
        out_ref[:, i * share : (i + 1) * share] = piece
        flip_ref[i * share : (i + 1) * share, :] = piece.T


def joined_kernel(core_ref, x_ref, near_ref, far_ref, out_ref):
    core = core_ref[0]
    width = x_ref.shape[-1]
    for pair in range(2):
        total = jnp.dot(near_ref[...], x_ref[core, pair], preferred_element_type=f32)
        total += jnp.dot(far_ref[...], x_ref[1 - core, pair], preferred_element_type=f32)
        out_ref[:, pair * width : (pair + 1) * width] = total.astype(bf16)


def back_kernel(rows_ref, near_ref, far_ref, out_ref):
    blocks, _, part, feats = rows_ref.shape
    width = blocks * part
    half = feats // 2
    for pair in range(2):
        rows = rows_ref[:, pair].reshape(width, feats)
        total = lax.dot_general(
            near_ref[...], rows[:, :half], contract_last, preferred_element_type=f32
        )
        total += lax.dot_general(
            far_ref[...], rows[:, half:], contract_last, preferred_element_type=f32
        )
        out_ref[:, pair * width : (pair + 1) * width] = total.astype(bf16)


def grad_kernel(joined_ref, back_ref, out_ref):
    n_x, hidden, _ = back_ref.shape
    gate_sum, up_sum, back_sum = (
        sum(ref[i, begin : begin + hidden, :].astype(f32) for i in range(n_x))
        for ref, begin in ((joined_ref, 0), (joined_ref, hidden), (back_ref, 0))
    )
    sigmoid_gate = jax.nn.sigmoid(gate_sum)
    grad_up = (back_sum * (gate_sum * sigmoid_gate)).astype(bf16)
    grad_gate = (
        back_sum * up_sum * sigmoid_gate * (1.0 + gate_sum * (1.0 - sigmoid_gate))
    ).astype(bf16)
    for i in range(n_x):
        out_ref[i, :hidden, :] = grad_gate
        out_ref[i, hidden:, :] = grad_up


def result_kernel(core_ref, g_ref, near_ref, far_ref, out_ref):
    core = core_ref[0]
    width = out_ref.shape[-1]
    for side, weight in ((core, near_ref), (1 - core, far_ref)):
        rows = jnp.dot(weight[...], g_ref[...], preferred_element_type=f32).astype(bf16)
        for pair in range(2):
            out_ref[side, pair] = rows[:, pair * width : (pair + 1) * width]


def combine_kernel(pay_ref, rows_ref, out_ref):
    n_blocks, quarter, count = out_ref.shape
    part = rows_ref.shape[-1] // n_blocks
    blocks = 128 // part
    for first in range(0, n_blocks, blocks):
        span = slice(first * part, (first + blocks) * part)
        total = None
        for e, select in enumerate(selects(pay_ref, first, blocks, part)):
            values = jnp.concatenate(
                [rows_ref[core, pair, e, :, span] for core in range(2) for pair in range(2)],
                axis=1,
            )
            chosen = jnp.concatenate([select[core] for core in range(2) for _ in range(2)], axis=0)
            term = jnp.dot(values, chosen, preferred_element_type=f32)
            total = term if total is None else total + term
        for i in range(blocks):
            out_ref[first + i] = total[:, i * count : (i + 1) * count].astype(bf16)


def token_path(args):
    pay, gate, up, down, core_id = args
    n_high, n_x = lax.axis_size("zh"), lax.axis_size("x")
    count = pay.shape[1]
    quarter = pay.shape[0] - table_rows
    feats, hidden = gate.shape
    width = n_high * count // 4
    pay = lax.all_to_all(
        jnp.broadcast_to(pay[None], (n_high, *pay.shape)), "zh", 0, 0, tiled=True
    )
    paired, paired_t = kernel_call(
        functools.partial(pair_kernel, n_x),
        (
            jax.ShapeDtypeStruct((feats, 2 * hidden), bf16),
            jax.ShapeDtypeStruct((2 * hidden, feats), bf16),
        ),
        2,
    )(gate, up)
    paired_far = lax.ppermute(paired, "c", swap_cores)
    paired_t_far = lax.ppermute(paired_t, "c", swap_cores)
    down_far = lax.ppermute(down, "c", swap_cores)
    picks = kernel_call(
        pick_kernel, jax.ShapeDtypeStruct((2, 2, window, quarter, width), bf16), 1
    )(pay)
    rows_in = lax.all_to_all(
        picks.reshape(4 * window, quarter, width), group, 0, 0, tiled=True
    ).reshape(2, 2, feats, width)
    joined = kernel_call(
        joined_kernel, jax.ShapeDtypeStruct((2 * hidden, 2 * width), bf16), 3, 1
    )(core_id, rows_in, paired_t, paired_t_far)
    return pay, joined, paired, paired_far, down_far


def per_device(tokens, cotangent, experts, route_weight, gate_weight, up_weight, down_weight):
    core, expert_id = lax.axis_index("c"), lax.axis_index("y")
    n_high, n_x = lax.axis_size("zh"), lax.axis_size("x")
    n_group = 4 * window
    count, feats = tokens.shape
    quarter = feats // window
    part = count // 4
    width = n_high * part
    gate, up, down = gate_weight[0], up_weight[0], down_weight[0]
    hidden = gate.shape[1]
    share_h = hidden // n_x
    core_id = core.reshape(1).astype(jnp.int32)

    cot_far = lax.ppermute(cotangent, "c", swap_cores)
    table = slot_map(experts)
    share = (
        jnp.sum(jnp.where(experts == expert_id, route_weight, 0), axis=1).astype(f32) * unit_scale
    )
    own_slots = lax.dynamic_slice_in_dim(table, expert_id, 1, axis=0)
    slot_ids = lax.broadcasted_iota(jnp.int32, (part, count), 0) + core * part
    select_half = jnp.where(own_slots == slot_ids.astype(f32), 1.0, 0.0).astype(bf16)
    both = jnp.concatenate([cotangent, cot_far], axis=1)
    scaled = (share[:, None] * both.astype(f32)).astype(bf16)
    picked = jnp.dot(select_half, scaled, preferred_element_type=f32).astype(bf16)
    rows_grad = lax.all_gather(picked, ("zh", "zl"), axis=0, tiled=True)

    own_quarter = lax.dynamic_slice_in_dim(tokens, expert_id * quarter, quarter, axis=1)
    table_pad = jnp.pad(table.astype(bf16), ((0, table_rows - window), (0, 0)))
    pay = jnp.concatenate([own_quarter.T, table_pad], axis=0)
    pay, joined, paired, paired_far, down_far = lax.cond(
        route_weight[0, 0] > 0, token_path, token_path, (pay, gate, up, down, core_id)
    )
    joined = lax.all_to_all(
        joined.reshape(n_x, 2 * share_h, 2 * width), "x", 0, 0, tiled=True
    )

    back = kernel_call(back_kernel, jax.ShapeDtypeStruct((hidden, 2 * width), bf16), 3)(
        rows_grad.reshape(n_high, 2, part, 2 * feats), down, down_far
    )
    back = lax.all_to_all(back.reshape(n_x, share_h, 2 * width), "x", 0, 0, tiled=True)

    grads = kernel_call(
        grad_kernel, jax.ShapeDtypeStruct((n_x, 2 * share_h, 2 * width), bf16), 2
    )(joined, back)
    grads = lax.all_to_all(grads, "x", 0, 0, tiled=True).reshape(2 * hidden, 2 * width)

    result = kernel_call(
        result_kernel, jax.ShapeDtypeStruct((2, 2, feats, width), bf16), 3, 1
    )(core_id, grads, paired, paired_far)
    result = lax.all_to_all(
        result.reshape(n_group, quarter, width), group, 0, 0, tiled=True
    )
    dense = kernel_call(
        combine_kernel, jax.ShapeDtypeStruct((n_high, quarter, count), bf16), 2
    )(pay, result.reshape(2, 2, window, quarter, width))
    dense = lax.all_to_all(dense, "zh", 0, 0, tiled=True)
    return jnp.sum(dense.astype(f32), axis=0).astype(bf16).T


def solution(mesh):
    split = Mesh(
        mesh.devices.reshape(mesh.shape["seq"] // 2, 2, mesh.shape["etp"] // 2, 2, -1),
        ("zh", "zl", "x", "c", "y"),
    )
    seq, etp = ("zh", "zl"), ("x", "c")
    placed = (
        P(seq, etp),
        P(seq, etp),
        P(seq, None),
        P(seq, None),
        P("y", etp, seq),
        P("y", etp, seq),
        P("y", seq, etp),
    )
    return jax.shard_map(
        per_device, mesh=split, in_specs=placed, out_specs=P(seq, ("x", "c", "y")), check_vma=False
    )
```

```python
import jax
import jax.numpy as jnp
from jax import lax
from jax.experimental import pallas as pl
from jax.experimental.pallas import tpu as pltpu
from jax.sharding import Mesh
from jax.sharding import PartitionSpec as P

unit_scale = 1.0 / 65536.0
window = 4
block_step = 1024
bf16 = jnp.bfloat16
f32 = jnp.float32
contract_last = (((1,), (1,)), ((), ()))
swap_cores = [(0, 1), (1, 0)]
group = ("c", "zl", "y")
vmem_bytes = 48 * 1024 * 1024


def kernel_call(body, out_shape, n_in, scalars=0):
    vmem = pl.BlockSpec(memory_space=pltpu.VMEM)
    smem = pl.BlockSpec(memory_space=pltpu.SMEM)
    return pl.pallas_call(
        body,
        out_shape=out_shape,
        in_specs=[smem] * scalars + [vmem] * n_in,
        out_specs=jax.tree.map(lambda _: vmem, out_shape),
        compiler_params=pltpu.CompilerParams(vmem_limit_bytes=vmem_bytes),
    )


def prep_kernel(
    place_ref, experts_ref, weight_ref, tok_ref, cot_ref, tok_far_ref, cot_far_ref, out_ref
):
    core, expert_id = place_ref[0], place_ref[1]
    part = out_ref.shape[0]
    count, feats = tok_ref.shape
    first, second = experts_ref[0:1, :], experts_ref[1:2, :]
    ids = lax.broadcasted_iota(jnp.int32, (window, count), 0)
    named = (first == ids) | (second == ids)
    before = lax.broadcasted_iota(jnp.int32, (count, count), 0) <= lax.broadcasted_iota(
        jnp.int32, (count, count), 1
    )
    order = jnp.dot(
        jnp.where(named, 1.0, 0.0).astype(bf16),
        jnp.where(before, 1.0, 0.0).astype(bf16),
        preferred_element_type=f32,
    )
    table = jnp.where(named, order - 1.0, -1.0)
    own = jnp.sum(jnp.where(ids == expert_id, table, 0.0), axis=0, keepdims=True)
    share = (
        jnp.where(first == expert_id, weight_ref[0:1, :], 0)
        + jnp.where(second == expert_id, weight_ref[1:2, :], 0)
    ).astype(f32) * unit_scale
    slot = (lax.broadcasted_iota(jnp.int32, (part, count), 0) + core * part).astype(f32)
    hit = own == slot
    select = jnp.where(hit, 1.0, 0.0).astype(bf16)
    slot_share = jnp.sum(jnp.where(hit, share, 0.0), axis=1, keepdims=True)
    for i, ref in enumerate((tok_ref, tok_far_ref, cot_ref, cot_far_ref)):
        picked = jnp.dot(select, ref[...], preferred_element_type=f32)
        if i >= 2:
            picked = slot_share * picked
        out_ref[:, i * feats : (i + 1) * feats] = picked.astype(bf16)
    out_ref[:, 4 * feats :] = jnp.concatenate(
        [table, jnp.zeros((part - window, count), f32)], axis=0
    ).astype(bf16)


def flip_kernel(in_ref, out_ref):
    out_ref[...] = in_ref[...].T


def products_kernel(
    rows_ref, gate_ref, up_ref, down_ref, gate_far_ref, up_far_ref, down_far_ref, out_ref
):
    feats, hidden = gate_ref.shape
    n_x, share, _ = out_ref.shape
    for m, (begin, near, far) in enumerate(
        ((0, gate_ref, gate_far_ref), (0, up_ref, up_far_ref), (2, down_ref, down_far_ref))
    ):
        total = jnp.dot(
            rows_ref[:, begin * feats : (begin + 1) * feats],
            near[...],
            preferred_element_type=f32,
        )
        total += jnp.dot(
            rows_ref[:, (begin + 1) * feats : (begin + 2) * feats],
            far[...],
            preferred_element_type=f32,
        )
        out_ref[:, :, m * hidden : (m + 1) * hidden] = total.astype(bf16).reshape(
            n_x, share, hidden
        )


def grad_kernel(sums_ref, out_ref):
    n_x, _, width = sums_ref.shape
    hidden = width // 3
    gate_sum, up_sum, back_sum = (
        sum(sums_ref[i, :, m * hidden : (m + 1) * hidden].astype(f32) for i in range(n_x))
        for m in range(3)
    )
    sigmoid_gate = jax.nn.sigmoid(gate_sum)
    grad_up = (back_sum * (gate_sum * sigmoid_gate)).astype(bf16)
    grad_gate = (
        back_sum * up_sum * sigmoid_gate * (1.0 + gate_sum * (1.0 - sigmoid_gate))
    ).astype(bf16)
    for i in range(n_x):
        out_ref[i, :, :hidden] = grad_gate
        out_ref[i, :, hidden:] = grad_up


def result_kernel(core_ref, g_ref, gate_ref, up_ref, gate_far_ref, up_far_ref, out_ref):
    core = core_ref[0]
    blocks, _, part, both = g_ref.shape
    hidden = both // 2
    for pair in range(2):
        grads = g_ref[:, pair].reshape(blocks * part, both)
        for side, gate, up in ((core, gate_ref, up_ref), (1 - core, gate_far_ref, up_far_ref)):
            rows = lax.dot_general(
                gate[...], grads[:, :hidden], contract_last, preferred_element_type=f32
            )
            rows += lax.dot_general(
                up[...], grads[:, hidden:], contract_last, preferred_element_type=f32
            )
            out_ref[side, pair] = rows.astype(bf16)


def combine_kernel(pair_ref, table_ref, rows_ref, out_ref):
    pair_id = pair_ref[0]
    n_blocks, quarter, count = out_ref.shape
    part = rows_ref.shape[-1] // n_blocks
    blocks = 128 // part
    row = lax.broadcasted_iota(jnp.int32, (blocks * part, blocks * count), 0)
    slot = (row // part * block_step + row % part).astype(f32)
    for first in range(0, n_blocks, blocks):
        span = slice(first * part, (first + blocks) * part)
        table = jnp.concatenate(
            [
                table_ref[first + i, pair_id].astype(f32)[:window] + float(i * block_step)
                for i in range(blocks)
            ],
            axis=1,
        )
        total = None
        for e in range(window):
            values, chosen = [], []
            for core in range(2):
                select = jnp.where(
                    table[e : e + 1] == slot + float(core * part), 1.0, 0.0
                ).astype(bf16)
                for pair in range(2):
                    values.append(rows_ref[core, pair, e, :, span])
                    chosen.append(select)
            term = jnp.dot(
                jnp.concatenate(values, axis=1),
                jnp.concatenate(chosen, axis=0),
                preferred_element_type=f32,
            )
            total = term if total is None else total + term
        for i in range(blocks):
            out_ref[first + i] = total[:, i * count : (i + 1) * count].astype(bf16)


def per_device(tokens, cotangent, experts, route_weight, gate_weight, up_weight, down_weight):
    core, expert_id = lax.axis_index("c"), lax.axis_index("y")
    n_high, n_x = lax.axis_size("zh"), lax.axis_size("x")
    n_group = 4 * window
    count, feats = tokens.shape
    quarter = feats // window
    part = count // 4
    width = n_high * part
    gate, up, down = gate_weight[0], up_weight[0], down_weight[0]
    hidden = gate.shape[1]
    core_id = core.reshape(1).astype(jnp.int32)
    pair_id = lax.axis_index("zl").reshape(1).astype(jnp.int32)
    place = jnp.stack([core, expert_id]).astype(jnp.int32)

    tok_far = lax.ppermute(tokens, "c", swap_cores)
    cot_far = lax.ppermute(cotangent, "c", swap_cores)
    picked = kernel_call(
        prep_kernel, jax.ShapeDtypeStruct((part, 4 * feats + count), bf16), 6, 1
    )(place, experts.T, route_weight.T, tokens, cotangent, tok_far, cot_far)
    rows = lax.all_gather(picked, ("zh", "zl"), axis=0, tiled=True)

    down_t = kernel_call(flip_kernel, jax.ShapeDtypeStruct((feats, hidden), bf16), 1)(down)
    gate_far, up_far, down_far = (lax.ppermute(w, "c", swap_cores) for w in (gate, up, down_t))

    sums = kernel_call(
        products_kernel, jax.ShapeDtypeStruct((n_x, 2 * width // n_x, 3 * hidden), bf16), 7
    )(rows, gate, up, down_t, gate_far, up_far, down_far)
    sums = lax.all_to_all(sums, "x", 0, 0, tiled=True)
    grads = kernel_call(
        grad_kernel, jax.ShapeDtypeStruct((n_x, 2 * width // n_x, 2 * hidden), bf16), 1
    )(sums)
    grads = lax.all_to_all(grads, "x", 0, 0, tiled=True)

    result = kernel_call(
        result_kernel, jax.ShapeDtypeStruct((2, 2, feats, width), bf16), 5, 1
    )(core_id, grads.reshape(n_high, 2, part, 2 * hidden), gate, up, gate_far, up_far)
    result = lax.all_to_all(result.reshape(n_group, quarter, width), group, 0, 0, tiled=True)
    dense = kernel_call(
        combine_kernel, jax.ShapeDtypeStruct((n_high, quarter, count), bf16), 2, 1
    )(
        pair_id,
        rows[:, 4 * feats :].reshape(n_high, 2, part, count),
        result.reshape(2, 2, window, quarter, width),
    )
    dense = lax.all_to_all(dense, "zh", 0, 0, tiled=True)
    return jnp.sum(dense.astype(f32), axis=0).astype(bf16).T


def solution(mesh):
    split = Mesh(
        mesh.devices.reshape(mesh.shape["seq"] // 2, 2, mesh.shape["etp"] // 2, 2, -1),
        ("zh", "zl", "x", "c", "y"),
    )
    seq, etp = ("zh", "zl"), ("x", "c")
    placed = (
        P(seq, etp),
        P(seq, etp),
        P(seq, None),
        P(seq, None),
        P("y", etp, seq),
        P("y", etp, seq),
        P("y", seq, etp),
    )
    return jax.shard_map(
        per_device, mesh=split, in_specs=placed, out_specs=P(seq, ("x", "c", "y")), check_vma=False
    )
```

```python
import jax
import jax.numpy as jnp
from jax import lax
from jax.experimental import pallas as pl
from jax.experimental.pallas import tpu as pltpu
from jax.sharding import Mesh
from jax.sharding import PartitionSpec as P

unit_scale = 1.0 / 65536.0
window = 4
table_rows = 16
bf16 = jnp.bfloat16
f32 = jnp.float32
contract_last = (((1,), (1,)), ((), ()))
contract_first = (((0,), (0,)), ((), ()))
vmem_bytes = 56 * 1024 * 1024
blocks_at = ((0, 0), (0, 1), (-1, 0), (1, 0), (-1, 1), (1, 1), (2, 0), (2, 1))


def kernel_call(body, out_shape, spaces, scratch=()):
    return pl.pallas_call(
        body,
        out_shape=out_shape,
        in_specs=[pl.BlockSpec(memory_space=space) for space in spaces],
        out_specs=jax.tree.map(lambda _: pl.BlockSpec(memory_space=pltpu.VMEM), out_shape),
        scratch_shapes=list(scratch),
        compiler_params=pltpu.CompilerParams(vmem_limit_bytes=vmem_bytes),
    )


def prep_kernel(expert_ref, experts_ref, weight_ref, tok_ref, cot_ref, out_ref, table_ref):
    expert_id = expert_ref[0]
    n_dest, both, feats = out_ref.shape
    part = both // 2
    count = tok_ref.shape[0]
    first, second = experts_ref[0:1, :], experts_ref[1:2, :]
    ids = lax.broadcasted_iota(jnp.int32, (window, count), 0)
    named = (first == ids) | (second == ids)
    before = lax.broadcasted_iota(jnp.int32, (count, count), 0) <= lax.broadcasted_iota(
        jnp.int32, (count, count), 1
    )
    order = jnp.dot(
        jnp.where(named, 1.0, 0.0).astype(bf16),
        jnp.where(before, 1.0, 0.0).astype(bf16),
        preferred_element_type=f32,
    )
    table = jnp.where(named, order - 1.0, -1.0)
    own = jnp.sum(jnp.where(ids == expert_id, table, 0.0), axis=0, keepdims=True)
    share = (
        jnp.where(first == expert_id, weight_ref[0:1, :], 0)
        + jnp.where(second == expert_id, weight_ref[1:2, :], 0)
    ).astype(f32) * unit_scale
    slot = lax.broadcasted_iota(jnp.int32, (n_dest * part, count), 0).astype(f32)
    hit = own == slot
    select = jnp.where(hit, 1.0, 0.0).astype(bf16)
    slot_share = jnp.sum(jnp.where(hit, share, 0.0), axis=1, keepdims=True)
    tok = jnp.dot(select, tok_ref[...], preferred_element_type=f32)
    cot = slot_share * jnp.dot(select, cot_ref[...], preferred_element_type=f32)
    for d in range(n_dest):
        span = slice(d * part, (d + 1) * part)
        out_ref[d] = jnp.concatenate([tok[span], cot[span]], axis=0).astype(bf16)
    padded = jnp.concatenate(
        [table, jnp.zeros((table_rows - window, count), f32)], axis=0
    ).astype(bf16)
    for i in range(table_ref.shape[0]):
        table_ref[i] = padded


def weights_kernel(gate_ref, up_ref, down_ref, low_ref, high_ref):
    half = low_ref.shape[1]
    for i, ref in enumerate((low_ref, high_ref)):
        span = slice(i * half, (i + 1) * half)
        ref[0] = gate_ref[span, :]
        ref[1] = up_ref[span, :]
        ref[2] = down_ref[:, span].T


def block_kernel(place_ref, *refs):
    n_w = 2 * len(blocks_at)
    rows_hbm, weights_hbm = refs[0], refs[1 : 1 + n_w]
    out_ref, rows_ref, weights_ref, total_ref, sems = refs[1 + n_w :]
    x, core = place_ref[0], place_ref[1]
    n_z, n_s, both, feats = rows_ref.shape
    n_x = n_s // 2
    _, _, half, hidden = weights_ref.shape[1:]
    copies = [pltpu.make_async_copy(rows_hbm, rows_ref, sems.at[n_w])]
    copies += [
        pltpu.make_async_copy(w, weights_ref.at[i // 2, i % 2], sems.at[i])
        for i, w in enumerate(weights_hbm)
    ]
    for copy in copies:
        copy.start()
    copies[0].wait()

    def source(dx, dc):
        return lax.rem(x + dx + n_x, n_x) * 2 + (1 - core if dc else core)

    for b, (dx, dc) in enumerate(blocks_at):
        copies[1 + 2 * b].wait()
        copies[2 + 2 * b].wait()
        rows = rows_ref[:, source(dx, dc)].reshape(n_z * both, feats)
        for m in range(3):
            span = slice(m * hidden, (m + 1) * hidden)
            term = jnp.dot(rows[:, :half], weights_ref[b, 0, m], preferred_element_type=f32)
            term += jnp.dot(rows[:, half:], weights_ref[b, 1, m], preferred_element_type=f32)
            if b == 0:
                total_ref[:, span] = term
            else:
                total_ref[:, span] += term

    part = both // 2
    gate_sum, up_sum, back_sum = (
        total_ref[:, m * hidden : (m + 1) * hidden]
        .reshape(n_z, both, hidden)[:, begin : begin + part]
        .reshape(n_z * part, hidden)
        for m, begin in ((0, 0), (1, 0), (2, part))
    )
    sigmoid_gate = jax.nn.sigmoid(gate_sum)
    grad_up = (back_sum * (gate_sum * sigmoid_gate)).astype(bf16)
    grad_gate = (
        back_sum * up_sum * sigmoid_gate * (1.0 + gate_sum * (1.0 - sigmoid_gate))
    ).astype(bf16)

    slots = n_z * part
    quarter = feats // window
    for b, (dx, dc) in enumerate(blocks_at):
        s = source(dx, dc)
        for y in range(window):
            side, begin = y * quarter // half, y * quarter % half
            span = slice(begin, begin + quarter)
            rows = lax.dot_general(
                grad_gate, weights_ref[b, side, 0, span], contract_last, preferred_element_type=f32
            ) + lax.dot_general(
                grad_up, weights_ref[b, side, 1, span], contract_last, preferred_element_type=f32
            )
            out_ref[s, y, :slots, :] = rows[:, :128].astype(bf16)
            out_ref[s, y, slots:, :] = jnp.concatenate(
                [rows[: slots // 2, 128:], rows[slots // 2 :, 128:]], axis=1
            ).astype(bf16)


def combine_kernel(table_ref, rows_ref, out_ref):
    n_z, quarter, count = out_ref.shape
    n_d = rows_ref.shape[0]
    part = 64 // n_d
    slots = n_z * part
    rest = quarter - 128
    slot = lax.broadcasted_iota(jnp.int32, (n_d * part, count), 0).astype(f32)
    sources = [(d, e) for e in range(window) for d in range(n_d)]
    for p in range(n_z // 4):
        begin = 2 * part * p
        tails = [
            rows_ref[d, e, slots + begin : slots + begin + 2 * part, :].astype(f32)
            for d, e in sources
        ]
        for upper in range(2):
            at = upper * slots // 2 + begin
            heads = [rows_ref[d, e, at : at + 2 * part, :].astype(f32) for d, e in sources]
            for j in range(2):
                z = upper * n_z // 2 + 2 * p + j
                span = slice(j * part, (j + 1) * part)
                values = jnp.concatenate(
                    [
                        jnp.concatenate([v[span] for v in heads], axis=0),
                        jnp.concatenate([v[span] for v in tails], axis=0),
                    ],
                    axis=1,
                ).astype(bf16)
                table = table_ref[z].astype(f32)
                select = jnp.concatenate(
                    [jnp.where(table[e : e + 1] == slot, 1.0, 0.0) for e in range(window)], axis=0
                ).astype(bf16)
                dense = lax.dot_general(
                    values, select, contract_first, preferred_element_type=f32
                ).astype(bf16)
                out_ref[z, :128, :] = dense[:128]
                out_ref[z, 128:, :] = dense[128 + upper * rest : 128 + (upper + 1) * rest]


def gather_weights(low, high):
    n_x = lax.axis_size("x")
    ahead = [(i, (i + 1) % n_x) for i in range(n_x)]
    behind = [(i, (i - 1) % n_x) for i in range(n_x)]

    def swap(value):
        return lax.ppermute(value, "c", [(0, 1), (1, 0)])

    low_before = lax.ppermute(low, "x", ahead)
    high_after = lax.ppermute(high, "x", behind)
    high_before = lax.ppermute(high, "x", ahead)
    low_after = lax.ppermute(low, "x", behind)
    low_across = lax.ppermute(low_before, "x", ahead)
    high_across = lax.ppermute(high_after, "x", behind)
    near = [(low, high), (low_before, high_before), (low_after, high_after), (low_across, high_across)]
    far = [(swap(a), swap(b)) for a, b in near]
    return [near[0], far[0], near[1], near[2], far[1], far[2], near[3], far[3]]


def per_device(tokens, cotangent, experts, route_weight, gate_weight, up_weight, down_weight):
    n_z = lax.axis_size("zh") * lax.axis_size("zl")
    n_s = lax.axis_size("x") * lax.axis_size("c")
    count, feats = tokens.shape
    quarter = feats // window
    part = count // 2 // n_s
    gate, up, down = gate_weight[0], up_weight[0], down_weight[0]
    hidden = gate.shape[1]
    expert_id = lax.axis_index("y").reshape(1).astype(jnp.int32)
    place = jnp.stack([lax.axis_index("x"), lax.axis_index("c")]).astype(jnp.int32)
    smem, vmem, anywhere = pltpu.SMEM, pltpu.VMEM, pl.ANY

    pieces, tables = kernel_call(
        prep_kernel,
        (
            jax.ShapeDtypeStruct((n_s, 2 * part, feats), bf16),
            jax.ShapeDtypeStruct((n_z, table_rows, count), bf16),
        ),
        [smem] + [vmem] * 4,
    )(expert_id, experts.T, route_weight.T, tokens, cotangent)
    pieces = lax.all_to_all(pieces, ("x", "c"), 0, 0, tiled=True)
    rows = lax.all_gather(
        pieces.reshape(n_s * 2 * part, feats), ("zh", "zl"), axis=0, tiled=True
    ).reshape(n_z, n_s, 2 * part, feats)

    tables, gate, up, down, pieces = lax.optimization_barrier((tables, gate, up, down, pieces))
    low, high = kernel_call(
        weights_kernel,
        (jax.ShapeDtypeStruct((3, feats // 2, hidden), bf16),) * 2,
        [vmem] * 3,
    )(gate, up, down)
    weights = gather_weights(low, high)
    tables = lax.all_to_all(tables, ("zh", "zl"), 0, 0, tiled=True)

    result = kernel_call(
        block_kernel,
        jax.ShapeDtypeStruct((n_s, window, quarter, n_z * part), bf16),
        [smem] + [anywhere] * (1 + 2 * len(blocks_at)),
        [
            pltpu.VMEM((n_z, n_s, 2 * part, feats), bf16),
            pltpu.VMEM((len(blocks_at), 2, 3, feats // 2, hidden), bf16),
            pltpu.VMEM((n_z * 2 * part, 3 * hidden), f32),
            pltpu.SemaphoreType.DMA((2 * len(blocks_at) + 1,)),
        ],
    )(place, rows, *[half for block in weights for half in block])
    result = lax.all_to_all(
        result.reshape(n_s * window, quarter, n_z * part), ("x", "c", "y"), 0, 0, tiled=True
    ).reshape(n_s, window, quarter, n_z * part)
    dense = kernel_call(
        combine_kernel, jax.ShapeDtypeStruct((n_z, quarter, count), bf16), [vmem] * 2
    )(tables, result)
    dense = lax.all_to_all(dense, ("zh", "zl"), 0, 0, tiled=True)
    return jnp.sum(dense.astype(f32), axis=0).astype(bf16).T


def solution(mesh):
    split = Mesh(
        mesh.devices.reshape(mesh.shape["seq"] // 2, 2, mesh.shape["etp"] // 2, 2, -1),
        ("zh", "zl", "x", "c", "y"),
    )
    seq, etp = ("zh", "zl"), ("x", "c")
    placed = (
        P(seq, etp),
        P(seq, etp),
        P(seq, None),
        P(seq, None),
        P("y", etp, seq),
        P("y", etp, seq),
        P("y", seq, etp),
    )
    return jax.shard_map(
        per_device, mesh=split, in_specs=placed, out_specs=P(seq, ("x", "c", "y")), check_vma=False
    )
```

```python
import jax
import jax.numpy as jnp
from jax import lax
from jax.experimental import pallas as pl
from jax.experimental.pallas import tpu as pltpu
from jax.sharding import Mesh
from jax.sharding import PartitionSpec as P

unit_scale = 1.0 / 65536.0
window = 4
table_rows = 16
bf16 = jnp.bfloat16
f32 = jnp.float32
contract_last = (((1,), (1,)), ((), ()))
contract_first = (((0,), (0,)), ((), ()))
vmem_bytes = 56 * 1024 * 1024
blocks_at = ((0, 0), (0, 1), (-1, 0), (1, 0), (-1, 1), (1, 1), (2, 0), (2, 1))


def kernel_call(body, out_shape, spaces, scratch=()):
    return pl.pallas_call(
        body,
        out_shape=out_shape,
        in_specs=[pl.BlockSpec(memory_space=space) for space in spaces],
        out_specs=jax.tree.map(lambda _: pl.BlockSpec(memory_space=pltpu.VMEM), out_shape),
        scratch_shapes=list(scratch),
        compiler_params=pltpu.CompilerParams(vmem_limit_bytes=vmem_bytes),
    )


def prep_kernel(expert_ref, experts_ref, weight_ref, tok_ref, cot_ref, out_ref, table_ref):
    expert_id = expert_ref[0]
    n_dest, both, feats = out_ref.shape
    part = both // 2
    count = tok_ref.shape[0]
    first, second = experts_ref[0:1, :], experts_ref[1:2, :]
    ids = lax.broadcasted_iota(jnp.int32, (window, count), 0)
    named = (first == ids) | (second == ids)
    before = lax.broadcasted_iota(jnp.int32, (count, count), 0) <= lax.broadcasted_iota(
        jnp.int32, (count, count), 1
    )
    order = jnp.dot(
        jnp.where(named, 1.0, 0.0).astype(bf16),
        jnp.where(before, 1.0, 0.0).astype(bf16),
        preferred_element_type=f32,
    )
    table = jnp.where(named, order - 1.0, -1.0)
    own = jnp.sum(jnp.where(ids == expert_id, table, 0.0), axis=0, keepdims=True)
    share = (
        jnp.where(first == expert_id, weight_ref[0:1, :], 0)
        + jnp.where(second == expert_id, weight_ref[1:2, :], 0)
    ).astype(f32) * unit_scale
    slot = lax.broadcasted_iota(jnp.int32, (n_dest * part, count), 0).astype(f32)
    hit = own == slot
    select = jnp.where(hit, 1.0, 0.0).astype(bf16)
    slot_share = jnp.sum(jnp.where(hit, share, 0.0), axis=1, keepdims=True)
    tok = jnp.dot(select, tok_ref[...], preferred_element_type=f32)
    cot = slot_share * jnp.dot(select, cot_ref[...], preferred_element_type=f32)
    for d in range(n_dest):
        span = slice(d * part, (d + 1) * part)
        out_ref[d] = jnp.concatenate([tok[span], cot[span]], axis=0).astype(bf16)
    padded = jnp.concatenate(
        [table, jnp.zeros((table_rows - window, count), f32)], axis=0
    ).astype(bf16)
    for i in range(table_ref.shape[0]):
        table_ref[i] = padded


def weights_kernel(gate_ref, up_ref, down_ref, low_ref, high_ref):
    half = low_ref.shape[1]
    for i, ref in enumerate((low_ref, high_ref)):
        span = slice(i * half, (i + 1) * half)
        ref[0] = gate_ref[span, :]
        ref[1] = up_ref[span, :]
        ref[2] = down_ref[:, span].T


def block_kernel(place_ref, *refs):
    n_w = 2 * len(blocks_at)
    rows_hbm, weights_hbm = refs[0], refs[1 : 1 + n_w]
    out_ref, rows_ref, weights_ref, total_ref, sems = refs[1 + n_w :]
    x, core = place_ref[0], place_ref[1]
    n_z, n_s, both, feats = rows_ref.shape
    n_x = n_s // 2
    _, _, half, hidden = weights_ref.shape[1:]
    part = both // 2
    slots = n_z * part
    copies = [pltpu.make_async_copy(rows_hbm, rows_ref, sems.at[n_w])]
    copies += [
        pltpu.make_async_copy(w, weights_ref.at[i // 2, i % 2], sems.at[i])
        for i, w in enumerate(weights_hbm)
    ]
    for copy in copies:
        copy.start()
    copies[0].wait()

    def source(dx, dc):
        return lax.rem(x + dx + n_x, n_x) * 2 + (1 - core if dc else core)

    for b, (dx, dc) in enumerate(blocks_at):
        copies[1 + 2 * b].wait()
        copies[2 + 2 * b].wait()
        loaded = rows_ref[:, source(dx, dc)].astype(f32)
        tok, cot = (
            loaded[:, begin : begin + part].reshape(slots, feats).astype(bf16)
            for begin in (0, part)
        )
        for m, rows in enumerate((tok, tok, cot)):
            span = slice(m * hidden, (m + 1) * hidden)
            term = jnp.dot(rows[:, :half], weights_ref[b, 0, m], preferred_element_type=f32)
            term += jnp.dot(rows[:, half:], weights_ref[b, 1, m], preferred_element_type=f32)
            if b == 0:
                total_ref[:, span] = term
            else:
                total_ref[:, span] += term

    gate_sum, up_sum, back_sum = (
        jnp.concatenate(
            [
                total_ref[:, m * hidden : (m + 1) * hidden]
                .reshape(n_z // 2, 2, part, hidden)[:, pair]
                .reshape(slots // 2, hidden)
                for pair in range(2)
            ],
            axis=0,
        )
        for m in range(3)
    )
    sigmoid_gate = jax.nn.sigmoid(gate_sum)
    grad_up = (back_sum * (gate_sum * sigmoid_gate)).astype(bf16)
    grad_gate = (
        back_sum * up_sum * sigmoid_gate * (1.0 + gate_sum * (1.0 - sigmoid_gate))
    ).astype(bf16)

    quarter = feats // window
    for b, (dx, dc) in enumerate(blocks_at):
        s = source(dx, dc)
        for y in range(window):
            side, begin = y * quarter // half, y * quarter % half
            span = slice(begin, begin + quarter)
            rows = lax.dot_general(
                grad_gate, weights_ref[b, side, 0, span], contract_last, preferred_element_type=f32
            ) + lax.dot_general(
                grad_up, weights_ref[b, side, 1, span], contract_last, preferred_element_type=f32
            )
            for pair in range(2):
                mine = rows[pair * slots // 2 : (pair + 1) * slots // 2]
                out_ref[s, y, pair, : slots // 2, :] = mine[:, :128].astype(bf16)
                out_ref[s, y, pair, slots // 2 :, :] = jnp.concatenate(
                    [mine[: slots // 4, 128:], mine[slots // 4 :, 128:]], axis=1
                ).astype(bf16)


def combine_kernel(table_ref, rows_ref, out_ref):
    n_blocks, quarter, count = out_ref.shape
    n_d = rows_ref.shape[0]
    part = 64 // n_d
    slots = n_blocks * part
    rest = quarter - 128
    slot = lax.broadcasted_iota(jnp.int32, (n_d * part, count), 0).astype(f32)
    sources = [(d, e, pair) for pair in range(2) for e in range(window) for d in range(n_d)]
    for p in range(n_blocks // 4):
        begin = 2 * part * p
        tails = [
            rows_ref[(*source, slice(slots + begin, slots + begin + 2 * part))].astype(f32)
            for source in sources
        ]
        for upper in range(2):
            at = upper * slots // 2 + begin
            heads = [
                rows_ref[(*source, slice(at, at + 2 * part))].astype(f32) for source in sources
            ]
            for j in range(2):
                block = upper * n_blocks // 2 + 2 * p + j
                span = slice(j * part, (j + 1) * part)
                values = jnp.concatenate(
                    [
                        jnp.concatenate([v[span] for v in heads], axis=0),
                        jnp.concatenate([v[span] for v in tails], axis=0),
                    ],
                    axis=1,
                ).astype(bf16)
                table = table_ref[block].astype(f32)
                select = jnp.concatenate(
                    [jnp.where(table[e : e + 1] == slot, 1.0, 0.0) for e in range(window)] * 2,
                    axis=0,
                ).astype(bf16)
                dense = lax.dot_general(
                    values, select, contract_first, preferred_element_type=f32
                ).astype(bf16)
                out_ref[block, :128, :] = dense[:128]
                out_ref[block, 128:, :] = dense[128 + upper * rest : 128 + (upper + 1) * rest]


def gather_weights(low, high, tables):
    n_x = lax.axis_size("x")
    ahead = [(i, (i + 1) % n_x) for i in range(n_x)]
    behind = [(i, (i - 1) % n_x) for i in range(n_x)]

    def swap(value):
        return lax.ppermute(value, "c", [(0, 1), (1, 0)])

    low_before = lax.ppermute(low, "x", ahead)
    high_after = lax.ppermute(high, "x", behind)
    far = (swap(low), swap(high))
    low_later, high_later, tables, far = lax.optimization_barrier((low, high, tables, far))
    high_before = lax.ppermute(high_later, "x", ahead)
    low_after = lax.ppermute(low_later, "x", behind)
    tables = lax.all_to_all(tables, "zh", 0, 0, tiled=True)
    low_before, high_after, tables = lax.optimization_barrier((low_before, high_after, tables))
    low_across = lax.ppermute(low_before, "x", ahead)
    high_across = lax.ppermute(high_after, "x", behind)
    near = [(low_before, high_before), (low_after, high_after), (low_across, high_across)]
    swapped = [(swap(a), swap(b)) for a, b in near]
    blocks = [(low, high), far, near[0], near[1], swapped[0], swapped[1], near[2], swapped[2]]
    return blocks, tables


def per_device(tokens, cotangent, experts, route_weight, gate_weight, up_weight, down_weight):
    n_high = lax.axis_size("zh")
    n_z = n_high * lax.axis_size("zl")
    n_s = lax.axis_size("x") * lax.axis_size("c")
    count, feats = tokens.shape
    quarter = feats // window
    part = count // 2 // n_s
    gate, up, down = gate_weight[0], up_weight[0], down_weight[0]
    hidden = gate.shape[1]
    expert_id = lax.axis_index("y").reshape(1).astype(jnp.int32)
    place = jnp.stack([lax.axis_index("x"), lax.axis_index("c")]).astype(jnp.int32)
    smem, vmem, anywhere = pltpu.SMEM, pltpu.VMEM, pl.ANY

    pieces, tables = kernel_call(
        prep_kernel,
        (
            jax.ShapeDtypeStruct((n_s, 2 * part, feats), bf16),
            jax.ShapeDtypeStruct((n_high, table_rows, count), bf16),
        ),
        [smem] + [vmem] * 4,
    )(expert_id, experts.T, route_weight.T, tokens, cotangent)
    pieces = lax.all_to_all(pieces, ("x", "c"), 0, 0, tiled=True)
    rows = lax.all_gather(
        pieces.reshape(n_s * 2 * part, feats), ("zh", "zl"), axis=0, tiled=True
    ).reshape(n_z, n_s, 2 * part, feats)

    tables, gate, up, down, pieces = lax.optimization_barrier((tables, gate, up, down, pieces))
    low, high = kernel_call(
        weights_kernel,
        (jax.ShapeDtypeStruct((3, feats // 2, hidden), bf16),) * 2,
        [vmem] * 3,
    )(gate, up, down)
    weights, tables = gather_weights(low, high, tables)

    result = kernel_call(
        block_kernel,
        jax.ShapeDtypeStruct((n_s, window, 2, quarter // 2, n_z * part), bf16),
        [smem] + [anywhere] * (1 + 2 * len(blocks_at)),
        [
            pltpu.VMEM((n_z, n_s, 2 * part, feats), bf16),
            pltpu.VMEM((len(blocks_at), 2, 3, feats // 2, hidden), bf16),
            pltpu.VMEM((n_z * part, 3 * hidden), f32),
            pltpu.SemaphoreType.DMA((2 * len(blocks_at) + 1,)),
        ],
    )(place, rows, *[half for block in weights for half in block])
    shape = result.shape
    result = lax.all_to_all(
        result.reshape(n_s * window * 2, *shape[3:]), ("x", "c", "y", "zl"), 0, 0, tiled=True
    ).reshape(shape)
    dense = kernel_call(
        combine_kernel, jax.ShapeDtypeStruct((n_high, quarter, count), bf16), [vmem] * 2
    )(tables, result)
    dense = lax.all_to_all(dense, "zh", 0, 0, tiled=True)
    return jnp.sum(dense.astype(f32), axis=0).astype(bf16).T


def solution(mesh):
    split = Mesh(
        mesh.devices.reshape(mesh.shape["seq"] // 2, 2, mesh.shape["etp"] // 2, 2, -1),
        ("zh", "zl", "x", "c", "y"),
    )
    seq, etp = ("zh", "zl"), ("x", "c")
    placed = (
        P(seq, etp),
        P(seq, etp),
        P(seq, None),
        P(seq, None),
        P("y", etp, seq),
        P("y", etp, seq),
        P("y", seq, etp),
    )
    return jax.shard_map(
        per_device, mesh=split, in_specs=placed, out_specs=P(seq, ("x", "c", "y")), check_vma=False
    )
```

```python
import jax
import jax.numpy as jnp
from jax import lax
from jax.experimental import pallas as pl
from jax.experimental.pallas import tpu as pltpu
from jax.sharding import Mesh
from jax.sharding import PartitionSpec as P

unit_scale = 1.0 / 65536.0
window = 4
table_rows = 16
bf16 = jnp.bfloat16
f32 = jnp.float32
contract_last = (((1,), (1,)), ((), ()))
contract_first = (((0,), (0,)), ((), ()))
vmem_bytes = 56 * 1024 * 1024
blocks_at = ((0, 0), (0, 1), (-1, 0), (1, 0), (-1, 1), (1, 1), (2, 0), (2, 1))


def kernel_call(body, out_shape, spaces, scratch=()):
    return pl.pallas_call(
        body,
        out_shape=out_shape,
        in_specs=[pl.BlockSpec(memory_space=space) for space in spaces],
        out_specs=jax.tree.map(lambda _: pl.BlockSpec(memory_space=pltpu.VMEM), out_shape),
        scratch_shapes=list(scratch),
        compiler_params=pltpu.CompilerParams(vmem_limit_bytes=vmem_bytes),
    )


def prep_kernel(expert_ref, experts_ref, weight_ref, tok_ref, cot_ref, out_ref, table_ref):
    expert_id = expert_ref[0]
    n_dest, both, feats = out_ref.shape
    part = both // 2
    count = tok_ref.shape[0]
    first, second = experts_ref[0:1, :], experts_ref[1:2, :]
    ids = lax.broadcasted_iota(jnp.int32, (window, count), 0)
    named = (first == ids) | (second == ids)
    before = lax.broadcasted_iota(jnp.int32, (count, count), 0) <= lax.broadcasted_iota(
        jnp.int32, (count, count), 1
    )
    order = jnp.dot(
        jnp.where(named, 1.0, 0.0).astype(bf16),
        jnp.where(before, 1.0, 0.0).astype(bf16),
        preferred_element_type=f32,
    )
    table = jnp.where(named, order - 1.0, -1.0)
    own = jnp.sum(jnp.where(ids == expert_id, table, 0.0), axis=0, keepdims=True)
    share = (
        jnp.where(first == expert_id, weight_ref[0:1, :], 0)
        + jnp.where(second == expert_id, weight_ref[1:2, :], 0)
    ).astype(f32) * unit_scale
    slot = lax.broadcasted_iota(jnp.int32, (n_dest * part, count), 0).astype(f32)
    hit = own == slot
    select = jnp.where(hit, 1.0, 0.0).astype(bf16)
    slot_share = jnp.sum(jnp.where(hit, share, 0.0), axis=1, keepdims=True)
    tok = jnp.dot(select, tok_ref[...], preferred_element_type=f32)
    cot = slot_share * jnp.dot(select, cot_ref[...], preferred_element_type=f32)
    for d in range(n_dest):
        span = slice(d * part, (d + 1) * part)
        out_ref[d] = jnp.concatenate([tok[span], cot[span]], axis=0).astype(bf16)
    padded = jnp.concatenate(
        [table, jnp.zeros((table_rows - window, count), f32)], axis=0
    ).astype(bf16)
    for i in range(table_ref.shape[0]):
        table_ref[i] = padded


def weights_kernel(gate_ref, up_ref, down_ref, low_ref, high_ref):
    half = low_ref.shape[1]
    for i, ref in enumerate((low_ref, high_ref)):
        span = slice(i * half, (i + 1) * half)
        ref[0] = gate_ref[span, :]
        ref[1] = up_ref[span, :]
        ref[2] = down_ref[:, span].T


def block_kernel(place_ref, *refs):
    n_w = 2 * len(blocks_at)
    rows_hbm, weights_hbm = refs[0], refs[1 : 1 + n_w]
    out_ref, rows_ref, weights_ref, total_ref, sems = refs[1 + n_w :]
    x, core = place_ref[0], place_ref[1]
    n_z, n_s, both, feats = rows_ref.shape
    n_x = n_s // 2
    _, _, half, hidden = weights_ref.shape[1:]
    part = both // 2
    slots = n_z * part
    copies = [pltpu.make_async_copy(rows_hbm, rows_ref, sems.at[n_w])]
    copies += [
        pltpu.make_async_copy(w, weights_ref.at[i // 2, i % 2], sems.at[i])
        for i, w in enumerate(weights_hbm)
    ]
    for copy in copies:
        copy.start()
    copies[0].wait()

    def source(dx, dc):
        return lax.rem(x + dx + n_x, n_x) * 2 + (1 - core if dc else core)

    for b, (dx, dc) in enumerate(blocks_at):
        copies[1 + 2 * b].wait()
        copies[2 + 2 * b].wait()
        loaded = rows_ref[:, source(dx, dc)].astype(f32)
        tok, cot = (
            loaded[:, begin : begin + part].reshape(slots, feats).astype(bf16)
            for begin in (0, part)
        )
        for m, rows in enumerate((tok, tok, cot)):
            span = slice(m * hidden, (m + 1) * hidden)
            term = jnp.dot(rows[:, :half], weights_ref[b, 0, m], preferred_element_type=f32)
            term += jnp.dot(rows[:, half:], weights_ref[b, 1, m], preferred_element_type=f32)
            if b == 0:
                total_ref[:, span] = term
            else:
                total_ref[:, span] += term

    gate_sum, up_sum, back_sum = (
        jnp.concatenate(
            [
                total_ref[:, m * hidden : (m + 1) * hidden]
                .reshape(n_z // 2, 2, part, hidden)[:, pair]
                .reshape(slots // 2, hidden)
                for pair in range(2)
            ],
            axis=0,
        )
        for m in range(3)
    )
    sigmoid_gate = jax.nn.sigmoid(gate_sum)
    grad_up = (back_sum * (gate_sum * sigmoid_gate)).astype(bf16)
    grad_gate = (
        back_sum * up_sum * sigmoid_gate * (1.0 + gate_sum * (1.0 - sigmoid_gate))
    ).astype(bf16)

    quarter = feats // window
    for b, (dx, dc) in enumerate(blocks_at):
        s = source(dx, dc)
        for y in range(window):
            side, begin = y * quarter // half, y * quarter % half
            span = slice(begin, begin + quarter)
            rows = lax.dot_general(
                grad_gate, weights_ref[b, side, 0, span], contract_last, preferred_element_type=f32
            ) + lax.dot_general(
                grad_up, weights_ref[b, side, 1, span], contract_last, preferred_element_type=f32
            )
            for pair in range(2):
                mine = rows[pair * slots // 2 : (pair + 1) * slots // 2]
                out_ref[s, y, pair, : slots // 2, :] = mine[:, :128].astype(bf16)
                out_ref[s, y, pair, slots // 2 :, :] = jnp.concatenate(
                    [mine[: slots // 4, 128:], mine[slots // 4 :, 128:]], axis=1
                ).astype(bf16)


def combine_kernel(table_ref, rows_ref, out_ref):
    n_blocks, quarter, count = out_ref.shape
    n_d = rows_ref.shape[0]
    part = 64 // n_d
    slots = n_blocks * part
    rest = quarter - 128
    slot = lax.broadcasted_iota(jnp.int32, (n_d * part, count), 0).astype(f32)
    sources = [(d, e, pair) for pair in range(2) for e in range(window) for d in range(n_d)]
    for p in range(n_blocks // 4):
        begin = 2 * part * p
        tails = [
            rows_ref[(*source, slice(slots + begin, slots + begin + 2 * part))].astype(f32)
            for source in sources
        ]
        for upper in range(2):
            at = upper * slots // 2 + begin
            heads = [
                rows_ref[(*source, slice(at, at + 2 * part))].astype(f32) for source in sources
            ]
            for j in range(2):
                block = upper * n_blocks // 2 + 2 * p + j
                span = slice(j * part, (j + 1) * part)
                values = jnp.concatenate(
                    [
                        jnp.concatenate([v[span] for v in heads], axis=0),
                        jnp.concatenate([v[span] for v in tails], axis=0),
                    ],
                    axis=1,
                ).astype(bf16)
                table = table_ref[block].astype(f32)
                select = jnp.concatenate(
                    [jnp.where(table[e : e + 1] == slot, 1.0, 0.0) for e in range(window)] * 2,
                    axis=0,
                ).astype(bf16)
                dense = lax.dot_general(
                    values, select, contract_first, preferred_element_type=f32
                ).astype(bf16)
                out_ref[block, :128, :] = dense[:128]
                out_ref[block, 128:, :] = dense[128 + upper * rest : 128 + (upper + 1) * rest]


def swap(value):
    return lax.ppermute(value, "c", [(0, 1), (1, 0)])


def gather_weights(low, high, tables):
    n_x = lax.axis_size("x")
    ahead = [(i, (i + 1) % n_x) for i in range(n_x)]
    behind = [(i, (i - 1) % n_x) for i in range(n_x)]
    low_before = lax.ppermute(low, "x", ahead)
    high_after = lax.ppermute(high, "x", behind)
    far = (swap(low), swap(high))
    low_later, high_later, far = lax.optimization_barrier((low, high, far))
    high_before = lax.ppermute(high_later, "x", ahead)
    low_after = lax.ppermute(low_later, "x", behind)
    low_across = lax.ppermute(low_before, "x", ahead)
    high_across = lax.ppermute(high_after, "x", behind)
    tables, low_before, high_after = lax.optimization_barrier((tables, low_before, high_after))
    tables = lax.all_to_all(tables, "zh", 0, 0, tiled=True)
    tables, high_before, low_after = lax.optimization_barrier((tables, high_before, low_after))
    near = [(low_before, high_before), (low_after, high_after), (low_across, high_across)]
    swapped = [(swap(a), swap(b)) for a, b in near]
    blocks = [(low, high), far, near[0], near[1], swapped[0], swapped[1], near[2], swapped[2]]
    return blocks, tables


def per_device(tokens, cotangent, experts, route_weight, gate_weight, up_weight, down_weight):
    n_high = lax.axis_size("zh")
    n_z = n_high * lax.axis_size("zl")
    n_s = lax.axis_size("x") * lax.axis_size("c")
    count, feats = tokens.shape
    quarter = feats // window
    part = count // 2 // n_s
    gate, up, down = gate_weight[0], up_weight[0], down_weight[0]
    hidden = gate.shape[1]
    expert_id = lax.axis_index("y").reshape(1).astype(jnp.int32)
    place = jnp.stack([lax.axis_index("x"), lax.axis_index("c")]).astype(jnp.int32)
    smem, vmem, anywhere = pltpu.SMEM, pltpu.VMEM, pl.ANY

    pieces, tables = kernel_call(
        prep_kernel,
        (
            jax.ShapeDtypeStruct((n_s, 2 * part, feats), bf16),
            jax.ShapeDtypeStruct((n_high, table_rows, count), bf16),
        ),
        [smem] + [vmem] * 4,
    )(expert_id, experts.T, route_weight.T, tokens, cotangent)
    gate, up, down, pieces = lax.optimization_barrier((gate, up, down, pieces))
    pieces = lax.all_to_all(pieces, ("x", "c"), 0, 0, tiled=True)
    low, high = kernel_call(
        weights_kernel,
        (jax.ShapeDtypeStruct((3, feats // 2, hidden), bf16),) * 2,
        [vmem] * 3,
    )(gate, up, down)
    pieces, low, high, tables = lax.optimization_barrier((pieces, low, high, tables))
    rows = lax.all_gather(
        pieces.reshape(n_s * 2 * part, feats), ("zh", "zl"), axis=0, tiled=True
    ).reshape(n_z, n_s, 2 * part, feats)

    weights, tables = gather_weights(low, high, tables)

    result = kernel_call(
        block_kernel,
        jax.ShapeDtypeStruct((n_s, window, 2, quarter // 2, n_z * part), bf16),
        [smem] + [anywhere] * (1 + 2 * len(blocks_at)),
        [
            pltpu.VMEM((n_z, n_s, 2 * part, feats), bf16),
            pltpu.VMEM((len(blocks_at), 2, 3, feats // 2, hidden), bf16),
            pltpu.VMEM((n_z * part, 3 * hidden), f32),
            pltpu.SemaphoreType.DMA((2 * len(blocks_at) + 1,)),
        ],
    )(place, rows, *[half for block in weights for half in block])
    shape = result.shape
    result = lax.all_to_all(
        result.reshape(n_s * window * 2, *shape[3:]), ("x", "c", "y", "zl"), 0, 0, tiled=True
    ).reshape(shape)
    dense = kernel_call(
        combine_kernel, jax.ShapeDtypeStruct((n_high, quarter, count), bf16), [vmem] * 2
    )(tables, result)
    dense = lax.all_to_all(dense, "zh", 0, 0, tiled=True)
    return jnp.sum(dense.astype(f32), axis=0).astype(bf16).T


def solution(mesh):
    split = Mesh(
        mesh.devices.reshape(mesh.shape["seq"] // 2, 2, mesh.shape["etp"] // 2, 2, -1),
        ("zh", "zl", "x", "c", "y"),
    )
    seq, etp = ("zh", "zl"), ("x", "c")
    placed = (
        P(seq, etp),
        P(seq, etp),
        P(seq, None),
        P(seq, None),
        P("y", etp, seq),
        P("y", etp, seq),
        P("y", seq, etp),
    )
    return jax.shard_map(
        per_device, mesh=split, in_specs=placed, out_specs=P(seq, ("x", "c", "y")), check_vma=False
    )
```

```python
import jax
import jax.numpy as jnp
from jax import lax
from jax.experimental import pallas as pl
from jax.experimental.pallas import tpu as pltpu
from jax.sharding import Mesh
from jax.sharding import PartitionSpec as P

unit_scale = 1.0 / 65536.0
window = 4
table_rows = 16
bf16 = jnp.bfloat16
f32 = jnp.float32
contract_last = (((1,), (1,)), ((), ()))
contract_first = (((0,), (0,)), ((), ()))
vmem_bytes = 56 * 1024 * 1024
blocks_at = ((0, 0), (0, 1), (-1, 0), (1, 0), (-1, 1), (1, 1), (2, 0), (2, 1))


def kernel_call(body, out_shape, spaces, scratch=()):
    return pl.pallas_call(
        body,
        out_shape=out_shape,
        in_specs=[pl.BlockSpec(memory_space=space) for space in spaces],
        out_specs=jax.tree.map(lambda _: pl.BlockSpec(memory_space=pltpu.VMEM), out_shape),
        scratch_shapes=list(scratch),
        compiler_params=pltpu.CompilerParams(vmem_limit_bytes=vmem_bytes),
    )


def prep_kernel(
    place_ref,
    experts_ref,
    weight_ref,
    tok_ref,
    cot_ref,
    tok_out_ref,
    keep_ref,
    send_ref,
    table_ref,
):
    expert_id, core = place_ref[0], place_ref[1]
    n_dest, both, half = tok_out_ref.shape
    part = both // 2
    count = tok_ref.shape[0]
    first, second = experts_ref[0:1, :], experts_ref[1:2, :]
    ids = lax.broadcasted_iota(jnp.int32, (window, count), 0)
    named = (first == ids) | (second == ids)
    before = lax.broadcasted_iota(jnp.int32, (count, count), 0) <= lax.broadcasted_iota(
        jnp.int32, (count, count), 1
    )
    order = jnp.dot(
        jnp.where(named, 1.0, 0.0).astype(bf16),
        jnp.where(before, 1.0, 0.0).astype(bf16),
        preferred_element_type=f32,
    )
    table = jnp.where(named, order - 1.0, -1.0)
    own = jnp.sum(jnp.where(ids == expert_id, table, 0.0), axis=0, keepdims=True)
    share = (
        jnp.where(first == expert_id, weight_ref[0:1, :], 0)
        + jnp.where(second == expert_id, weight_ref[1:2, :], 0)
    ).astype(f32) * unit_scale
    slot = lax.broadcasted_iota(jnp.int32, (n_dest * part, count), 0).astype(f32)
    hit = own == slot
    select = jnp.where(hit, 1.0, 0.0).astype(bf16)
    slot_share = jnp.sum(jnp.where(hit, share, 0.0), axis=1, keepdims=True)
    tok = jnp.dot(select, tok_ref[...], preferred_element_type=f32)
    cot = slot_share * jnp.dot(select, cot_ref[...], preferred_element_type=f32)
    for d in range(n_dest):
        rows = tok[d * part : (d + 1) * part]
        tok_out_ref[d] = jnp.concatenate([rows[:, :half], rows[:, half:]], axis=0).astype(bf16)
    sets = [
        jnp.concatenate(
            [cot[d * part : (d + 1) * part] for d in range(side, n_dest, 2)], axis=0
        )
        for side in range(2)
    ]
    mine = jnp.where(core == 0, sets[0], sets[1]).astype(bf16)
    other = jnp.where(core == 0, sets[1], sets[0]).astype(bf16)
    for h in range(2):
        keep_ref[h] = mine[:, h * half : (h + 1) * half]
        send_ref[h] = other[:, h * half : (h + 1) * half]
    padded = jnp.concatenate(
        [table, jnp.zeros((table_rows - window, count), f32)], axis=0
    ).astype(bf16)
    for i in range(table_ref.shape[0]):
        table_ref[i] = padded


def weights_kernel(gate_ref, up_ref, down_ref, low_ref, high_ref, flip_ref):
    half = low_ref.shape[1]
    for i, ref in enumerate((low_ref, high_ref)):
        span = slice(i * half, (i + 1) * half)
        ref[0] = gate_ref[span, :]
        ref[1] = up_ref[span, :]
        flip_ref[span, :] = down_ref[:, span].T


def source(place_ref, n_x, dx, dc):
    x, core = place_ref[0], place_ref[1]
    return lax.rem(x + dx + n_x, n_x) * 2 + (1 - core if dc else core)


def back_kernel(rows_hbm, down_ref, down_far_ref, out_ref, rows_ref, sem):
    n_x, slots, hidden = out_ref.shape
    n_z, _, sub, half = rows_ref.shape
    per_z = 2 * sub
    copy = pltpu.make_async_copy(rows_hbm.at[:, pl.ds(8, 8)], rows_ref, sem)
    copy.start()
    copy.wait()
    total = None
    for side, weight in enumerate((down_ref, down_far_ref)):
        for h in range(2):
            at = 4 * side + 2 * h
            rows = rows_ref[:, at : at + 2].reshape(n_z * per_z, half)
            term = jnp.dot(
                rows, weight[h * half : (h + 1) * half, :], preferred_element_type=f32
            )
            total = term if total is None else total + term
    total = total.reshape(n_z, n_x, slots // n_z, hidden)
    for i in range(n_x):
        out_ref[i] = total[:, i].reshape(slots, hidden).astype(bf16)


def start_weights(weights_hbm, weights_ref, sems):
    copies = [
        pltpu.make_async_copy(w, weights_ref.at[i // 2, i % 2], sems.at[i])
        for i, w in enumerate(weights_hbm)
    ]
    for copy in copies:
        copy.start()
    return copies


def products_kernel(place_ref, *refs):
    n_w = 2 * len(blocks_at)
    rows_hbm, weights_hbm = refs[0], refs[1 : 1 + n_w]
    total_ref, rows_ref, weights_ref, sems = refs[1 + n_w :]
    n_z, n_s, both, half = rows_ref.shape
    part = both // 2
    hidden = weights_ref.shape[-1]
    rows_copy = pltpu.make_async_copy(rows_hbm.at[:, pl.ds(0, n_s)], rows_ref, sems.at[n_w])
    rows_copy.start()
    copies = start_weights(weights_hbm, weights_ref, sems)
    rows_copy.wait()
    for b, (dx, dc) in enumerate(blocks_at):
        copies[2 * b].wait()
        copies[2 * b + 1].wait()
        loaded = rows_ref[:, source(place_ref, n_s // 2, dx, dc)].astype(f32)
        low, high = (
            loaded[:, begin : begin + part].reshape(n_z * part, half).astype(bf16)
            for begin in (0, part)
        )
        for m in range(2):
            span = slice(m * hidden, (m + 1) * hidden)
            term = jnp.dot(low, weights_ref[b, 0, m], preferred_element_type=f32)
            term += jnp.dot(high, weights_ref[b, 1, m], preferred_element_type=f32)
            if b == 0:
                total_ref[:, span] = term
            else:
                total_ref[:, span] += term


def result_kernel(place_ref, *refs):
    n_w = 2 * len(blocks_at)
    sums_ref, back_ref, weights_hbm = refs[0], refs[1], refs[2 : 2 + n_w]
    out_ref, weights_ref, sems = refs[2 + n_w :]
    n_x, slots, hidden = back_ref.shape
    half = weights_ref.shape[3]
    n_z = slots // 8
    copies = start_weights(weights_hbm, weights_ref, sems)

    back = sum(back_ref[i].astype(f32) for i in range(n_x))
    gate_sum, up_sum, back_sum = (
        jnp.concatenate(
            [
                value.reshape(n_z // 2, 2, 8, hidden)[:, pair].reshape(slots // 2, hidden)
                for pair in range(2)
            ],
            axis=0,
        )
        for value in (sums_ref[:, :hidden], sums_ref[:, hidden:], back)
    )
    sigmoid_gate = jax.nn.sigmoid(gate_sum)
    grad_up = (back_sum * (gate_sum * sigmoid_gate)).astype(bf16)
    grad_gate = (
        back_sum * up_sum * sigmoid_gate * (1.0 + gate_sum * (1.0 - sigmoid_gate))
    ).astype(bf16)

    quarter = 2 * half // window
    for b, (dx, dc) in enumerate(blocks_at):
        s = source(place_ref, n_x, dx, dc)
        copies[2 * b].wait()
        copies[2 * b + 1].wait()
        for y in range(window):
            side, begin = y * quarter // half, y * quarter % half
            span = slice(begin, begin + quarter)
            rows = lax.dot_general(
                grad_gate, weights_ref[b, side, 0, span], contract_last, preferred_element_type=f32
            ) + lax.dot_general(
                grad_up, weights_ref[b, side, 1, span], contract_last, preferred_element_type=f32
            )
            for pair in range(2):
                mine = rows[pair * slots // 2 : (pair + 1) * slots // 2]
                out_ref[s, y, pair, : slots // 2, :] = mine[:, :128].astype(bf16)
                out_ref[s, y, pair, slots // 2 :, :] = jnp.concatenate(
                    [mine[: slots // 4, 128:], mine[slots // 4 :, 128:]], axis=1
                ).astype(bf16)


def combine_kernel(table_ref, rows_ref, out_ref):
    n_blocks, quarter, count = out_ref.shape
    n_d = rows_ref.shape[0]
    part = 64 // n_d
    slots = n_blocks * part
    rest = quarter - 128
    slot = lax.broadcasted_iota(jnp.int32, (n_d * part, count), 0).astype(f32)
    sources = [(d, e, pair) for pair in range(2) for e in range(window) for d in range(n_d)]
    for p in range(n_blocks // 4):
        begin = 2 * part * p
        tails = [
            rows_ref[(*source, slice(slots + begin, slots + begin + 2 * part))].astype(f32)
            for source in sources
        ]
        for upper in range(2):
            at = upper * slots // 2 + begin
            heads = [
                rows_ref[(*source, slice(at, at + 2 * part))].astype(f32) for source in sources
            ]
            for j in range(2):
                block = upper * n_blocks // 2 + 2 * p + j
                span = slice(j * part, (j + 1) * part)
                values = jnp.concatenate(
                    [
                        jnp.concatenate([v[span] for v in heads], axis=0),
                        jnp.concatenate([v[span] for v in tails], axis=0),
                    ],
                    axis=1,
                ).astype(bf16)
                table = table_ref[block].astype(f32)
                select = jnp.concatenate(
                    [jnp.where(table[e : e + 1] == slot, 1.0, 0.0) for e in range(window)] * 2,
                    axis=0,
                ).astype(bf16)
                dense = lax.dot_general(
                    values, select, contract_first, preferred_element_type=f32
                ).astype(bf16)
                out_ref[block, :128, :] = dense[:128]
                out_ref[block, 128:, :] = dense[128 + upper * rest : 128 + (upper + 1) * rest]


def swap(value):
    return lax.ppermute(value, "c", [(0, 1), (1, 0)])


def gather_weights(low, high, tables):
    n_x = lax.axis_size("x")
    ahead = [(i, (i + 1) % n_x) for i in range(n_x)]
    behind = [(i, (i - 1) % n_x) for i in range(n_x)]
    low_before = lax.ppermute(low, "x", ahead)
    high_after = lax.ppermute(high, "x", behind)
    far = (swap(low), swap(high))
    low_later, high_later, far = lax.optimization_barrier((low, high, far))
    high_before = lax.ppermute(high_later, "x", ahead)
    low_after = lax.ppermute(low_later, "x", behind)
    low_across = lax.ppermute(low_before, "x", ahead)
    high_across = lax.ppermute(high_after, "x", behind)
    tables, low_before, high_after = lax.optimization_barrier((tables, low_before, high_after))
    tables = lax.all_to_all(tables, "zh", 0, 0, tiled=True)
    tables, high_before, low_after = lax.optimization_barrier((tables, high_before, low_after))
    near = [(low_before, high_before), (low_after, high_after), (low_across, high_across)]
    swapped = [(swap(a), swap(b)) for a, b in near]
    blocks = [(low, high), far, near[0], near[1], swapped[0], swapped[1], near[2], swapped[2]]
    return blocks, tables


def per_device(tokens, cotangent, experts, route_weight, gate_weight, up_weight, down_weight):
    n_high = lax.axis_size("zh")
    n_z = n_high * lax.axis_size("zl")
    n_x = lax.axis_size("x")
    n_s = n_x * lax.axis_size("c")
    count, feats = tokens.shape
    quarter = feats // window
    part = count // 2 // n_s
    gate, up, down = gate_weight[0], up_weight[0], down_weight[0]
    hidden = gate.shape[1]
    x, core = lax.axis_index("x"), lax.axis_index("c")
    prep_place = jnp.stack([lax.axis_index("y"), core]).astype(jnp.int32)
    place = jnp.stack([x, core]).astype(jnp.int32)
    smem, vmem, anywhere = pltpu.SMEM, pltpu.VMEM, pl.ANY
    half = feats // 2

    pieces, keep, send, tables = kernel_call(
        prep_kernel,
        (
            jax.ShapeDtypeStruct((n_s, 2 * part, half), bf16),
            jax.ShapeDtypeStruct((2, n_s * part // 2, half), bf16),
            jax.ShapeDtypeStruct((2, n_s * part // 2, half), bf16),
            jax.ShapeDtypeStruct((n_high, table_rows, count), bf16),
        ),
        [smem] + [vmem] * 4,
    )(prep_place, experts.T, route_weight.T, tokens, cotangent)
    gate, up, down, pieces = lax.optimization_barrier((gate, up, down, pieces))
    pieces = lax.all_to_all(pieces, ("x", "c"), 0, 0, tiled=True)
    cot_far = swap(send)
    low, high, down_t = kernel_call(
        weights_kernel,
        (
            jax.ShapeDtypeStruct((2, half, hidden), bf16),
            jax.ShapeDtypeStruct((2, half, hidden), bf16),
            jax.ShapeDtypeStruct((feats, hidden), bf16),
        ),
        [vmem] * 3,
    )(gate, up, down)
    pieces, low, high, down_t, tables = lax.optimization_barrier(
        (pieces, low, high, down_t, tables)
    )
    own = jnp.concatenate([v.reshape(-1, half) for v in (pieces, keep, cot_far)], axis=0)
    rows = lax.all_gather(own, ("zh", "zl"), axis=0, tiled=True).reshape(
        n_z, 2 * n_s, 2 * part, half
    )
    weights, tables = gather_weights(low, high, tables)
    weights = [value for block in weights for value in block]
    down_far = swap(down_t)

    back = kernel_call(
        back_kernel,
        jax.ShapeDtypeStruct((n_x, n_z * part, hidden), bf16),
        [anywhere, vmem, vmem],
        [pltpu.VMEM((n_z, n_s, 2 * part, half), bf16), pltpu.SemaphoreType.DMA],
    )(rows, down_t, down_far)
    back = lax.all_to_all(back, "x", 0, 0, tiled=True)
    sums = kernel_call(
        products_kernel,
        jax.ShapeDtypeStruct((n_z * part, 2 * hidden), f32),
        [smem] + [anywhere] * (1 + len(weights)),
        [
            pltpu.VMEM((n_z, n_s, 2 * part, half), bf16),
            pltpu.VMEM((len(blocks_at), 2, 2, half, hidden), bf16),
            pltpu.SemaphoreType.DMA((len(weights) + 1,)),
        ],
    )(place, rows, *weights)
    result = kernel_call(
        result_kernel,
        jax.ShapeDtypeStruct((n_s, window, 2, quarter // 2, n_z * part), bf16),
        [smem, vmem, vmem] + [anywhere] * len(weights),
        [
            pltpu.VMEM((len(blocks_at), 2, 2, half, hidden), bf16),
            pltpu.SemaphoreType.DMA((len(weights),)),
        ],
    )(place, sums, back, *weights)
    shape = result.shape
    result = lax.all_to_all(
        result.reshape(n_s * window * 2, *shape[3:]), ("x", "c", "y", "zl"), 0, 0, tiled=True
    ).reshape(shape)
    dense = kernel_call(
        combine_kernel, jax.ShapeDtypeStruct((n_high, quarter, count), bf16), [vmem] * 2
    )(tables, result)
    dense = lax.all_to_all(dense, "zh", 0, 0, tiled=True)
    return jnp.sum(dense.astype(f32), axis=0).astype(bf16).T


def solution(mesh):
    split = Mesh(
        mesh.devices.reshape(mesh.shape["seq"] // 2, 2, mesh.shape["etp"] // 2, 2, -1),
        ("zh", "zl", "x", "c", "y"),
    )
    seq, etp = ("zh", "zl"), ("x", "c")
    placed = (
        P(seq, etp),
        P(seq, etp),
        P(seq, None),
        P(seq, None),
        P("y", etp, seq),
        P("y", etp, seq),
        P("y", seq, etp),
    )
    return jax.shard_map(
        per_device, mesh=split, in_specs=placed, out_specs=P(seq, ("x", "c", "y")), check_vma=False
    )
```

```python
import jax
import jax.numpy as jnp
from jax import lax
from jax.experimental import pallas as pl
from jax.experimental.pallas import tpu as pltpu
from jax.sharding import Mesh
from jax.sharding import PartitionSpec as P

unit_scale = 1.0 / 65536.0
window = 4
table_rows = 16
bf16 = jnp.bfloat16
f32 = jnp.float32
contract_last = (((1,), (1,)), ((), ()))
contract_first = (((0,), (0,)), ((), ()))
vmem_bytes = 56 * 1024 * 1024
small_vmem_bytes = 16 * 1024 * 1024
blocks_at = ((0, 0), (0, 1), (-1, 0), (1, 0), (-1, 1), (1, 1), (2, 0), (2, 1))


def kernel_call(
    body, out_shape, spaces, scratch=(), out_space=pltpu.VMEM, vmem_limit=vmem_bytes
):
    return pl.pallas_call(
        body,
        out_shape=out_shape,
        in_specs=[pl.BlockSpec(memory_space=space) for space in spaces],
        out_specs=jax.tree.map(lambda _: pl.BlockSpec(memory_space=out_space), out_shape),
        scratch_shapes=list(scratch),
        compiler_params=pltpu.CompilerParams(vmem_limit_bytes=vmem_limit),
    )


def prep_kernel(
    expert_ref,
    core_ref,
    experts_ref,
    weight_ref,
    tok_ref,
    cot_ref,
    tok_out_ref,
    keep_ref,
    send_ref,
    table_ref,
):
    expert_id, core = expert_ref[0], core_ref[0]
    n_dest, both, half = tok_out_ref.shape
    part = both // 2
    count = tok_ref.shape[0]
    first, second = experts_ref[0:1, :], experts_ref[1:2, :]
    ids = lax.broadcasted_iota(jnp.int32, (window, count), 0)
    named = (first == ids) | (second == ids)
    before = lax.broadcasted_iota(jnp.int32, (count, count), 0) <= lax.broadcasted_iota(
        jnp.int32, (count, count), 1
    )
    order = jnp.dot(
        jnp.where(named, 1.0, 0.0).astype(bf16),
        jnp.where(before, 1.0, 0.0).astype(bf16),
        preferred_element_type=f32,
    )
    table = jnp.where(named, order - 1.0, -1.0)
    own = jnp.sum(jnp.where(ids == expert_id, table, 0.0), axis=0, keepdims=True)
    share = (
        jnp.where(first == expert_id, weight_ref[0:1, :], 0)
        + jnp.where(second == expert_id, weight_ref[1:2, :], 0)
    ).astype(f32) * unit_scale
    slot = lax.broadcasted_iota(jnp.int32, (n_dest * part, count), 0).astype(f32)
    hit = own == slot
    select = jnp.where(hit, 1.0, 0.0).astype(bf16)
    slot_share = jnp.sum(jnp.where(hit, share, 0.0), axis=1, keepdims=True)
    tok = jnp.dot(select, tok_ref[...], preferred_element_type=f32)
    cot = slot_share * jnp.dot(select, cot_ref[...], preferred_element_type=f32)
    for d in range(n_dest):
        rows = tok[d * part : (d + 1) * part]
        tok_out_ref[d] = jnp.concatenate([rows[:, :half], rows[:, half:]], axis=0).astype(bf16)
    sets = [
        jnp.concatenate(
            [cot[d * part : (d + 1) * part] for d in range(side, n_dest, 2)], axis=0
        )
        for side in range(2)
    ]
    mine = jnp.where(core == 0, sets[0], sets[1]).astype(bf16)
    other = jnp.where(core == 0, sets[1], sets[0]).astype(bf16)
    for h in range(2):
        keep_ref[h] = mine[:, h * half : (h + 1) * half]
        send_ref[h] = other[:, h * half : (h + 1) * half]
    padded = jnp.concatenate([table, jnp.zeros((table_rows - window, count), f32)], axis=0)
    table_ref[...] = jnp.concatenate(
        [padded, jnp.zeros((table_rows, half - count), f32)], axis=1
    ).astype(bf16)


def weights_kernel(gate_ref, up_ref, down_ref, low_ref, high_ref, flip_ref):
    half = low_ref.shape[1]
    for i, ref in enumerate((low_ref, high_ref)):
        span = slice(i * half, (i + 1) * half)
        ref[0] = gate_ref[span, :]
        ref[1] = up_ref[span, :]
        flip_ref[span, :] = down_ref[:, span].T


def source(x_ref, core_ref, n_x, dx, dc):
    x, core = x_ref[0], core_ref[0]
    return lax.rem(x + dx + n_x, n_x) * 2 + (1 - core if dc else core)


def back_kernel(rows_hbm, near_hbm, far_hbm, out_ref, rows_ref, near_ref, far_ref, sems):
    n_x, slots, hidden = out_ref.shape
    n_z, sub, half = rows_ref.shape[1:2] + rows_ref.shape[3:]
    per_z = 2 * sub
    copies = []
    for side, (weight_hbm, weight_ref) in enumerate(((near_hbm, near_ref), (far_hbm, far_ref))):
        at = 8 + 4 * side
        copies.append(
            pltpu.make_async_copy(
                rows_hbm.at[:, pl.ds(at, 4)], rows_ref.at[side], sems.at[2 * side]
            )
        )
        copies.append(pltpu.make_async_copy(weight_hbm, weight_ref, sems.at[2 * side + 1]))
    for copy in copies:
        copy.start()
    total = None
    for side, weight_ref in enumerate((near_ref, far_ref)):
        copies[2 * side].wait()
        copies[2 * side + 1].wait()
        for h in range(2):
            rows = rows_ref[side, :, 2 * h : 2 * h + 2].reshape(n_z * per_z, half)
            term = jnp.dot(
                rows, weight_ref[h * half : (h + 1) * half, :], preferred_element_type=f32
            )
            total = term if total is None else total + term
    total = total.reshape(n_z, n_x, slots // n_z, hidden)
    for i in range(n_x):
        out_ref[i] = total[:, i].reshape(slots, hidden).astype(bf16)


def start_weights(weights_hbm, weights_ref, sems):
    copies = [
        pltpu.make_async_copy(w, weights_ref.at[i // 2, i % 2], sems.at[i])
        for i, w in enumerate(weights_hbm)
    ]
    for copy in copies:
        copy.start()
    return copies


def products_kernel(x_ref, core_ref, *refs):
    n_w = 2 * len(blocks_at)
    rows_hbm, weights_hbm = refs[0], refs[1 : 1 + n_w]
    total_ref, rows_ref, weights_ref, sems = refs[1 + n_w :]
    n_z, n_s, both, half = rows_ref.shape
    part = both // 2
    hidden = weights_ref.shape[-1]
    rows_copy = pltpu.make_async_copy(rows_hbm.at[:, pl.ds(0, n_s)], rows_ref, sems.at[n_w])
    rows_copy.start()
    copies = start_weights(weights_hbm, weights_ref, sems)
    rows_copy.wait()
    for b, (dx, dc) in enumerate(blocks_at):
        copies[2 * b].wait()
        copies[2 * b + 1].wait()
        loaded = rows_ref[:, source(x_ref, core_ref, n_s // 2, dx, dc)].astype(f32)
        low, high = (
            loaded[:, begin : begin + part].reshape(n_z * part, half).astype(bf16)
            for begin in (0, part)
        )
        for m in range(2):
            span = slice(m * hidden, (m + 1) * hidden)
            term = jnp.dot(low, weights_ref[b, 0, m], preferred_element_type=f32)
            term += jnp.dot(high, weights_ref[b, 1, m], preferred_element_type=f32)
            if b == 0:
                total_ref[:, span] = term
            else:
                total_ref[:, span] += term


def result_kernel(x_ref, core_ref, *refs):
    n_w = 2 * len(blocks_at)
    sums_hbm, back_hbm, weights_hbm = refs[0], refs[1], refs[2 : 2 + n_w]
    out_hbm, sums_ref, back_ref, weights_ref, out_ref, sems, out_sems = refs[2 + n_w :]
    n_x, slots, hidden = back_ref.shape
    half = weights_ref.shape[3]
    n_z = slots // 8
    sums_copy = pltpu.make_async_copy(sums_hbm, sums_ref, sems.at[n_w])
    back_copy = pltpu.make_async_copy(back_hbm, back_ref, sems.at[n_w + 1])
    sums_copy.start()
    back_copy.start()
    copies = start_weights(weights_hbm, weights_ref, sems)
    sums_copy.wait()
    back_copy.wait()

    back = sum(back_ref[i].astype(f32) for i in range(n_x))
    gate_sum, up_sum, back_sum = (
        jnp.concatenate(
            [
                value.reshape(n_z // 2, 2, 8, hidden)[:, pair].reshape(slots // 2, hidden)
                for pair in range(2)
            ],
            axis=0,
        )
        for value in (sums_ref[:, :hidden], sums_ref[:, hidden:], back)
    )
    sigmoid_gate = jax.nn.sigmoid(gate_sum)
    grad_up = (back_sum * (gate_sum * sigmoid_gate)).astype(bf16)
    grad_gate = (
        back_sum * up_sum * sigmoid_gate * (1.0 + gate_sum * (1.0 - sigmoid_gate))
    ).astype(bf16)

    quarter = 2 * half // window
    sent = []
    for b, (dx, dc) in enumerate(blocks_at):
        s = source(x_ref, core_ref, n_x, dx, dc)
        copies[2 * b].wait()
        copies[2 * b + 1].wait()
        for y in range(window):
            side, begin = y * quarter // half, y * quarter % half
            span = slice(begin, begin + quarter)
            rows = lax.dot_general(
                grad_gate, weights_ref[b, side, 0, span], contract_last, preferred_element_type=f32
            ) + lax.dot_general(
                grad_up, weights_ref[b, side, 1, span], contract_last, preferred_element_type=f32
            )
            for pair in range(2):
                mine = rows[pair * slots // 2 : (pair + 1) * slots // 2]
                out_ref[s, y, pair, : slots // 2, :] = mine[:, :128].astype(bf16)
                out_ref[s, y, pair, slots // 2 :, :] = jnp.concatenate(
                    [mine[: slots // 4, 128:], mine[slots // 4 :, 128:]], axis=1
                ).astype(bf16)
        sent.append(pltpu.make_async_copy(out_ref.at[s], out_hbm.at[s], out_sems.at[b]))
        sent[-1].start()
    for copy in sent:
        copy.wait()


def combine_kernel(table_ref, rows_ref, out_ref):
    n_blocks, quarter, count = out_ref.shape
    n_d = rows_ref.shape[0]
    part = 64 // n_d
    slots = n_blocks * part
    rest = quarter - 128
    slot = lax.broadcasted_iota(jnp.int32, (n_d * part, count), 0).astype(f32)
    sources = [(d, e, pair) for pair in range(2) for e in range(window) for d in range(n_d)]
    for p in range(n_blocks // 4):
        begin = 2 * part * p
        tails = [
            rows_ref[(*source, slice(slots + begin, slots + begin + 2 * part))].astype(f32)
            for source in sources
        ]
        for upper in range(2):
            at = upper * slots // 2 + begin
            heads = [
                rows_ref[(*source, slice(at, at + 2 * part))].astype(f32) for source in sources
            ]
            for j in range(2):
                block = upper * n_blocks // 2 + 2 * p + j
                span = slice(j * part, (j + 1) * part)
                values = jnp.concatenate(
                    [
                        jnp.concatenate([v[span] for v in heads], axis=0),
                        jnp.concatenate([v[span] for v in tails], axis=0),
                    ],
                    axis=1,
                ).astype(bf16)
                table = table_ref[block].astype(f32)
                select = jnp.concatenate(
                    [jnp.where(table[e : e + 1] == slot, 1.0, 0.0) for e in range(window)] * 2,
                    axis=0,
                ).astype(bf16)
                dense = lax.dot_general(
                    values, select, contract_first, preferred_element_type=f32
                ).astype(bf16)
                out_ref[block, :128, :] = dense[:128]
                out_ref[block, 128:, :] = dense[128 + upper * rest : 128 + (upper + 1) * rest]


def swap(value):
    return lax.ppermute(value, "c", [(0, 1), (1, 0)])


def gather_weights(low, high):
    n_x = lax.axis_size("x")
    ahead = [(i, (i + 1) % n_x) for i in range(n_x)]
    behind = [(i, (i - 1) % n_x) for i in range(n_x)]
    low_before = lax.ppermute(low, "x", ahead)
    high_after = lax.ppermute(high, "x", behind)
    far = (swap(low), swap(high))
    low_later, high_later, far = lax.optimization_barrier((low, high, far))
    high_before = lax.ppermute(high_later, "x", ahead)
    low_after = lax.ppermute(low_later, "x", behind)
    low_across = lax.ppermute(low_before, "x", ahead)
    high_across = lax.ppermute(high_after, "x", behind)
    near = [(low_before, high_before), (low_after, high_after), (low_across, high_across)]
    swapped = [(swap(a), swap(b)) for a, b in near]
    blocks = [(low, high), far, near[0], near[1], swapped[0], swapped[1], near[2], swapped[2]]
    return blocks


def per_device(tokens, cotangent, experts, route_weight, gate_weight, up_weight, down_weight):
    n_high = lax.axis_size("zh")
    n_z = n_high * lax.axis_size("zl")
    n_x = lax.axis_size("x")
    n_s = n_x * lax.axis_size("c")
    count, feats = tokens.shape
    quarter = feats // window
    part = count // 2 // n_s
    gate, up, down = gate_weight[0], up_weight[0], down_weight[0]
    hidden = gate.shape[1]
    x, core, expert_id = (
        lax.axis_index(name).reshape(1).astype(jnp.int32) for name in ("x", "c", "y")
    )
    smem, vmem, anywhere = pltpu.SMEM, pltpu.VMEM, pl.ANY
    half = feats // 2
    groups = 2 * n_s + 1

    pieces, keep, send, table = kernel_call(
        prep_kernel,
        (
            jax.ShapeDtypeStruct((n_s, 2 * part, half), bf16),
            jax.ShapeDtypeStruct((2, n_s * part // 2, half), bf16),
            jax.ShapeDtypeStruct((2, n_s * part // 2, half), bf16),
            jax.ShapeDtypeStruct((table_rows, half), bf16),
        ),
        [smem] * 2 + [vmem] * 4,
    )(expert_id, core, experts.T, route_weight.T, tokens, cotangent)
    pieces = lax.all_to_all(pieces, ("x", "c"), 0, 0, tiled=True)
    own = jnp.concatenate([v.reshape(-1, half) for v in (pieces, keep, swap(send), table)], axis=0)
    gate, up, down, own = lax.optimization_barrier((gate, up, down, own))
    rows = lax.all_gather(own, ("zh", "zl"), axis=0, tiled=True).reshape(
        n_z, groups, 2 * part, half
    )

    low, high, down_t = kernel_call(
        weights_kernel,
        (
            jax.ShapeDtypeStruct((2, half, hidden), bf16),
            jax.ShapeDtypeStruct((2, half, hidden), bf16),
            jax.ShapeDtypeStruct((feats, hidden), bf16),
        ),
        [vmem] * 3,
    )(gate, up, down)
    weights = [value for block in gather_weights(low, high) for value in block]
    down_far = swap(down_t)

    back = kernel_call(
        back_kernel,
        jax.ShapeDtypeStruct((n_x, n_z * part, hidden), bf16),
        [anywhere] * 3,
        [
            pltpu.VMEM((2, n_z, n_s // 2, 2 * part, half), bf16),
            pltpu.VMEM((feats, hidden), bf16),
            pltpu.VMEM((feats, hidden), bf16),
            pltpu.SemaphoreType.DMA((4,)),
        ],
    )(rows, down_t, down_far)
    back = lax.all_to_all(back, "x", 0, 0, tiled=True)
    sums = kernel_call(
        products_kernel,
        jax.ShapeDtypeStruct((n_z * part, 2 * hidden), f32),
        [smem] * 2 + [anywhere] * (1 + len(weights)),
        [
            pltpu.VMEM((n_z, n_s, 2 * part, half), bf16),
            pltpu.VMEM((len(blocks_at), 2, 2, half, hidden), bf16),
            pltpu.SemaphoreType.DMA((len(weights) + 1,)),
        ],
    )(x, core, rows, *weights)
    result_shape = (n_s, window, 2, quarter // 2, n_z * part)
    result = kernel_call(
        result_kernel,
        jax.ShapeDtypeStruct(result_shape, bf16),
        [smem] * 2 + [anywhere] * (2 + len(weights)),
        [
            pltpu.VMEM((n_z * part, 2 * hidden), f32),
            pltpu.VMEM((n_x, n_z * part, hidden), bf16),
            pltpu.VMEM((len(blocks_at), 2, 2, half, hidden), bf16),
            pltpu.VMEM(result_shape, bf16),
            pltpu.SemaphoreType.DMA((len(weights) + 2,)),
            pltpu.SemaphoreType.DMA((len(blocks_at),)),
        ],
        anywhere,
    )(x, core, sums, back, *weights)
    tables = lax.dynamic_index_in_dim(
        rows.reshape(n_high, 2, groups, 2 * part, half)[:, :, groups - 1, :, :count],
        lax.axis_index("zl"),
        axis=1,
        keepdims=False,
    )
    shape = result.shape
    result = lax.all_to_all(
        result.reshape(n_s * window * 2, *shape[3:]), ("x", "c", "y", "zl"), 0, 0, tiled=True
    ).reshape(shape)
    dense = kernel_call(
        combine_kernel,
        jax.ShapeDtypeStruct((n_high, quarter, count), bf16),
        [vmem] * 2,
        vmem_limit=small_vmem_bytes,
    )(tables, result)
    dense = lax.all_to_all(dense, "zh", 0, 0, tiled=True)
    return jnp.sum(dense.astype(f32), axis=0).astype(bf16).T


def solution(mesh):
    split = Mesh(
        mesh.devices.reshape(mesh.shape["seq"] // 2, 2, mesh.shape["etp"] // 2, 2, -1),
        ("zh", "zl", "x", "c", "y"),
    )
    seq, etp = ("zh", "zl"), ("x", "c")
    placed = (
        P(seq, etp),
        P(seq, etp),
        P(seq, None),
        P(seq, None),
        P("y", etp, seq),
        P("y", etp, seq),
        P("y", seq, etp),
    )
    return jax.shard_map(
        per_device, mesh=split, in_specs=placed, out_specs=P(seq, ("x", "c", "y")), check_vma=False
    )
```

```python
import jax
import jax.numpy as jnp
from jax import lax
from jax.experimental import pallas as pl
from jax.experimental.pallas import tpu as pltpu
from jax.sharding import Mesh
from jax.sharding import PartitionSpec as P

unit_scale = 1.0 / 65536.0
window = 4
table_rows = 16
bf16 = jnp.bfloat16
f32 = jnp.float32
contract_last = (((1,), (1,)), ((), ()))
contract_first = (((0,), (0,)), ((), ()))
vmem_bytes = 56 * 1024 * 1024
small_vmem_bytes = 16 * 1024 * 1024
blocks_at = ((0, 0), (0, 1), (-1, 0), (1, 0), (-1, 1), (1, 1), (2, 0), (2, 1))


def kernel_call(
    body, out_shape, spaces, scratch=(), out_space=pltpu.VMEM, vmem_limit=vmem_bytes
):
    return pl.pallas_call(
        body,
        out_shape=out_shape,
        in_specs=[pl.BlockSpec(memory_space=space) for space in spaces],
        out_specs=jax.tree.map(lambda _: pl.BlockSpec(memory_space=out_space), out_shape),
        scratch_shapes=list(scratch),
        compiler_params=pltpu.CompilerParams(vmem_limit_bytes=vmem_limit),
    )


def prep_kernel(
    expert_ref,
    core_ref,
    experts_ref,
    weight_ref,
    tok_ref,
    cot_ref,
    tok_out_ref,
    keep_ref,
    send_ref,
    table_ref,
):
    expert_id, core = expert_ref[0], core_ref[0]
    n_dest, both, half = tok_out_ref.shape
    part = both // 2
    count = tok_ref.shape[0]
    first, second = experts_ref[0:1, :], experts_ref[1:2, :]
    ids = lax.broadcasted_iota(jnp.int32, (window, count), 0)
    named = (first == ids) | (second == ids)
    before = lax.broadcasted_iota(jnp.int32, (count, count), 0) <= lax.broadcasted_iota(
        jnp.int32, (count, count), 1
    )
    order = jnp.dot(
        jnp.where(named, 1.0, 0.0).astype(bf16),
        jnp.where(before, 1.0, 0.0).astype(bf16),
        preferred_element_type=f32,
    )
    table = jnp.where(named, order - 1.0, -1.0)
    own = jnp.sum(jnp.where(ids == expert_id, table, 0.0), axis=0, keepdims=True)
    share = (
        jnp.where(first == expert_id, weight_ref[0:1, :], 0)
        + jnp.where(second == expert_id, weight_ref[1:2, :], 0)
    ).astype(f32) * unit_scale
    slot = lax.broadcasted_iota(jnp.int32, (n_dest * part, count), 0).astype(f32)
    hit = own == slot
    select = jnp.where(hit, 1.0, 0.0).astype(bf16)
    slot_share = jnp.sum(jnp.where(hit, share, 0.0), axis=1, keepdims=True)
    tok = jnp.dot(select, tok_ref[...], preferred_element_type=f32)
    cot = slot_share * jnp.dot(select, cot_ref[...], preferred_element_type=f32)
    for d in range(n_dest):
        rows = tok[d * part : (d + 1) * part]
        tok_out_ref[d] = jnp.concatenate([rows[:, :half], rows[:, half:]], axis=0).astype(bf16)
    sets = [
        jnp.concatenate(
            [cot[d * part : (d + 1) * part] for d in range(side, n_dest, 2)], axis=0
        )
        for side in range(2)
    ]
    mine = jnp.where(core == 0, sets[0], sets[1]).astype(bf16)
    other = jnp.where(core == 0, sets[1], sets[0]).astype(bf16)
    for h in range(2):
        keep_ref[h] = mine[:, h * half : (h + 1) * half]
        send_ref[h] = other[:, h * half : (h + 1) * half]
    padded = jnp.concatenate([table, jnp.zeros((table_rows - window, count), f32)], axis=0)
    table_ref[...] = jnp.concatenate(
        [padded, jnp.zeros((table_rows, half - count), f32)], axis=1
    ).astype(bf16)


def pack_kernel(tok_ref, keep_ref, far_ref, table_ref, out_ref):
    n_dest, rows, half = tok_ref.shape
    out_ref[:n_dest] = tok_ref[...]
    for i, ref in enumerate((keep_ref, far_ref)):
        begin = n_dest + i * n_dest // 2
        out_ref[begin : begin + n_dest // 2] = ref[...].reshape(n_dest // 2, rows, half)
    out_ref[2 * n_dest] = table_ref[...]


def weights_kernel(gate_ref, up_ref, down_ref, low_ref, high_ref, flip_ref):
    half = low_ref.shape[1]
    for i, ref in enumerate((low_ref, high_ref)):
        span = slice(i * half, (i + 1) * half)
        ref[0] = gate_ref[span, :]
        ref[1] = up_ref[span, :]
        flip_ref[span, :] = down_ref[:, span].T


def source(x_ref, core_ref, n_x, dx, dc):
    x, core = x_ref[0], core_ref[0]
    return lax.rem(x + dx + n_x, n_x) * 2 + (1 - core if dc else core)


def back_kernel(rows_hbm, near_hbm, far_hbm, out_ref, rows_ref, near_ref, far_ref, sems):
    n_x, slots, hidden = out_ref.shape
    n_z, sub, half = rows_ref.shape[1:2] + rows_ref.shape[3:]
    per_z = 2 * sub
    copies = []
    for side, (weight_hbm, weight_ref) in enumerate(((near_hbm, near_ref), (far_hbm, far_ref))):
        at = 8 + 4 * side
        copies.append(
            pltpu.make_async_copy(
                rows_hbm.at[:, pl.ds(at, 4)], rows_ref.at[side], sems.at[2 * side]
            )
        )
        copies.append(pltpu.make_async_copy(weight_hbm, weight_ref, sems.at[2 * side + 1]))
    for copy in copies:
        copy.start()
    total = None
    for side, weight_ref in enumerate((near_ref, far_ref)):
        copies[2 * side].wait()
        copies[2 * side + 1].wait()
        for h in range(2):
            rows = rows_ref[side, :, 2 * h : 2 * h + 2].reshape(n_z * per_z, half)
            term = jnp.dot(
                rows, weight_ref[h * half : (h + 1) * half, :], preferred_element_type=f32
            )
            total = term if total is None else total + term
    total = total.reshape(n_z, n_x, slots // n_z, hidden)
    for i in range(n_x):
        out_ref[i] = total[:, i].reshape(slots, hidden).astype(bf16)


def start_weights(weights_hbm, weights_ref, sems):
    copies = [
        pltpu.make_async_copy(w, weights_ref.at[i // 2, i % 2], sems.at[i])
        for i, w in enumerate(weights_hbm)
    ]
    for copy in copies:
        copy.start()
    return copies


def products_kernel(x_ref, core_ref, *refs):
    n_w = 2 * len(blocks_at)
    rows_hbm, weights_hbm = refs[0], refs[1 : 1 + n_w]
    total_ref, rows_ref, weights_ref, sems = refs[1 + n_w :]
    n_z, n_s, both, half = rows_ref.shape
    part = both // 2
    hidden = weights_ref.shape[-1]
    rows_copy = pltpu.make_async_copy(rows_hbm.at[:, pl.ds(0, n_s)], rows_ref, sems.at[n_w])
    rows_copy.start()
    copies = start_weights(weights_hbm, weights_ref, sems)
    rows_copy.wait()
    for b, (dx, dc) in enumerate(blocks_at):
        copies[2 * b].wait()
        copies[2 * b + 1].wait()
        loaded = rows_ref[:, source(x_ref, core_ref, n_s // 2, dx, dc)].astype(f32)
        low, high = (
            loaded[:, begin : begin + part].reshape(n_z * part, half).astype(bf16)
            for begin in (0, part)
        )
        for m in range(2):
            span = slice(m * hidden, (m + 1) * hidden)
            term = jnp.dot(low, weights_ref[b, 0, m], preferred_element_type=f32)
            term += jnp.dot(high, weights_ref[b, 1, m], preferred_element_type=f32)
            if b == 0:
                total_ref[:, span] = term
            else:
                total_ref[:, span] += term


def result_kernel(x_ref, core_ref, *refs):
    n_w = 2 * len(blocks_at)
    sums_hbm, back_hbm, weights_hbm = refs[0], refs[1], refs[2 : 2 + n_w]
    out_hbm, sums_ref, back_ref, weights_ref, out_ref, sems, out_sems = refs[2 + n_w :]
    n_x, slots, hidden = back_ref.shape
    half = weights_ref.shape[3]
    n_z = slots // 8
    sums_copy = pltpu.make_async_copy(sums_hbm, sums_ref, sems.at[n_w])
    back_copy = pltpu.make_async_copy(back_hbm, back_ref, sems.at[n_w + 1])
    sums_copy.start()
    back_copy.start()
    copies = start_weights(weights_hbm, weights_ref, sems)
    sums_copy.wait()
    back_copy.wait()

    back = sum(back_ref[i].astype(f32) for i in range(n_x))
    gate_sum, up_sum, back_sum = (
        jnp.concatenate(
            [
                value.reshape(n_z // 2, 2, 8, hidden)[:, pair].reshape(slots // 2, hidden)
                for pair in range(2)
            ],
            axis=0,
        )
        for value in (sums_ref[:, :hidden], sums_ref[:, hidden:], back)
    )
    sigmoid_gate = jax.nn.sigmoid(gate_sum)
    grad_up = (back_sum * (gate_sum * sigmoid_gate)).astype(bf16)
    grad_gate = (
        back_sum * up_sum * sigmoid_gate * (1.0 + gate_sum * (1.0 - sigmoid_gate))
    ).astype(bf16)

    quarter = 2 * half // window
    sent = []
    for b, (dx, dc) in enumerate(blocks_at):
        s = source(x_ref, core_ref, n_x, dx, dc)
        copies[2 * b].wait()
        copies[2 * b + 1].wait()
        for y in range(window):
            side, begin = y * quarter // half, y * quarter % half
            span = slice(begin, begin + quarter)
            rows = lax.dot_general(
                grad_gate, weights_ref[b, side, 0, span], contract_last, preferred_element_type=f32
            ) + lax.dot_general(
                grad_up, weights_ref[b, side, 1, span], contract_last, preferred_element_type=f32
            )
            for pair in range(2):
                mine = rows[pair * slots // 2 : (pair + 1) * slots // 2]
                out_ref[s, y, pair, : slots // 2, :] = mine[:, :128].astype(bf16)
                out_ref[s, y, pair, slots // 2 :, :] = jnp.concatenate(
                    [mine[: slots // 4, 128:], mine[slots // 4 :, 128:]], axis=1
                ).astype(bf16)
        sent.append(pltpu.make_async_copy(out_ref.at[s], out_hbm.at[s], out_sems.at[b]))
        sent[-1].start()
    for copy in sent:
        copy.wait()


def combine_kernel(table_ref, rows_ref, out_ref):
    n_blocks, quarter, count = out_ref.shape
    n_d = rows_ref.shape[0]
    part = 64 // n_d
    slots = n_blocks * part
    rest = quarter - 128
    slot = lax.broadcasted_iota(jnp.int32, (n_d * part, count), 0).astype(f32)
    sources = [(d, e, pair) for pair in range(2) for e in range(window) for d in range(n_d)]
    for p in range(n_blocks // 4):
        begin = 2 * part * p
        tails = [
            rows_ref[(*source, slice(slots + begin, slots + begin + 2 * part))].astype(f32)
            for source in sources
        ]
        for upper in range(2):
            at = upper * slots // 2 + begin
            heads = [
                rows_ref[(*source, slice(at, at + 2 * part))].astype(f32) for source in sources
            ]
            for j in range(2):
                block = upper * n_blocks // 2 + 2 * p + j
                span = slice(j * part, (j + 1) * part)
                values = jnp.concatenate(
                    [
                        jnp.concatenate([v[span] for v in heads], axis=0),
                        jnp.concatenate([v[span] for v in tails], axis=0),
                    ],
                    axis=1,
                ).astype(bf16)
                table = table_ref[block].astype(f32)
                select = jnp.concatenate(
                    [jnp.where(table[e : e + 1] == slot, 1.0, 0.0) for e in range(window)] * 2,
                    axis=0,
                ).astype(bf16)
                dense = lax.dot_general(
                    values, select, contract_first, preferred_element_type=f32
                ).astype(bf16)
                out_ref[block, :128, :] = dense[:128]
                out_ref[block, 128:, :] = dense[128 + upper * rest : 128 + (upper + 1) * rest]


def swap(value):
    return lax.ppermute(value, "c", [(0, 1), (1, 0)])


def gather_weights(low, high):
    n_x = lax.axis_size("x")
    ahead = [(i, (i + 1) % n_x) for i in range(n_x)]
    behind = [(i, (i - 1) % n_x) for i in range(n_x)]
    low_before = lax.ppermute(low, "x", ahead)
    high_after = lax.ppermute(high, "x", behind)
    high_before = lax.ppermute(high, "x", ahead)
    low_after = lax.ppermute(low, "x", behind)
    low_before, high_after, high_before, low_after = lax.optimization_barrier(
        (low_before, high_after, high_before, low_after)
    )
    low_across = lax.ppermute(low_before, "x", ahead)
    high_across = lax.ppermute(high_after, "x", behind)
    far = (swap(low), swap(high))
    near = [(low_before, high_before), (low_after, high_after), (low_across, high_across)]
    swapped = [(swap(a), swap(b)) for a, b in near]
    blocks = [(low, high), far, near[0], near[1], swapped[0], swapped[1], near[2], swapped[2]]
    return blocks


def per_device(tokens, cotangent, experts, route_weight, gate_weight, up_weight, down_weight):
    n_high = lax.axis_size("zh")
    n_z = n_high * lax.axis_size("zl")
    n_x = lax.axis_size("x")
    n_s = n_x * lax.axis_size("c")
    count, feats = tokens.shape
    quarter = feats // window
    part = count // 2 // n_s
    gate, up, down = gate_weight[0], up_weight[0], down_weight[0]
    hidden = gate.shape[1]
    x, core, expert_id = (
        lax.axis_index(name).reshape(1).astype(jnp.int32) for name in ("x", "c", "y")
    )
    smem, vmem, anywhere = pltpu.SMEM, pltpu.VMEM, pl.ANY
    half = feats // 2
    groups = 2 * n_s + 1

    pieces, keep, send, table = kernel_call(
        prep_kernel,
        (
            jax.ShapeDtypeStruct((n_s, 2 * part, half), bf16),
            jax.ShapeDtypeStruct((2, n_s * part // 2, half), bf16),
            jax.ShapeDtypeStruct((2, n_s * part // 2, half), bf16),
            jax.ShapeDtypeStruct((table_rows, half), bf16),
        ),
        [smem] * 2 + [vmem] * 4,
    )(expert_id, core, experts.T, route_weight.T, tokens, cotangent)
    pieces = lax.all_to_all(pieces, ("x", "c"), 0, 0, tiled=True)
    own = kernel_call(
        pack_kernel,
        jax.ShapeDtypeStruct((groups, 2 * part, half), bf16),
        [vmem] * 4,
        vmem_limit=small_vmem_bytes,
    )(pieces, keep, swap(send), table)
    gate, up, down, own = lax.optimization_barrier((gate, up, down, own))
    rows = lax.all_gather(own.reshape(-1, half), ("zh", "zl"), axis=0, tiled=True).reshape(
        n_z, groups, 2 * part, half
    )

    low, high, down_t = kernel_call(
        weights_kernel,
        (
            jax.ShapeDtypeStruct((2, half, hidden), bf16),
            jax.ShapeDtypeStruct((2, half, hidden), bf16),
            jax.ShapeDtypeStruct((feats, hidden), bf16),
        ),
        [vmem] * 3,
    )(gate, up, down)
    weights = [value for block in gather_weights(low, high) for value in block]
    down_far = swap(down_t)

    back = kernel_call(
        back_kernel,
        jax.ShapeDtypeStruct((n_x, n_z * part, hidden), bf16),
        [anywhere] * 3,
        [
            pltpu.VMEM((2, n_z, n_s // 2, 2 * part, half), bf16),
            pltpu.VMEM((feats, hidden), bf16),
            pltpu.VMEM((feats, hidden), bf16),
            pltpu.SemaphoreType.DMA((4,)),
        ],
    )(rows, down_t, down_far)
    back = lax.all_to_all(back, "x", 0, 0, tiled=True)
    sums = kernel_call(
        products_kernel,
        jax.ShapeDtypeStruct((n_z * part, 2 * hidden), f32),
        [smem] * 2 + [anywhere] * (1 + len(weights)),
        [
            pltpu.VMEM((n_z, n_s, 2 * part, half), bf16),
            pltpu.VMEM((len(blocks_at), 2, 2, half, hidden), bf16),
            pltpu.SemaphoreType.DMA((len(weights) + 1,)),
        ],
    )(x, core, rows, *weights)
    result_shape = (n_s, window, 2, quarter // 2, n_z * part)
    result = kernel_call(
        result_kernel,
        jax.ShapeDtypeStruct(result_shape, bf16),
        [smem] * 2 + [anywhere] * (2 + len(weights)),
        [
            pltpu.VMEM((n_z * part, 2 * hidden), f32),
            pltpu.VMEM((n_x, n_z * part, hidden), bf16),
            pltpu.VMEM((len(blocks_at), 2, 2, half, hidden), bf16),
            pltpu.VMEM(result_shape, bf16),
            pltpu.SemaphoreType.DMA((len(weights) + 2,)),
            pltpu.SemaphoreType.DMA((len(blocks_at),)),
        ],
        anywhere,
    )(x, core, sums, back, *weights)
    tables = lax.dynamic_index_in_dim(
        rows.reshape(n_high, 2, groups, 2 * part, half)[:, :, groups - 1, :, :count],
        lax.axis_index("zl"),
        axis=1,
        keepdims=False,
    )
    shape = result.shape
    result = lax.all_to_all(
        result.reshape(n_s * window * 2, *shape[3:]), ("x", "c", "y", "zl"), 0, 0, tiled=True
    ).reshape(shape)
    dense = kernel_call(
        combine_kernel,
        jax.ShapeDtypeStruct((n_high, quarter, count), bf16),
        [vmem] * 2,
        vmem_limit=small_vmem_bytes,
    )(tables, result)
    dense = lax.all_to_all(dense, "zh", 0, 0, tiled=True)
    return jnp.sum(dense.astype(f32), axis=0).astype(bf16).T


def solution(mesh):
    split = Mesh(
        mesh.devices.reshape(mesh.shape["seq"] // 2, 2, mesh.shape["etp"] // 2, 2, -1),
        ("zh", "zl", "x", "c", "y"),
    )
    seq, etp = ("zh", "zl"), ("x", "c")
    placed = (
        P(seq, etp),
        P(seq, etp),
        P(seq, None),
        P(seq, None),
        P("y", etp, seq),
        P("y", etp, seq),
        P("y", seq, etp),
    )
    return jax.shard_map(
        per_device, mesh=split, in_specs=placed, out_specs=P(seq, ("x", "c", "y")), check_vma=False
    )
```

```python
import jax
import jax.numpy as jnp
from jax import lax
from jax.experimental import pallas as pl
from jax.experimental.pallas import tpu as pltpu
from jax.sharding import Mesh
from jax.sharding import PartitionSpec as P

unit_scale = 1.0 / 65536.0
window = 4
table_rows = 16
bf16 = jnp.bfloat16
f32 = jnp.float32
contract_last = (((1,), (1,)), ((), ()))
contract_first = (((0,), (0,)), ((), ()))
vmem_bytes = 56 * 1024 * 1024
small_vmem_bytes = 16 * 1024 * 1024
blocks_at = ((0, 0), (0, 1), (-1, 0), (1, 0), (-1, 1), (1, 1), (2, 0), (2, 1))


def kernel_call(
    body, out_shape, spaces, scratch=(), out_space=pltpu.VMEM, vmem_limit=vmem_bytes
):
    return pl.pallas_call(
        body,
        out_shape=out_shape,
        in_specs=[pl.BlockSpec(memory_space=space) for space in spaces],
        out_specs=jax.tree.map(lambda _: pl.BlockSpec(memory_space=out_space), out_shape),
        scratch_shapes=list(scratch),
        compiler_params=pltpu.CompilerParams(vmem_limit_bytes=vmem_limit),
    )


def prep_kernel(
    expert_ref,
    core_ref,
    experts_ref,
    weight_ref,
    tok_ref,
    cot_ref,
    tok_out_ref,
    keep_ref,
    send_ref,
    table_ref,
):
    expert_id, core = expert_ref[0], core_ref[0]
    n_dest, both, half = tok_out_ref.shape
    part = both // 2
    count = tok_ref.shape[0]
    first, second = experts_ref[0:1, :], experts_ref[1:2, :]
    ids = lax.broadcasted_iota(jnp.int32, (window, count), 0)
    named = (first == ids) | (second == ids)
    before = lax.broadcasted_iota(jnp.int32, (count, count), 0) <= lax.broadcasted_iota(
        jnp.int32, (count, count), 1
    )
    order = jnp.dot(
        jnp.where(named, 1.0, 0.0).astype(bf16),
        jnp.where(before, 1.0, 0.0).astype(bf16),
        preferred_element_type=f32,
    )
    table = jnp.where(named, order - 1.0, -1.0)
    own = jnp.sum(jnp.where(ids == expert_id, table, 0.0), axis=0, keepdims=True)
    share = (
        jnp.where(first == expert_id, weight_ref[0:1, :], 0)
        + jnp.where(second == expert_id, weight_ref[1:2, :], 0)
    ).astype(f32) * unit_scale
    slot = lax.broadcasted_iota(jnp.int32, (n_dest * part, count), 0).astype(f32)
    hit = own == slot
    select = jnp.where(hit, 1.0, 0.0).astype(bf16)
    slot_share = jnp.sum(jnp.where(hit, share, 0.0), axis=1, keepdims=True)
    tok = jnp.dot(select, tok_ref[...], preferred_element_type=f32)
    cot = slot_share * jnp.dot(select, cot_ref[...], preferred_element_type=f32)
    for d in range(n_dest):
        rows = tok[d * part : (d + 1) * part]
        tok_out_ref[d] = jnp.concatenate([rows[:, :half], rows[:, half:]], axis=0).astype(bf16)
    sets = [
        jnp.concatenate(
            [cot[d * part : (d + 1) * part] for d in range(side, n_dest, 2)], axis=0
        )
        for side in range(2)
    ]
    mine = jnp.where(core == 0, sets[0], sets[1]).astype(bf16)
    other = jnp.where(core == 0, sets[1], sets[0]).astype(bf16)
    for h in range(2):
        for i in range(2):
            span = slice(i * both, (i + 1) * both)
            keep_ref[2 * h + i] = mine[span, h * half : (h + 1) * half]
            send_ref[2 * h + i] = other[span, h * half : (h + 1) * half]
    padded = jnp.concatenate([table, jnp.zeros((table_rows - window, count), f32)], axis=0)
    table_ref[0] = jnp.concatenate(
        [padded, jnp.zeros((table_rows, half - count), f32)], axis=1
    ).astype(bf16)


def pack_kernel(tok_ref, keep_ref, far_ref, table_ref, out_ref, sems):
    begin, copies = 0, []
    for i, ref in enumerate((tok_ref, keep_ref, far_ref, table_ref)):
        size = ref.shape[0]
        copies.append(pltpu.make_async_copy(ref, out_ref.at[pl.ds(begin, size)], sems.at[i]))
        copies[-1].start()
        begin += size
    for copy in copies:
        copy.wait()


def weights_kernel(gate_ref, up_ref, down_ref, low_ref, high_ref, flip_ref):
    half = low_ref.shape[1]
    for i, ref in enumerate((low_ref, high_ref)):
        span = slice(i * half, (i + 1) * half)
        ref[0] = gate_ref[span, :]
        ref[1] = up_ref[span, :]
        flip_ref[span, :] = down_ref[:, span].T


def source(x_ref, core_ref, n_x, dx, dc):
    x, core = x_ref[0], core_ref[0]
    return lax.rem(x + dx + n_x, n_x) * 2 + (1 - core if dc else core)


def back_kernel(rows_hbm, near_hbm, far_hbm, out_ref, rows_ref, near_ref, far_ref, sems):
    n_x, slots, hidden = out_ref.shape
    n_z, sub, half = rows_ref.shape[1:2] + rows_ref.shape[3:]
    per_z = 2 * sub
    copies = []
    for side, (weight_hbm, weight_ref) in enumerate(((near_hbm, near_ref), (far_hbm, far_ref))):
        at = 8 + 4 * side
        copies.append(
            pltpu.make_async_copy(
                rows_hbm.at[:, pl.ds(at, 4)], rows_ref.at[side], sems.at[2 * side]
            )
        )
        copies.append(pltpu.make_async_copy(weight_hbm, weight_ref, sems.at[2 * side + 1]))
    for copy in copies:
        copy.start()
    total = None
    for side, weight_ref in enumerate((near_ref, far_ref)):
        copies[2 * side].wait()
        copies[2 * side + 1].wait()
        for h in range(2):
            rows = rows_ref[side, :, 2 * h : 2 * h + 2].reshape(n_z * per_z, half)
            term = jnp.dot(
                rows, weight_ref[h * half : (h + 1) * half, :], preferred_element_type=f32
            )
            total = term if total is None else total + term
    total = total.reshape(n_z, n_x, slots // n_z, hidden)
    for i in range(n_x):
        out_ref[i] = total[:, i].reshape(slots, hidden).astype(bf16)


def start_weights(weights_hbm, weights_ref, sems):
    copies = [
        pltpu.make_async_copy(w, weights_ref.at[i // 2, i % 2], sems.at[i])
        for i, w in enumerate(weights_hbm)
    ]
    for copy in copies:
        copy.start()
    return copies


def products_kernel(x_ref, core_ref, *refs):
    n_w = 2 * len(blocks_at)
    rows_hbm, weights_hbm = refs[0], refs[1 : 1 + n_w]
    total_ref, rows_ref, weights_ref, sems = refs[1 + n_w :]
    n_z, n_s, both, half = rows_ref.shape
    part = both // 2
    hidden = weights_ref.shape[-1]
    rows_copy = pltpu.make_async_copy(rows_hbm.at[:, pl.ds(0, n_s)], rows_ref, sems.at[n_w])
    rows_copy.start()
    copies = start_weights(weights_hbm, weights_ref, sems)
    rows_copy.wait()
    for b, (dx, dc) in enumerate(blocks_at):
        copies[2 * b].wait()
        copies[2 * b + 1].wait()
        loaded = rows_ref[:, source(x_ref, core_ref, n_s // 2, dx, dc)].astype(f32)
        low, high = (
            loaded[:, begin : begin + part].reshape(n_z * part, half).astype(bf16)
            for begin in (0, part)
        )
        for m in range(2):
            span = slice(m * hidden, (m + 1) * hidden)
            term = jnp.dot(low, weights_ref[b, 0, m], preferred_element_type=f32)
            term += jnp.dot(high, weights_ref[b, 1, m], preferred_element_type=f32)
            if b == 0:
                total_ref[:, span] = term
            else:
                total_ref[:, span] += term


def result_kernel(x_ref, core_ref, *refs):
    n_w = 2 * len(blocks_at)
    sums_hbm, back_hbm, weights_hbm = refs[0], refs[1], refs[2 : 2 + n_w]
    out_hbm, sums_ref, back_ref, weights_ref, out_ref, sems, out_sems = refs[2 + n_w :]
    n_x, slots, hidden = back_ref.shape
    half = weights_ref.shape[3]
    n_z = slots // 8
    sums_copy = pltpu.make_async_copy(sums_hbm, sums_ref, sems.at[n_w])
    back_copy = pltpu.make_async_copy(back_hbm, back_ref, sems.at[n_w + 1])
    sums_copy.start()
    back_copy.start()
    copies = start_weights(weights_hbm, weights_ref, sems)
    sums_copy.wait()
    back_copy.wait()

    back = sum(back_ref[i].astype(f32) for i in range(n_x))
    gate_sum, up_sum, back_sum = (
        jnp.concatenate(
            [
                value.reshape(n_z // 2, 2, 8, hidden)[:, pair].reshape(slots // 2, hidden)
                for pair in range(2)
            ],
            axis=0,
        )
        for value in (sums_ref[:, :hidden], sums_ref[:, hidden:], back)
    )
    sigmoid_gate = jax.nn.sigmoid(gate_sum)
    grad_up = (back_sum * (gate_sum * sigmoid_gate)).astype(bf16)
    grad_gate = (
        back_sum * up_sum * sigmoid_gate * (1.0 + gate_sum * (1.0 - sigmoid_gate))
    ).astype(bf16)

    quarter = 2 * half // window
    sent = []
    for b, (dx, dc) in enumerate(blocks_at):
        s = source(x_ref, core_ref, n_x, dx, dc)
        copies[2 * b].wait()
        copies[2 * b + 1].wait()
        for y in range(window):
            side, begin = y * quarter // half, y * quarter % half
            span = slice(begin, begin + quarter)
            rows = lax.dot_general(
                grad_gate, weights_ref[b, side, 0, span], contract_last, preferred_element_type=f32
            ) + lax.dot_general(
                grad_up, weights_ref[b, side, 1, span], contract_last, preferred_element_type=f32
            )
            for pair in range(2):
                mine = rows[pair * slots // 2 : (pair + 1) * slots // 2]
                out_ref[s, y, pair, : slots // 2, :] = mine[:, :128].astype(bf16)
                out_ref[s, y, pair, slots // 2 :, :] = jnp.concatenate(
                    [mine[: slots // 4, 128:], mine[slots // 4 :, 128:]], axis=1
                ).astype(bf16)
        sent.append(pltpu.make_async_copy(out_ref.at[s], out_hbm.at[s], out_sems.at[b]))
        sent[-1].start()
    for copy in sent:
        copy.wait()


def combine_kernel(table_ref, rows_ref, out_ref):
    n_blocks, quarter, count = out_ref.shape
    n_d = rows_ref.shape[0]
    part = 64 // n_d
    slots = n_blocks * part
    rest = quarter - 128
    slot = lax.broadcasted_iota(jnp.int32, (n_d * part, count), 0).astype(f32)
    sources = [(d, e, pair) for pair in range(2) for e in range(window) for d in range(n_d)]
    for p in range(n_blocks // 4):
        begin = 2 * part * p
        tails = [
            rows_ref[(*source, slice(slots + begin, slots + begin + 2 * part))].astype(f32)
            for source in sources
        ]
        for upper in range(2):
            at = upper * slots // 2 + begin
            heads = [
                rows_ref[(*source, slice(at, at + 2 * part))].astype(f32) for source in sources
            ]
            for j in range(2):
                block = upper * n_blocks // 2 + 2 * p + j
                span = slice(j * part, (j + 1) * part)
                values = jnp.concatenate(
                    [
                        jnp.concatenate([v[span] for v in heads], axis=0),
                        jnp.concatenate([v[span] for v in tails], axis=0),
                    ],
                    axis=1,
                ).astype(bf16)
                table = table_ref[block].astype(f32)
                select = jnp.concatenate(
                    [jnp.where(table[e : e + 1] == slot, 1.0, 0.0) for e in range(window)] * 2,
                    axis=0,
                ).astype(bf16)
                dense = lax.dot_general(
                    values, select, contract_first, preferred_element_type=f32
                ).astype(bf16)
                out_ref[block, :128, :] = dense[:128]
                out_ref[block, 128:, :] = dense[128 + upper * rest : 128 + (upper + 1) * rest]


def swap(value):
    return lax.ppermute(value, "c", [(0, 1), (1, 0)])


def gather_weights(low, high):
    n_x = lax.axis_size("x")
    ahead = [(i, (i + 1) % n_x) for i in range(n_x)]
    behind = [(i, (i - 1) % n_x) for i in range(n_x)]
    low_before = lax.ppermute(low, "x", ahead)
    high_after = lax.ppermute(high, "x", behind)
    high_before = lax.ppermute(high, "x", ahead)
    low_after = lax.ppermute(low, "x", behind)
    low_before, high_after, high_before, low_after = lax.optimization_barrier(
        (low_before, high_after, high_before, low_after)
    )
    low_across = lax.ppermute(low_before, "x", ahead)
    high_across = lax.ppermute(high_after, "x", behind)
    far = (swap(low), swap(high))
    near = [(low_before, high_before), (low_after, high_after), (low_across, high_across)]
    swapped = [(swap(a), swap(b)) for a, b in near]
    blocks = [(low, high), far, near[0], near[1], swapped[0], swapped[1], near[2], swapped[2]]
    return blocks


def per_device(tokens, cotangent, experts, route_weight, gate_weight, up_weight, down_weight):
    n_high = lax.axis_size("zh")
    n_z = n_high * lax.axis_size("zl")
    n_x = lax.axis_size("x")
    n_s = n_x * lax.axis_size("c")
    count, feats = tokens.shape
    quarter = feats // window
    part = count // 2 // n_s
    gate, up, down = gate_weight[0], up_weight[0], down_weight[0]
    hidden = gate.shape[1]
    x, core, expert_id = (
        lax.axis_index(name).reshape(1).astype(jnp.int32) for name in ("x", "c", "y")
    )
    smem, vmem, anywhere = pltpu.SMEM, pltpu.VMEM, pl.ANY
    half = feats // 2
    groups = 2 * n_s + 1

    pieces, keep, send, table = kernel_call(
        prep_kernel,
        (
            jax.ShapeDtypeStruct((n_s, 2 * part, half), bf16),
            jax.ShapeDtypeStruct((n_s // 2, 2 * part, half), bf16),
            jax.ShapeDtypeStruct((n_s // 2, 2 * part, half), bf16),
            jax.ShapeDtypeStruct((1, table_rows, half), bf16),
        ),
        [smem] * 2 + [vmem] * 4,
    )(expert_id, core, experts.T, route_weight.T, tokens, cotangent)
    gate, up, down, pieces = lax.optimization_barrier((gate, up, down, pieces))
    pieces = lax.all_to_all(pieces, ("x", "c"), 0, 0, tiled=True)
    low, high, down_t = kernel_call(
        weights_kernel,
        (
            jax.ShapeDtypeStruct((2, half, hidden), bf16),
            jax.ShapeDtypeStruct((2, half, hidden), bf16),
            jax.ShapeDtypeStruct((feats, hidden), bf16),
        ),
        [vmem] * 3,
    )(gate, up, down)
    pieces, low, high, down_t = lax.optimization_barrier((pieces, low, high, down_t))
    own = kernel_call(
        pack_kernel,
        jax.ShapeDtypeStruct((groups, 2 * part, half), bf16),
        [anywhere] * 4,
        [pltpu.SemaphoreType.DMA((4,))],
        anywhere,
        small_vmem_bytes,
    )(pieces, keep, swap(send), table)
    rows = lax.all_gather(own.reshape(-1, half), ("zh", "zl"), axis=0, tiled=True).reshape(
        n_z, groups, 2 * part, half
    )
    weights = [value for block in gather_weights(low, high) for value in block]
    down_far = swap(down_t)

    back = kernel_call(
        back_kernel,
        jax.ShapeDtypeStruct((n_x, n_z * part, hidden), bf16),
        [anywhere] * 3,
        [
            pltpu.VMEM((2, n_z, n_s // 2, 2 * part, half), bf16),
            pltpu.VMEM((feats, hidden), bf16),
            pltpu.VMEM((feats, hidden), bf16),
            pltpu.SemaphoreType.DMA((4,)),
        ],
    )(rows, down_t, down_far)
    back = lax.all_to_all(back, "x", 0, 0, tiled=True)
    sums = kernel_call(
        products_kernel,
        jax.ShapeDtypeStruct((n_z * part, 2 * hidden), f32),
        [smem] * 2 + [anywhere] * (1 + len(weights)),
        [
            pltpu.VMEM((n_z, n_s, 2 * part, half), bf16),
            pltpu.VMEM((len(blocks_at), 2, 2, half, hidden), bf16),
            pltpu.SemaphoreType.DMA((len(weights) + 1,)),
        ],
    )(x, core, rows, *weights)
    result_shape = (n_s, window, 2, quarter // 2, n_z * part)
    result = kernel_call(
        result_kernel,
        jax.ShapeDtypeStruct(result_shape, bf16),
        [smem] * 2 + [anywhere] * (2 + len(weights)),
        [
            pltpu.VMEM((n_z * part, 2 * hidden), f32),
            pltpu.VMEM((n_x, n_z * part, hidden), bf16),
            pltpu.VMEM((len(blocks_at), 2, 2, half, hidden), bf16),
            pltpu.VMEM(result_shape, bf16),
            pltpu.SemaphoreType.DMA((len(weights) + 2,)),
            pltpu.SemaphoreType.DMA((len(blocks_at),)),
        ],
        anywhere,
    )(x, core, sums, back, *weights)
    tables = lax.dynamic_index_in_dim(
        rows.reshape(n_high, 2, groups, 2 * part, half)[:, :, groups - 1, :, :count],
        lax.axis_index("zl"),
        axis=1,
        keepdims=False,
    )
    shape = result.shape
    result = lax.all_to_all(
        result.reshape(n_s * window * 2, *shape[3:]), ("x", "c", "y", "zl"), 0, 0, tiled=True
    ).reshape(shape)
    dense = kernel_call(
        combine_kernel,
        jax.ShapeDtypeStruct((n_high, quarter, count), bf16),
        [vmem] * 2,
        vmem_limit=small_vmem_bytes,
    )(tables, result)
    dense = lax.all_to_all(dense, "zh", 0, 0, tiled=True)
    return jnp.sum(dense.astype(f32), axis=0).astype(bf16).T


def solution(mesh):
    split = Mesh(
        mesh.devices.reshape(mesh.shape["seq"] // 2, 2, mesh.shape["etp"] // 2, 2, -1),
        ("zh", "zl", "x", "c", "y"),
    )
    seq, etp = ("zh", "zl"), ("x", "c")
    placed = (
        P(seq, etp),
        P(seq, etp),
        P(seq, None),
        P(seq, None),
        P("y", etp, seq),
        P("y", etp, seq),
        P("y", seq, etp),
    )
    return jax.shard_map(
        per_device, mesh=split, in_specs=placed, out_specs=P(seq, ("x", "c", "y")), check_vma=False
    )
```

```python
import jax
import jax.numpy as jnp
from jax import lax
from jax.experimental import pallas as pl
from jax.experimental.pallas import tpu as pltpu
from jax.sharding import Mesh
from jax.sharding import PartitionSpec as P

unit_scale = 1.0 / 65536.0
window = 4
table_rows = 16
bf16 = jnp.bfloat16
f32 = jnp.float32
contract_last = (((1,), (1,)), ((), ()))
contract_first = (((0,), (0,)), ((), ()))
vmem_bytes = 56 * 1024 * 1024
late_vmem_bytes = 52 * 1024 * 1024
small_vmem_bytes = 16 * 1024 * 1024
blocks_at = ((0, 0), (0, 1), (-1, 0), (1, 0), (-1, 1), (1, 1), (2, 0), (2, 1))


def kernel_call(
    body, out_shape, spaces, scratch=(), out_space=pltpu.VMEM, vmem_limit=vmem_bytes
):
    return pl.pallas_call(
        body,
        out_shape=out_shape,
        in_specs=[pl.BlockSpec(memory_space=space) for space in spaces],
        out_specs=jax.tree.map(lambda _: pl.BlockSpec(memory_space=out_space), out_shape),
        scratch_shapes=list(scratch),
        compiler_params=pltpu.CompilerParams(vmem_limit_bytes=vmem_limit),
    )


def prep_kernel(
    expert_ref,
    core_ref,
    experts_ref,
    weight_ref,
    tok_ref,
    cot_ref,
    tok_out_ref,
    keep_ref,
    send_ref,
    table_ref,
):
    expert_id, core = expert_ref[0], core_ref[0]
    n_dest, both, half = tok_out_ref.shape
    part = both // 2
    count = tok_ref.shape[0]
    first, second = experts_ref[0:1, :], experts_ref[1:2, :]
    ids = lax.broadcasted_iota(jnp.int32, (window, count), 0)
    named = (first == ids) | (second == ids)
    before = lax.broadcasted_iota(jnp.int32, (count, count), 0) <= lax.broadcasted_iota(
        jnp.int32, (count, count), 1
    )
    order = jnp.dot(
        jnp.where(named, 1.0, 0.0).astype(bf16),
        jnp.where(before, 1.0, 0.0).astype(bf16),
        preferred_element_type=f32,
    )
    table = jnp.where(named, order - 1.0, -1.0)
    own = jnp.sum(jnp.where(ids == expert_id, table, 0.0), axis=0, keepdims=True)
    share = (
        jnp.where(first == expert_id, weight_ref[0:1, :], 0)
        + jnp.where(second == expert_id, weight_ref[1:2, :], 0)
    ).astype(f32) * unit_scale
    slot = lax.broadcasted_iota(jnp.int32, (n_dest * part, count), 0).astype(f32)
    hit = own == slot
    select = jnp.where(hit, 1.0, 0.0).astype(bf16)
    slot_share = jnp.sum(jnp.where(hit, share, 0.0), axis=1, keepdims=True)
    tok = jnp.dot(select, tok_ref[...], preferred_element_type=f32)
    cot = slot_share * jnp.dot(select, cot_ref[...], preferred_element_type=f32)
    for d in range(n_dest):
        rows = tok[d * part : (d + 1) * part]
        tok_out_ref[d] = jnp.concatenate([rows[:, :half], rows[:, half:]], axis=0).astype(bf16)
    sets = [
        jnp.concatenate(
            [cot[d * part : (d + 1) * part] for d in range(side, n_dest, 2)], axis=0
        )
        for side in range(2)
    ]
    mine = jnp.where(core == 0, sets[0], sets[1]).astype(bf16)
    other = jnp.where(core == 0, sets[1], sets[0]).astype(bf16)
    for h in range(2):
        for i in range(2):
            span = slice(i * both, (i + 1) * both)
            keep_ref[2 * h + i] = mine[span, h * half : (h + 1) * half]
            send_ref[2 * h + i] = other[span, h * half : (h + 1) * half]
    padded = jnp.concatenate([table, jnp.zeros((table_rows - window, count), f32)], axis=0)
    table_ref[0] = jnp.concatenate(
        [padded, jnp.zeros((table_rows, half - count), f32)], axis=1
    ).astype(bf16)


def pack_kernel(tok_ref, keep_ref, far_ref, table_ref, out_ref, sems):
    begin, copies = 0, []
    for i, ref in enumerate((tok_ref, keep_ref, far_ref, table_ref)):
        size = ref.shape[0]
        copies.append(pltpu.make_async_copy(ref, out_ref.at[pl.ds(begin, size)], sems.at[i]))
        copies[-1].start()
        begin += size
    for copy in copies:
        copy.wait()


def weights_kernel(gate_ref, up_ref, down_ref, low_ref, high_ref, flip_ref):
    half = low_ref.shape[1]
    for i, ref in enumerate((low_ref, high_ref)):
        span = slice(i * half, (i + 1) * half)
        ref[0] = gate_ref[span, :]
        ref[1] = up_ref[span, :]
        flip_ref[span, :] = down_ref[:, span].T


def source(x_ref, core_ref, n_x, dx, dc):
    x, core = x_ref[0], core_ref[0]
    return lax.rem(x + dx + n_x, n_x) * 2 + (1 - core if dc else core)


def back_kernel(rows_hbm, near_hbm, far_hbm, out_ref, rows_ref, near_ref, far_ref, sems):
    n_x, slots, hidden = out_ref.shape
    n_z, sub, half = rows_ref.shape[1:2] + rows_ref.shape[3:]
    per_z = 2 * sub
    copies = []
    for side, (weight_hbm, weight_ref) in enumerate(((near_hbm, near_ref), (far_hbm, far_ref))):
        at = 8 + 4 * side
        copies.append(
            pltpu.make_async_copy(
                rows_hbm.at[:, pl.ds(at, 4)], rows_ref.at[side], sems.at[2 * side]
            )
        )
        copies.append(pltpu.make_async_copy(weight_hbm, weight_ref, sems.at[2 * side + 1]))
    for copy in copies:
        copy.start()
    total = None
    for side, weight_ref in enumerate((near_ref, far_ref)):
        copies[2 * side].wait()
        copies[2 * side + 1].wait()
        for h in range(2):
            rows = rows_ref[side, :, 2 * h : 2 * h + 2].reshape(n_z * per_z, half)
            term = jnp.dot(
                rows, weight_ref[h * half : (h + 1) * half, :], preferred_element_type=f32
            )
            total = term if total is None else total + term
    total = total.reshape(n_z, n_x, slots // n_z, hidden)
    for i in range(n_x):
        out_ref[i] = total[:, i].reshape(slots, hidden).astype(bf16)


def start_weights(weights_hbm, weights_ref, sems):
    copies = [
        pltpu.make_async_copy(w, weights_ref.at[i // 2, i % 2], sems.at[i])
        for i, w in enumerate(weights_hbm)
    ]
    for copy in copies:
        copy.start()
    return copies


def products_kernel(x_ref, core_ref, *refs):
    n_w = 2 * len(blocks_at)
    rows_hbm, weights_hbm = refs[0], refs[1 : 1 + n_w]
    total_ref, rows_ref, weights_ref, sems = refs[1 + n_w :]
    n_z, n_s, both, half = rows_ref.shape
    part = both // 2
    hidden = weights_ref.shape[-1]
    rows_copy = pltpu.make_async_copy(rows_hbm.at[:, pl.ds(0, n_s)], rows_ref, sems.at[n_w])
    rows_copy.start()
    copies = start_weights(weights_hbm, weights_ref, sems)
    rows_copy.wait()
    for b, (dx, dc) in enumerate(blocks_at):
        copies[2 * b].wait()
        copies[2 * b + 1].wait()
        loaded = rows_ref[:, source(x_ref, core_ref, n_s // 2, dx, dc)].astype(f32)
        low, high = (
            loaded[:, begin : begin + part].reshape(n_z * part, half).astype(bf16)
            for begin in (0, part)
        )
        for m in range(2):
            span = slice(m * hidden, (m + 1) * hidden)
            term = jnp.dot(low, weights_ref[b, 0, m], preferred_element_type=f32)
            term += jnp.dot(high, weights_ref[b, 1, m], preferred_element_type=f32)
            if b == 0:
                total_ref[:, span] = term
            else:
                total_ref[:, span] += term


def result_kernel(x_ref, core_ref, *refs):
    n_w = 2 * len(blocks_at)
    sums_ref, back_ref, weights_hbm = refs[0], refs[1], refs[2 : 2 + n_w]
    out_hbm, weights_ref, out_ref, sems, out_sems = refs[2 + n_w :]
    n_x, slots, hidden = back_ref.shape
    half = weights_ref.shape[3]
    n_z = slots // 8
    copies = start_weights(weights_hbm, weights_ref, sems)

    back = sum(back_ref[i].astype(f32) for i in range(n_x))
    gate_sum, up_sum, back_sum = (
        jnp.concatenate(
            [
                value.reshape(n_z // 2, 2, 8, hidden)[:, pair].reshape(slots // 2, hidden)
                for pair in range(2)
            ],
            axis=0,
        )
        for value in (sums_ref[:, :hidden], sums_ref[:, hidden:], back)
    )
    sigmoid_gate = jax.nn.sigmoid(gate_sum)
    grad_up = (back_sum * (gate_sum * sigmoid_gate)).astype(bf16)
    grad_gate = (
        back_sum * up_sum * sigmoid_gate * (1.0 + gate_sum * (1.0 - sigmoid_gate))
    ).astype(bf16)

    quarter = 2 * half // window
    sent = []
    for b, (dx, dc) in enumerate(blocks_at):
        s = source(x_ref, core_ref, n_x, dx, dc)
        copies[2 * b].wait()
        copies[2 * b + 1].wait()
        wide = [
            lax.dot_general(
                grad_gate, weights_ref[b, side, 0], contract_last, preferred_element_type=f32
            )
            + lax.dot_general(
                grad_up, weights_ref[b, side, 1], contract_last, preferred_element_type=f32
            )
            for side in range(2)
        ]
        for y in range(window):
            side, begin = y * quarter // half, y * quarter % half
            rows = wide[side][:, begin : begin + quarter]
            for pair in range(2):
                mine = rows[pair * slots // 2 : (pair + 1) * slots // 2]
                out_ref[s, y, pair, : slots // 2, :] = mine[:, :128].astype(bf16)
                out_ref[s, y, pair, slots // 2 :, :] = jnp.concatenate(
                    [mine[: slots // 4, 128:], mine[slots // 4 :, 128:]], axis=1
                ).astype(bf16)
        sent.append(pltpu.make_async_copy(out_ref.at[s], out_hbm.at[s], out_sems.at[b]))
        sent[-1].start()
    for copy in sent:
        copy.wait()


def combine_kernel(table_ref, rows_ref, out_ref):
    n_blocks, quarter, count = out_ref.shape
    n_d = rows_ref.shape[0]
    part = 64 // n_d
    slots = n_blocks * part
    rest = quarter - 128
    slot = lax.broadcasted_iota(jnp.int32, (n_d * part, count), 0).astype(f32)
    sources = [(d, e, pair) for pair in range(2) for e in range(window) for d in range(n_d)]
    for p in range(n_blocks // 4):
        begin = 2 * part * p
        tails = [
            rows_ref[(*source, slice(slots + begin, slots + begin + 2 * part))].astype(f32)
            for source in sources
        ]
        for upper in range(2):
            at = upper * slots // 2 + begin
            heads = [
                rows_ref[(*source, slice(at, at + 2 * part))].astype(f32) for source in sources
            ]
            for j in range(2):
                block = upper * n_blocks // 2 + 2 * p + j
                span = slice(j * part, (j + 1) * part)
                values = jnp.concatenate(
                    [
                        jnp.concatenate([v[span] for v in heads], axis=0),
                        jnp.concatenate([v[span] for v in tails], axis=0),
                    ],
                    axis=1,
                ).astype(bf16)
                table = table_ref[block].astype(f32)
                select = jnp.concatenate(
                    [jnp.where(table[e : e + 1] == slot, 1.0, 0.0) for e in range(window)] * 2,
                    axis=0,
                ).astype(bf16)
                dense = lax.dot_general(
                    values, select, contract_first, preferred_element_type=f32
                ).astype(bf16)
                out_ref[block, :128, :] = dense[:128]
                out_ref[block, 128:, :] = dense[128 + upper * rest : 128 + (upper + 1) * rest]


def swap(value):
    return lax.ppermute(value, "c", [(0, 1), (1, 0)])


def gather_weights(low, high):
    n_x = lax.axis_size("x")
    ahead = [(i, (i + 1) % n_x) for i in range(n_x)]
    behind = [(i, (i - 1) % n_x) for i in range(n_x)]
    low_before = lax.ppermute(low, "x", ahead)
    high_after = lax.ppermute(high, "x", behind)
    high_before = lax.ppermute(high, "x", ahead)
    low_after = lax.ppermute(low, "x", behind)
    low_before, high_after, high_before, low_after = lax.optimization_barrier(
        (low_before, high_after, high_before, low_after)
    )
    low_across = lax.ppermute(low_before, "x", ahead)
    high_across = lax.ppermute(high_after, "x", behind)
    far = (swap(low), swap(high))
    near = [(low_before, high_before), (low_after, high_after), (low_across, high_across)]
    swapped = [(swap(a), swap(b)) for a, b in near]
    blocks = [(low, high), far, near[0], near[1], swapped[0], swapped[1], near[2], swapped[2]]
    return blocks


def per_device(tokens, cotangent, experts, route_weight, gate_weight, up_weight, down_weight):
    n_high = lax.axis_size("zh")
    n_z = n_high * lax.axis_size("zl")
    n_x = lax.axis_size("x")
    n_s = n_x * lax.axis_size("c")
    count, feats = tokens.shape
    quarter = feats // window
    part = count // 2 // n_s
    gate, up, down = gate_weight[0], up_weight[0], down_weight[0]
    hidden = gate.shape[1]
    x, core, expert_id = (
        lax.axis_index(name).reshape(1).astype(jnp.int32) for name in ("x", "c", "y")
    )
    smem, vmem, anywhere = pltpu.SMEM, pltpu.VMEM, pl.ANY
    half = feats // 2
    groups = 2 * n_s + 1

    pieces, keep, send, table = kernel_call(
        prep_kernel,
        (
            jax.ShapeDtypeStruct((n_s, 2 * part, half), bf16),
            jax.ShapeDtypeStruct((n_s // 2, 2 * part, half), bf16),
            jax.ShapeDtypeStruct((n_s // 2, 2 * part, half), bf16),
            jax.ShapeDtypeStruct((1, table_rows, half), bf16),
        ),
        [smem] * 2 + [vmem] * 4,
    )(expert_id, core, experts.T, route_weight.T, tokens, cotangent)
    gate, up, down, pieces = lax.optimization_barrier((gate, up, down, pieces))
    pieces = lax.all_to_all(pieces, ("x", "c"), 0, 0, tiled=True)
    low, high, down_t = kernel_call(
        weights_kernel,
        (
            jax.ShapeDtypeStruct((2, half, hidden), bf16),
            jax.ShapeDtypeStruct((2, half, hidden), bf16),
            jax.ShapeDtypeStruct((feats, hidden), bf16),
        ),
        [vmem] * 3,
    )(gate, up, down)
    pieces, low, high, down_t = lax.optimization_barrier((pieces, low, high, down_t))
    own = kernel_call(
        pack_kernel,
        jax.ShapeDtypeStruct((groups, 2 * part, half), bf16),
        [anywhere] * 4,
        [pltpu.SemaphoreType.DMA((4,))],
        anywhere,
        small_vmem_bytes,
    )(pieces, keep, swap(send), table)
    rows = lax.all_gather(own.reshape(-1, half), ("zh", "zl"), axis=0, tiled=True).reshape(
        n_z, groups, 2 * part, half
    )
    weights = [value for block in gather_weights(low, high) for value in block]
    down_far = swap(down_t)

    back = kernel_call(
        back_kernel,
        jax.ShapeDtypeStruct((n_x, n_z * part, hidden), bf16),
        [anywhere] * 3,
        [
            pltpu.VMEM((2, n_z, n_s // 2, 2 * part, half), bf16),
            pltpu.VMEM((feats, hidden), bf16),
            pltpu.VMEM((feats, hidden), bf16),
            pltpu.SemaphoreType.DMA((4,)),
        ],
    )(rows, down_t, down_far)
    back = lax.all_to_all(back, "x", 0, 0, tiled=True)
    sums = kernel_call(
        products_kernel,
        jax.ShapeDtypeStruct((n_z * part, 2 * hidden), f32),
        [smem] * 2 + [anywhere] * (1 + len(weights)),
        [
            pltpu.VMEM((n_z, n_s, 2 * part, half), bf16),
            pltpu.VMEM((len(blocks_at), 2, 2, half, hidden), bf16),
            pltpu.SemaphoreType.DMA((len(weights) + 1,)),
        ],
        vmem_limit=late_vmem_bytes,
    )(x, core, rows, *weights)
    result_shape = (n_s, window, 2, quarter // 2, n_z * part)
    result = kernel_call(
        result_kernel,
        jax.ShapeDtypeStruct(result_shape, bf16),
        [smem] * 2 + [vmem] * 2 + [anywhere] * len(weights),
        [
            pltpu.VMEM((len(blocks_at), 2, 2, half, hidden), bf16),
            pltpu.VMEM(result_shape, bf16),
            pltpu.SemaphoreType.DMA((len(weights),)),
            pltpu.SemaphoreType.DMA((len(blocks_at),)),
        ],
        anywhere,
        late_vmem_bytes,
    )(x, core, sums, back, *weights)
    tables = lax.dynamic_index_in_dim(
        rows.reshape(n_high, 2, groups, 2 * part, half)[:, :, groups - 1, :, :count],
        lax.axis_index("zl"),
        axis=1,
        keepdims=False,
    )
    shape = result.shape
    result = lax.all_to_all(
        result.reshape(n_s * window * 2, *shape[3:]), ("x", "c", "y", "zl"), 0, 0, tiled=True
    ).reshape(shape)
    dense = kernel_call(
        combine_kernel,
        jax.ShapeDtypeStruct((n_high, quarter, count), bf16),
        [vmem] * 2,
        vmem_limit=small_vmem_bytes,
    )(tables, result)
    dense = lax.all_to_all(dense, "zh", 0, 0, tiled=True)
    return jnp.sum(dense.astype(f32), axis=0).astype(bf16).T


def solution(mesh):
    split = Mesh(
        mesh.devices.reshape(mesh.shape["seq"] // 2, 2, mesh.shape["etp"] // 2, 2, -1),
        ("zh", "zl", "x", "c", "y"),
    )
    seq, etp = ("zh", "zl"), ("x", "c")
    placed = (
        P(seq, etp),
        P(seq, etp),
        P(seq, None),
        P(seq, None),
        P("y", etp, seq),
        P("y", etp, seq),
        P("y", seq, etp),
    )
    return jax.shard_map(
        per_device, mesh=split, in_specs=placed, out_specs=P(seq, ("x", "c", "y")), check_vma=False
    )
```

```python
import jax
import jax.numpy as jnp
from jax import lax
from jax.experimental import pallas as pl
from jax.experimental.pallas import tpu as pltpu
from jax.sharding import Mesh
from jax.sharding import PartitionSpec as P

unit_scale = 1.0 / 65536.0
window = 4
table_rows = 16
bf16 = jnp.bfloat16
f32 = jnp.float32
contract_last = (((1,), (1,)), ((), ()))
contract_first = (((0,), (0,)), ((), ()))
vmem_bytes = 56 * 1024 * 1024
late_vmem_bytes = 52 * 1024 * 1024
small_vmem_bytes = 16 * 1024 * 1024
blocks_at = ((0, 0), (0, 1), (-1, 0), (1, 0), (-1, 1), (1, 1), (2, 0), (2, 1))


def kernel_call(
    body, out_shape, spaces, scratch=(), out_space=pltpu.VMEM, vmem_limit=vmem_bytes
):
    return pl.pallas_call(
        body,
        out_shape=out_shape,
        in_specs=[pl.BlockSpec(memory_space=space) for space in spaces],
        out_specs=jax.tree.map(lambda _: pl.BlockSpec(memory_space=out_space), out_shape),
        scratch_shapes=list(scratch),
        compiler_params=pltpu.CompilerParams(vmem_limit_bytes=vmem_limit),
    )


def prep_kernel(
    expert_ref,
    core_ref,
    experts_ref,
    weight_ref,
    tok_ref,
    cot_ref,
    tok_out_ref,
    keep_ref,
    send_ref,
    table_ref,
):
    expert_id, core = expert_ref[0], core_ref[0]
    n_dest, both, half = tok_out_ref.shape
    part = both // 2
    count = tok_ref.shape[0]
    first, second = experts_ref[0:1, :], experts_ref[1:2, :]
    ids = lax.broadcasted_iota(jnp.int32, (window, count), 0)
    named = (first == ids) | (second == ids)
    before = lax.broadcasted_iota(jnp.int32, (count, count), 0) <= lax.broadcasted_iota(
        jnp.int32, (count, count), 1
    )
    order = jnp.dot(
        jnp.where(named, 1.0, 0.0).astype(bf16),
        jnp.where(before, 1.0, 0.0).astype(bf16),
        preferred_element_type=f32,
    )
    table = jnp.where(named, order - 1.0, -1.0)
    own = jnp.sum(jnp.where(ids == expert_id, table, 0.0), axis=0, keepdims=True)
    share = (
        jnp.where(first == expert_id, weight_ref[0:1, :], 0)
        + jnp.where(second == expert_id, weight_ref[1:2, :], 0)
    ).astype(f32) * unit_scale
    slot = lax.broadcasted_iota(jnp.int32, (n_dest * part, count), 0).astype(f32)
    hit = own == slot
    select = jnp.where(hit, 1.0, 0.0).astype(bf16)
    slot_share = jnp.sum(jnp.where(hit, share, 0.0), axis=1, keepdims=True)
    tok = jnp.dot(select, tok_ref[...], preferred_element_type=f32)
    cot = slot_share * jnp.dot(select, cot_ref[...], preferred_element_type=f32)
    for d in range(n_dest):
        rows = tok[d * part : (d + 1) * part]
        tok_out_ref[d] = jnp.concatenate([rows[:, :half], rows[:, half:]], axis=0).astype(bf16)
    sets = [
        jnp.concatenate(
            [cot[d * part : (d + 1) * part] for d in range(side, n_dest, 2)], axis=0
        )
        for side in range(2)
    ]
    mine = jnp.where(core == 0, sets[0], sets[1]).astype(bf16)
    other = jnp.where(core == 0, sets[1], sets[0]).astype(bf16)
    for h in range(2):
        for i in range(2):
            span = slice(i * both, (i + 1) * both)
            keep_ref[2 * h + i] = mine[span, h * half : (h + 1) * half]
            send_ref[2 * h + i] = other[span, h * half : (h + 1) * half]
    padded = jnp.concatenate([table, jnp.zeros((table_rows - window, count), f32)], axis=0)
    table_ref[0] = jnp.concatenate(
        [padded, jnp.zeros((table_rows, half - count), f32)], axis=1
    ).astype(bf16)


def pack_kernel(tok_ref, keep_ref, far_ref, table_ref, out_ref, sems):
    begin, copies = 0, []
    for i, ref in enumerate((tok_ref, keep_ref, far_ref, table_ref)):
        size = ref.shape[0]
        copies.append(pltpu.make_async_copy(ref, out_ref.at[pl.ds(begin, size)], sems.at[i]))
        copies[-1].start()
        begin += size
    for copy in copies:
        copy.wait()


def flip_kernel(in_ref, out_ref):
    out_ref[...] = in_ref[...].T


def source(x_ref, core_ref, n_x, dx, dc):
    x, core = x_ref[0], core_ref[0]
    return lax.rem(x + dx + n_x, n_x) * 2 + (1 - core if dc else core)


def back_kernel(rows_hbm, near_hbm, far_hbm, out_ref, rows_ref, near_ref, far_ref, sems):
    n_x, slots, hidden = out_ref.shape
    n_z, sub, half = rows_ref.shape[1:2] + rows_ref.shape[3:]
    per_z = 2 * sub
    copies = []
    for side, (weight_hbm, weight_ref) in enumerate(((near_hbm, near_ref), (far_hbm, far_ref))):
        at = 8 + 4 * side
        copies.append(
            pltpu.make_async_copy(
                rows_hbm.at[:, pl.ds(at, 4)], rows_ref.at[side], sems.at[2 * side]
            )
        )
        copies.append(pltpu.make_async_copy(weight_hbm, weight_ref, sems.at[2 * side + 1]))
    for copy in copies:
        copy.start()
    total = None
    for side, weight_ref in enumerate((near_ref, far_ref)):
        copies[2 * side].wait()
        copies[2 * side + 1].wait()
        for h in range(2):
            rows = rows_ref[side, :, 2 * h : 2 * h + 2].reshape(n_z * per_z, half)
            term = jnp.dot(
                rows, weight_ref[h * half : (h + 1) * half, :], preferred_element_type=f32
            )
            total = term if total is None else total + term
    total = total.reshape(n_z, n_x, slots // n_z, hidden)
    for i in range(n_x):
        out_ref[i] = total[:, i].reshape(slots, hidden).astype(bf16)


def start_weights(weights_hbm, weights_ref, sems):
    copies = [
        pltpu.make_async_copy(w, weights_ref.at[i // 2, i % 2], sems.at[i])
        for i, w in enumerate(weights_hbm)
    ]
    for copy in copies:
        copy.start()
    return copies


def products_kernel(x_ref, core_ref, *refs):
    n_w = 2 * len(blocks_at)
    rows_hbm, weights_hbm = refs[0], refs[1 : 1 + n_w]
    total_ref, rows_ref, weights_ref, sems = refs[1 + n_w :]
    n_z, n_s, both, half = rows_ref.shape
    part = both // 2
    hidden = weights_ref.shape[-1]
    rows_copy = pltpu.make_async_copy(rows_hbm.at[:, pl.ds(0, n_s)], rows_ref, sems.at[n_w])
    rows_copy.start()
    copies = start_weights(weights_hbm, weights_ref, sems)
    rows_copy.wait()
    for b, (dx, dc) in enumerate(blocks_at):
        copies[2 * b].wait()
        copies[2 * b + 1].wait()
        loaded = rows_ref[:, source(x_ref, core_ref, n_s // 2, dx, dc)].astype(f32)
        low, high = (
            loaded[:, begin : begin + part].reshape(n_z * part, half).astype(bf16)
            for begin in (0, part)
        )
        for m in range(2):
            span = slice(m * hidden, (m + 1) * hidden)
            term = jnp.dot(low, weights_ref[b, m, :half], preferred_element_type=f32)
            term += jnp.dot(high, weights_ref[b, m, half:], preferred_element_type=f32)
            if b == 0:
                total_ref[:, span] = term
            else:
                total_ref[:, span] += term


def result_kernel(x_ref, core_ref, *refs):
    n_w = 2 * len(blocks_at)
    sums_ref, back_ref, weights_hbm = refs[0], refs[1], refs[2 : 2 + n_w]
    out_hbm, weights_ref, out_ref, sems, out_sems = refs[2 + n_w :]
    n_x, slots, hidden = back_ref.shape
    feats = weights_ref.shape[2]
    n_z = slots // 8
    copies = start_weights(weights_hbm, weights_ref, sems)

    back = sum(back_ref[i].astype(f32) for i in range(n_x))
    gate_sum, up_sum, back_sum = (
        jnp.concatenate(
            [
                value.reshape(n_z // 2, 2, 8, hidden)[:, pair].reshape(slots // 2, hidden)
                for pair in range(2)
            ],
            axis=0,
        )
        for value in (sums_ref[:, :hidden], sums_ref[:, hidden:], back)
    )
    sigmoid_gate = jax.nn.sigmoid(gate_sum)
    grad_up = (back_sum * (gate_sum * sigmoid_gate)).astype(bf16)
    grad_gate = (
        back_sum * up_sum * sigmoid_gate * (1.0 + gate_sum * (1.0 - sigmoid_gate))
    ).astype(bf16)

    quarter = feats // window
    sent = []
    for b, (dx, dc) in enumerate(blocks_at):
        s = source(x_ref, core_ref, n_x, dx, dc)
        copies[2 * b].wait()
        copies[2 * b + 1].wait()
        wide = lax.dot_general(
            grad_gate, weights_ref[b, 0], contract_last, preferred_element_type=f32
        ) + lax.dot_general(
            grad_up, weights_ref[b, 1], contract_last, preferred_element_type=f32
        )
        for y in range(window):
            rows = wide[:, y * quarter : (y + 1) * quarter]
            for pair in range(2):
                mine = rows[pair * slots // 2 : (pair + 1) * slots // 2]
                out_ref[s, y, pair, : slots // 2, :] = mine[:, :128].astype(bf16)
                out_ref[s, y, pair, slots // 2 :, :] = jnp.concatenate(
                    [mine[: slots // 4, 128:], mine[slots // 4 :, 128:]], axis=1
                ).astype(bf16)
        sent.append(pltpu.make_async_copy(out_ref.at[s], out_hbm.at[s], out_sems.at[b]))
        sent[-1].start()
    for copy in sent:
        copy.wait()


def combine_kernel(table_ref, rows_ref, out_ref):
    n_blocks, quarter, count = out_ref.shape
    n_d = rows_ref.shape[0]
    part = 64 // n_d
    slots = n_blocks * part
    rest = quarter - 128
    slot = lax.broadcasted_iota(jnp.int32, (n_d * part, count), 0).astype(f32)
    sources = [(d, e, pair) for pair in range(2) for e in range(window) for d in range(n_d)]
    for p in range(n_blocks // 4):
        begin = 2 * part * p
        tails = [
            rows_ref[(*source, slice(slots + begin, slots + begin + 2 * part))].astype(f32)
            for source in sources
        ]
        for upper in range(2):
            at = upper * slots // 2 + begin
            heads = [
                rows_ref[(*source, slice(at, at + 2 * part))].astype(f32) for source in sources
            ]
            for j in range(2):
                block = upper * n_blocks // 2 + 2 * p + j
                span = slice(j * part, (j + 1) * part)
                values = jnp.concatenate(
                    [
                        jnp.concatenate([v[span] for v in heads], axis=0),
                        jnp.concatenate([v[span] for v in tails], axis=0),
                    ],
                    axis=1,
                ).astype(bf16)
                table = table_ref[block].astype(f32)
                select = jnp.concatenate(
                    [jnp.where(table[e : e + 1] == slot, 1.0, 0.0) for e in range(window)] * 2,
                    axis=0,
                ).astype(bf16)
                dense = lax.dot_general(
                    values, select, contract_first, preferred_element_type=f32
                ).astype(bf16)
                out_ref[block, :128, :] = dense[:128]
                out_ref[block, 128:, :] = dense[128 + upper * rest : 128 + (upper + 1) * rest]


def swap(value):
    return lax.ppermute(value, "c", [(0, 1), (1, 0)])


def gather_weights(gate, up):
    n_x = lax.axis_size("x")
    ahead = [(i, (i + 1) % n_x) for i in range(n_x)]
    behind = [(i, (i - 1) % n_x) for i in range(n_x)]
    gate_before = lax.ppermute(gate, "x", ahead)
    up_after = lax.ppermute(up, "x", behind)
    up_before = lax.ppermute(up, "x", ahead)
    gate_after = lax.ppermute(gate, "x", behind)
    gate_before, up_after, up_before, gate_after = lax.optimization_barrier(
        (gate_before, up_after, up_before, gate_after)
    )
    gate_across = lax.ppermute(gate_before, "x", ahead)
    up_across = lax.ppermute(up_after, "x", behind)
    far = (swap(gate), swap(up))
    near = [(gate_before, up_before), (gate_after, up_after), (gate_across, up_across)]
    swapped = [(swap(a), swap(b)) for a, b in near]
    return [(gate, up), far, near[0], near[1], swapped[0], swapped[1], near[2], swapped[2]]


def per_device(tokens, cotangent, experts, route_weight, gate_weight, up_weight, down_weight):
    n_high = lax.axis_size("zh")
    n_z = n_high * lax.axis_size("zl")
    n_x = lax.axis_size("x")
    n_s = n_x * lax.axis_size("c")
    count, feats = tokens.shape
    quarter = feats // window
    part = count // 2 // n_s
    gate, up, down = gate_weight[0], up_weight[0], down_weight[0]
    hidden = gate.shape[1]
    x, core, expert_id = (
        lax.axis_index(name).reshape(1).astype(jnp.int32) for name in ("x", "c", "y")
    )
    smem, vmem, anywhere = pltpu.SMEM, pltpu.VMEM, pl.ANY
    half = feats // 2
    groups = 2 * n_s + 1

    pieces, keep, send, table = kernel_call(
        prep_kernel,
        (
            jax.ShapeDtypeStruct((n_s, 2 * part, half), bf16),
            jax.ShapeDtypeStruct((n_s // 2, 2 * part, half), bf16),
            jax.ShapeDtypeStruct((n_s // 2, 2 * part, half), bf16),
            jax.ShapeDtypeStruct((1, table_rows, half), bf16),
        ),
        [smem] * 2 + [vmem] * 4,
    )(expert_id, core, experts.T, route_weight.T, tokens, cotangent)
    down, pieces = lax.optimization_barrier((down, pieces))
    pieces = lax.all_to_all(pieces, ("x", "c"), 0, 0, tiled=True)
    down_t = kernel_call(flip_kernel, jax.ShapeDtypeStruct((feats, hidden), bf16), [vmem])(down)
    pieces, down_t = lax.optimization_barrier((pieces, down_t))
    own = kernel_call(
        pack_kernel,
        jax.ShapeDtypeStruct((groups, 2 * part, half), bf16),
        [anywhere] * 4,
        [pltpu.SemaphoreType.DMA((4,))],
        anywhere,
        small_vmem_bytes,
    )(pieces, keep, swap(send), table)
    gate, up, own = lax.optimization_barrier((gate, up, own))
    rows = lax.all_gather(own.reshape(-1, half), ("zh", "zl"), axis=0, tiled=True).reshape(
        n_z, groups, 2 * part, half
    )
    weights = [value for block in gather_weights(gate, up) for value in block]
    down_far = swap(down_t)

    back = kernel_call(
        back_kernel,
        jax.ShapeDtypeStruct((n_x, n_z * part, hidden), bf16),
        [anywhere] * 3,
        [
            pltpu.VMEM((2, n_z, n_s // 2, 2 * part, half), bf16),
            pltpu.VMEM((feats, hidden), bf16),
            pltpu.VMEM((feats, hidden), bf16),
            pltpu.SemaphoreType.DMA((4,)),
        ],
    )(rows, down_t, down_far)
    back = lax.all_to_all(back, "x", 0, 0, tiled=True)
    sums = kernel_call(
        products_kernel,
        jax.ShapeDtypeStruct((n_z * part, 2 * hidden), f32),
        [smem] * 2 + [anywhere] * (1 + len(weights)),
        [
            pltpu.VMEM((n_z, n_s, 2 * part, half), bf16),
            pltpu.VMEM((len(blocks_at), 2, feats, hidden), bf16),
            pltpu.SemaphoreType.DMA((len(weights) + 1,)),
        ],
        vmem_limit=late_vmem_bytes,
    )(x, core, rows, *weights)
    result_shape = (n_s, window, 2, quarter // 2, n_z * part)
    result = kernel_call(
        result_kernel,
        jax.ShapeDtypeStruct(result_shape, bf16),
        [smem] * 2 + [vmem] * 2 + [anywhere] * len(weights),
        [
            pltpu.VMEM((len(blocks_at), 2, feats, hidden), bf16),
            pltpu.VMEM(result_shape, bf16),
            pltpu.SemaphoreType.DMA((len(weights),)),
            pltpu.SemaphoreType.DMA((len(blocks_at),)),
        ],
        anywhere,
        late_vmem_bytes,
    )(x, core, sums, back, *weights)
    tables = lax.dynamic_index_in_dim(
        rows.reshape(n_high, 2, groups, 2 * part, half)[:, :, groups - 1, :, :count],
        lax.axis_index("zl"),
        axis=1,
        keepdims=False,
    )
    shape = result.shape
    result = lax.all_to_all(
        result.reshape(n_s * window * 2, *shape[3:]), ("x", "c", "y", "zl"), 0, 0, tiled=True
    ).reshape(shape)
    dense = kernel_call(
        combine_kernel,
        jax.ShapeDtypeStruct((n_high, quarter, count), bf16),
        [vmem] * 2,
        vmem_limit=small_vmem_bytes,
    )(tables, result)
    dense = lax.all_to_all(dense, "zh", 0, 0, tiled=True)
    return jnp.sum(dense.astype(f32), axis=0).astype(bf16).T


def solution(mesh):
    split = Mesh(
        mesh.devices.reshape(mesh.shape["seq"] // 2, 2, mesh.shape["etp"] // 2, 2, -1),
        ("zh", "zl", "x", "c", "y"),
    )
    seq, etp = ("zh", "zl"), ("x", "c")
    placed = (
        P(seq, etp),
        P(seq, etp),
        P(seq, None),
        P(seq, None),
        P("y", etp, seq),
        P("y", etp, seq),
        P("y", seq, etp),
    )
    return jax.shard_map(
        per_device, mesh=split, in_specs=placed, out_specs=P(seq, ("x", "c", "y")), check_vma=False
    )
```

```python
import jax
import jax.numpy as jnp
from jax import lax
from jax.experimental import pallas as pl
from jax.experimental.pallas import tpu as pltpu
from jax.sharding import Mesh
from jax.sharding import PartitionSpec as P

unit_scale = 1.0 / 65536.0
window = 4
table_rows = 16
bf16 = jnp.bfloat16
f32 = jnp.float32
contract_last = (((1,), (1,)), ((), ()))
contract_first = (((0,), (0,)), ((), ()))
vmem_bytes = 56 * 1024 * 1024
late_vmem_bytes = 52 * 1024 * 1024
small_vmem_bytes = 16 * 1024 * 1024
blocks_at = ((0, 0), (0, 1), (-1, 0), (1, 0), (-1, 1), (1, 1), (2, 0), (2, 1))


def kernel_call(
    body, out_shape, spaces, scratch=(), out_space=pltpu.VMEM, vmem_limit=vmem_bytes
):
    return pl.pallas_call(
        body,
        out_shape=out_shape,
        in_specs=[pl.BlockSpec(memory_space=space) for space in spaces],
        out_specs=jax.tree.map(lambda _: pl.BlockSpec(memory_space=out_space), out_shape),
        scratch_shapes=list(scratch),
        compiler_params=pltpu.CompilerParams(vmem_limit_bytes=vmem_limit),
    )


def prep_kernel(
    expert_ref,
    core_ref,
    experts_ref,
    weight_ref,
    tok_ref,
    cot_ref,
    tok_out_ref,
    keep_ref,
    send_ref,
    table_ref,
):
    expert_id, core = expert_ref[0], core_ref[0]
    n_dest, both, half = tok_out_ref.shape
    part = both // 2
    count = tok_ref.shape[0]
    first, second = experts_ref[0:1, :], experts_ref[1:2, :]
    ids = lax.broadcasted_iota(jnp.int32, (window, count), 0)
    named = (first == ids) | (second == ids)
    before = lax.broadcasted_iota(jnp.int32, (count, count), 0) <= lax.broadcasted_iota(
        jnp.int32, (count, count), 1
    )
    order = jnp.dot(
        jnp.where(named, 1.0, 0.0).astype(bf16),
        jnp.where(before, 1.0, 0.0).astype(bf16),
        preferred_element_type=f32,
    )
    table = jnp.where(named, order - 1.0, -1.0)
    own = jnp.sum(jnp.where(ids == expert_id, table, 0.0), axis=0, keepdims=True)
    share = (
        jnp.where(first == expert_id, weight_ref[0:1, :], 0)
        + jnp.where(second == expert_id, weight_ref[1:2, :], 0)
    ).astype(f32) * unit_scale
    slot = lax.broadcasted_iota(jnp.int32, (n_dest * part, count), 0).astype(f32)
    hit = own == slot
    select = jnp.where(hit, 1.0, 0.0).astype(bf16)
    slot_share = jnp.sum(jnp.where(hit, share, 0.0), axis=1, keepdims=True)
    tok = jnp.dot(select, tok_ref[...], preferred_element_type=f32)
    cot = slot_share * jnp.dot(select, cot_ref[...], preferred_element_type=f32)
    for d in range(n_dest):
        rows = tok[d * part : (d + 1) * part]
        tok_out_ref[d] = jnp.concatenate([rows[:, :half], rows[:, half:]], axis=0).astype(bf16)
    sets = [
        jnp.concatenate(
            [cot[d * part : (d + 1) * part] for d in range(side, n_dest, 2)], axis=0
        )
        for side in range(2)
    ]
    mine = jnp.where(core == 0, sets[0], sets[1]).astype(bf16)
    other = jnp.where(core == 0, sets[1], sets[0]).astype(bf16)
    for h in range(2):
        for i in range(2):
            span = slice(i * both, (i + 1) * both)
            keep_ref[2 * h + i] = mine[span, h * half : (h + 1) * half]
            send_ref[2 * h + i] = other[span, h * half : (h + 1) * half]
    padded = jnp.concatenate([table, jnp.zeros((table_rows - window, count), f32)], axis=0)
    table_ref[0] = jnp.concatenate(
        [padded, jnp.zeros((table_rows, half - count), f32)], axis=1
    ).astype(bf16)


def pack_kernel(tok_ref, keep_ref, far_ref, table_ref, out_ref, sems):
    begin, copies = 0, []
    for i, ref in enumerate((tok_ref, keep_ref, far_ref, table_ref)):
        size = ref.shape[0]
        copies.append(pltpu.make_async_copy(ref, out_ref.at[pl.ds(begin, size)], sems.at[i]))
        copies[-1].start()
        begin += size
    for copy in copies:
        copy.wait()


def flip_kernel(in_ref, out_ref):
    out_ref[...] = in_ref[...].T


def source(x_ref, core_ref, n_x, dx, dc):
    x, core = x_ref[0], core_ref[0]
    return lax.rem(x + dx + n_x, n_x) * 2 + (1 - core if dc else core)


def back_kernel(rows_hbm, near_hbm, far_hbm, out_ref, rows_ref, near_ref, far_ref, sems):
    n_x, slots, hidden = out_ref.shape
    n_z, sub, half = rows_ref.shape[1:2] + rows_ref.shape[3:]
    per_z = 2 * sub
    copies = []
    for side, (weight_hbm, weight_ref) in enumerate(((near_hbm, near_ref), (far_hbm, far_ref))):
        at = 8 + 4 * side
        copies.append(
            pltpu.make_async_copy(
                rows_hbm.at[:, pl.ds(at, 4)], rows_ref.at[side], sems.at[2 * side]
            )
        )
        copies.append(pltpu.make_async_copy(weight_hbm, weight_ref, sems.at[2 * side + 1]))
    for copy in copies:
        copy.start()
    total = None
    for side, weight_ref in enumerate((near_ref, far_ref)):
        copies[2 * side].wait()
        copies[2 * side + 1].wait()
        for h in range(2):
            rows = rows_ref[side, :, 2 * h : 2 * h + 2].reshape(n_z * per_z, half)
            term = jnp.dot(
                rows, weight_ref[h * half : (h + 1) * half, :], preferred_element_type=f32
            )
            total = term if total is None else total + term
    total = total.reshape(n_z, n_x, slots // n_z, hidden)
    for i in range(n_x):
        out_ref[i] = total[:, i].reshape(slots, hidden).astype(bf16)


def start_weights(weights_hbm, weights_ref, sems):
    copies = [
        pltpu.make_async_copy(w, weights_ref.at[i // 2, i % 2], sems.at[i])
        for i, w in enumerate(weights_hbm)
    ]
    for copy in copies:
        copy.start()
    return copies


def products_kernel(x_ref, core_ref, *refs):
    n_w = 2 * len(blocks_at)
    rows_hbm, weights_hbm = refs[0], refs[1 : 1 + n_w]
    total_ref, rows_ref, weights_ref, sems = refs[1 + n_w :]
    n_z, n_s, both, half = rows_ref.shape
    part = both // 2
    hidden = weights_ref.shape[-1]
    rows_copy = pltpu.make_async_copy(rows_hbm.at[:, pl.ds(0, n_s)], rows_ref, sems.at[n_w])
    rows_copy.start()
    copies = start_weights(weights_hbm, weights_ref, sems)
    rows_copy.wait()
    for b, (dx, dc) in enumerate(blocks_at):
        copies[2 * b].wait()
        copies[2 * b + 1].wait()
        loaded = rows_ref[:, source(x_ref, core_ref, n_s // 2, dx, dc)].astype(f32)
        low, high = (
            loaded[:, begin : begin + part].reshape(n_z * part, half).astype(bf16)
            for begin in (0, part)
        )
        for m in range(2):
            span = slice(m * hidden, (m + 1) * hidden)
            term = jnp.dot(low, weights_ref[b, m, :half], preferred_element_type=f32)
            term += jnp.dot(high, weights_ref[b, m, half:], preferred_element_type=f32)
            if b == 0:
                total_ref[:, span] = term
            else:
                total_ref[:, span] += term


def result_kernel(x_ref, core_ref, *refs):
    n_w = 2 * len(blocks_at)
    sums_ref, back_ref, weights_hbm = refs[0], refs[1], refs[2 : 2 + n_w]
    out_hbm, weights_ref, out_ref, sems, out_sems = refs[2 + n_w :]
    n_x, slots, hidden = back_ref.shape
    feats = weights_ref.shape[2]
    half = feats // 2
    n_z = slots // 8
    copies = start_weights(weights_hbm, weights_ref, sems)

    back = sum(back_ref[i].astype(f32) for i in range(n_x))
    gate_sum, up_sum, back_sum = (
        jnp.concatenate(
            [
                value.reshape(n_z // 2, 2, 8, hidden)[:, pair].reshape(slots // 2, hidden)
                for pair in range(2)
            ],
            axis=0,
        )
        for value in (sums_ref[:, :hidden], sums_ref[:, hidden:], back)
    )
    sigmoid_gate = jax.nn.sigmoid(gate_sum)
    grad_up = (back_sum * (gate_sum * sigmoid_gate)).astype(bf16)
    grad_gate = (
        back_sum * up_sum * sigmoid_gate * (1.0 + gate_sum * (1.0 - sigmoid_gate))
    ).astype(bf16)

    quarter = feats // window
    sent = []
    for b, (dx, dc) in enumerate(blocks_at):
        s = source(x_ref, core_ref, n_x, dx, dc)
        copies[2 * b].wait()
        copies[2 * b + 1].wait()
        wide = [
            lax.dot_general(
                grad_gate, weights_ref[b, 0, span], contract_last, preferred_element_type=f32
            )
            + lax.dot_general(
                grad_up, weights_ref[b, 1, span], contract_last, preferred_element_type=f32
            )
            for span in (slice(0, half), slice(half, feats))
        ]
        for y in range(window):
            begin = y * quarter % half
            rows = wide[y * quarter // half][:, begin : begin + quarter]
            for pair in range(2):
                mine = rows[pair * slots // 2 : (pair + 1) * slots // 2]
                out_ref[s, y, pair, : slots // 2, :] = mine[:, :128].astype(bf16)
                out_ref[s, y, pair, slots // 2 :, :] = jnp.concatenate(
                    [mine[: slots // 4, 128:], mine[slots // 4 :, 128:]], axis=1
                ).astype(bf16)
        sent.append(pltpu.make_async_copy(out_ref.at[s], out_hbm.at[s], out_sems.at[b]))
        sent[-1].start()
    for copy in sent:
        copy.wait()


def combine_kernel(table_ref, rows_ref, out_ref):
    n_blocks, quarter, count = out_ref.shape
    n_d = rows_ref.shape[0]
    part = 64 // n_d
    slots = n_blocks * part
    rest = quarter - 128
    slot = lax.broadcasted_iota(jnp.int32, (n_d * part, count), 0).astype(f32)
    sources = [(d, e, pair) for pair in range(2) for e in range(window) for d in range(n_d)]
    for p in range(n_blocks // 4):
        begin = 2 * part * p
        tails = [
            rows_ref[(*source, slice(slots + begin, slots + begin + 2 * part))].astype(f32)
            for source in sources
        ]
        for upper in range(2):
            at = upper * slots // 2 + begin
            heads = [
                rows_ref[(*source, slice(at, at + 2 * part))].astype(f32) for source in sources
            ]
            for j in range(2):
                block = upper * n_blocks // 2 + 2 * p + j
                span = slice(j * part, (j + 1) * part)
                values = jnp.concatenate(
                    [
                        jnp.concatenate([v[span] for v in heads], axis=0),
                        jnp.concatenate([v[span] for v in tails], axis=0),
                    ],
                    axis=1,
                ).astype(bf16)
                table = table_ref[block].astype(f32)
                select = jnp.concatenate(
                    [jnp.where(table[e : e + 1] == slot, 1.0, 0.0) for e in range(window)] * 2,
                    axis=0,
                ).astype(bf16)
                dense = lax.dot_general(
                    values, select, contract_first, preferred_element_type=f32
                ).astype(bf16)
                out_ref[block, :128, :] = dense[:128]
                out_ref[block, 128:, :] = dense[128 + upper * rest : 128 + (upper + 1) * rest]


def swap(value):
    return lax.ppermute(value, "c", [(0, 1), (1, 0)])


def gather_weights(gate, up):
    n_x = lax.axis_size("x")
    ahead = [(i, (i + 1) % n_x) for i in range(n_x)]
    behind = [(i, (i - 1) % n_x) for i in range(n_x)]
    gate_before = lax.ppermute(gate, "x", ahead)
    up_after = lax.ppermute(up, "x", behind)
    up_before = lax.ppermute(up, "x", ahead)
    gate_after = lax.ppermute(gate, "x", behind)
    gate_before, up_after, up_before, gate_after = lax.optimization_barrier(
        (gate_before, up_after, up_before, gate_after)
    )
    gate_across = lax.ppermute(gate_before, "x", ahead)
    up_across = lax.ppermute(up_after, "x", behind)
    far = (swap(gate), swap(up))
    near = [(gate_before, up_before), (gate_after, up_after), (gate_across, up_across)]
    swapped = [(swap(a), swap(b)) for a, b in near]
    return [(gate, up), far, near[0], near[1], swapped[0], swapped[1], near[2], swapped[2]]


def per_device(tokens, cotangent, experts, route_weight, gate_weight, up_weight, down_weight):
    n_high = lax.axis_size("zh")
    n_z = n_high * lax.axis_size("zl")
    n_x = lax.axis_size("x")
    n_s = n_x * lax.axis_size("c")
    count, feats = tokens.shape
    quarter = feats // window
    part = count // 2 // n_s
    gate, up, down = gate_weight[0], up_weight[0], down_weight[0]
    hidden = gate.shape[1]
    x, core, expert_id = (
        lax.axis_index(name).reshape(1).astype(jnp.int32) for name in ("x", "c", "y")
    )
    smem, vmem, anywhere = pltpu.SMEM, pltpu.VMEM, pl.ANY
    half = feats // 2
    groups = 2 * n_s + 1

    pieces, keep, send, table = kernel_call(
        prep_kernel,
        (
            jax.ShapeDtypeStruct((n_s, 2 * part, half), bf16),
            jax.ShapeDtypeStruct((n_s // 2, 2 * part, half), bf16),
            jax.ShapeDtypeStruct((n_s // 2, 2 * part, half), bf16),
            jax.ShapeDtypeStruct((1, table_rows, half), bf16),
        ),
        [smem] * 2 + [vmem] * 4,
    )(expert_id, core, experts.T, route_weight.T, tokens, cotangent)
    down, pieces = lax.optimization_barrier((down, pieces))
    pieces = lax.all_to_all(pieces, ("x", "c"), 0, 0, tiled=True)
    down_t = kernel_call(flip_kernel, jax.ShapeDtypeStruct((feats, hidden), bf16), [vmem])(down)
    pieces, down_t = lax.optimization_barrier((pieces, down_t))
    own = kernel_call(
        pack_kernel,
        jax.ShapeDtypeStruct((groups, 2 * part, half), bf16),
        [anywhere] * 4,
        [pltpu.SemaphoreType.DMA((4,))],
        anywhere,
        small_vmem_bytes,
    )(pieces, keep, swap(send), table)
    gate, up, own = lax.optimization_barrier((gate, up, own))
    rows = lax.all_gather(own.reshape(-1, half), ("zh", "zl"), axis=0, tiled=True).reshape(
        n_z, groups, 2 * part, half
    )
    weights = [value for block in gather_weights(gate, up) for value in block]
    down_far = swap(down_t)

    back = kernel_call(
        back_kernel,
        jax.ShapeDtypeStruct((n_x, n_z * part, hidden), bf16),
        [anywhere] * 3,
        [
            pltpu.VMEM((2, n_z, n_s // 2, 2 * part, half), bf16),
            pltpu.VMEM((feats, hidden), bf16),
            pltpu.VMEM((feats, hidden), bf16),
            pltpu.SemaphoreType.DMA((4,)),
        ],
    )(rows, down_t, down_far)
    back = lax.all_to_all(back, "x", 0, 0, tiled=True)
    sums = kernel_call(
        products_kernel,
        jax.ShapeDtypeStruct((n_z * part, 2 * hidden), f32),
        [smem] * 2 + [anywhere] * (1 + len(weights)),
        [
            pltpu.VMEM((n_z, n_s, 2 * part, half), bf16),
            pltpu.VMEM((len(blocks_at), 2, feats, hidden), bf16),
            pltpu.SemaphoreType.DMA((len(weights) + 1,)),
        ],
        vmem_limit=late_vmem_bytes,
    )(x, core, rows, *weights)
    result_shape = (n_s, window, 2, quarter // 2, n_z * part)
    result = kernel_call(
        result_kernel,
        jax.ShapeDtypeStruct(result_shape, bf16),
        [smem] * 2 + [vmem] * 2 + [anywhere] * len(weights),
        [
            pltpu.VMEM((len(blocks_at), 2, feats, hidden), bf16),
            pltpu.VMEM(result_shape, bf16),
            pltpu.SemaphoreType.DMA((len(weights),)),
            pltpu.SemaphoreType.DMA((len(blocks_at),)),
        ],
        anywhere,
        late_vmem_bytes,
    )(x, core, sums, back, *weights)
    tables = lax.dynamic_index_in_dim(
        rows.reshape(n_high, 2, groups, 2 * part, half)[:, :, groups - 1, :, :count],
        lax.axis_index("zl"),
        axis=1,
        keepdims=False,
    )
    shape = result.shape
    result = lax.all_to_all(
        result.reshape(n_s * window * 2, *shape[3:]), ("x", "c", "y", "zl"), 0, 0, tiled=True
    ).reshape(shape)
    dense = kernel_call(
        combine_kernel,
        jax.ShapeDtypeStruct((n_high, quarter, count), bf16),
        [vmem] * 2,
        vmem_limit=small_vmem_bytes,
    )(tables, result)
    dense = lax.all_to_all(dense, "zh", 0, 0, tiled=True)
    return jnp.sum(dense.astype(f32), axis=0).astype(bf16).T


def solution(mesh):
    split = Mesh(
        mesh.devices.reshape(mesh.shape["seq"] // 2, 2, mesh.shape["etp"] // 2, 2, -1),
        ("zh", "zl", "x", "c", "y"),
    )
    seq, etp = ("zh", "zl"), ("x", "c")
    placed = (
        P(seq, etp),
        P(seq, etp),
        P(seq, None),
        P(seq, None),
        P("y", etp, seq),
        P("y", etp, seq),
        P("y", seq, etp),
    )
    return jax.shard_map(
        per_device, mesh=split, in_specs=placed, out_specs=P(seq, ("x", "c", "y")), check_vma=False
    )
```

```python
import jax
import jax.numpy as jnp
from jax import lax
from jax.experimental import pallas as pl
from jax.experimental.pallas import tpu as pltpu
from jax.sharding import Mesh
from jax.sharding import PartitionSpec as P

unit_scale = 1.0 / 65536.0
window = 4
table_rows = 16
bf16 = jnp.bfloat16
f32 = jnp.float32
contract_last = (((1,), (1,)), ((), ()))
contract_first = (((0,), (0,)), ((), ()))
vmem_bytes = 56 * 1024 * 1024
late_vmem_bytes = 52 * 1024 * 1024
result_vmem_bytes = 50 * 1024 * 1024
small_vmem_bytes = 16 * 1024 * 1024
blocks_at = ((0, 0), (0, 1), (-1, 0), (1, 0), (-1, 1), (1, 1), (2, 0), (2, 1))


def kernel_call(
    body, out_shape, spaces, scratch=(), out_space=pltpu.VMEM, vmem_limit=vmem_bytes
):
    return pl.pallas_call(
        body,
        out_shape=out_shape,
        in_specs=[pl.BlockSpec(memory_space=space) for space in spaces],
        out_specs=jax.tree.map(lambda _: pl.BlockSpec(memory_space=out_space), out_shape),
        scratch_shapes=list(scratch),
        compiler_params=pltpu.CompilerParams(vmem_limit_bytes=vmem_limit),
    )


def prep_kernel(
    expert_ref,
    core_ref,
    experts_ref,
    weight_ref,
    tok_ref,
    cot_ref,
    tok_out_ref,
    keep_ref,
    send_ref,
    table_ref,
):
    expert_id, core = expert_ref[0], core_ref[0]
    n_dest, both, half = tok_out_ref.shape
    part = both // 2
    count = tok_ref.shape[0]
    first, second = experts_ref[0:1, :], experts_ref[1:2, :]
    ids = lax.broadcasted_iota(jnp.int32, (window, count), 0)
    named = (first == ids) | (second == ids)
    before = lax.broadcasted_iota(jnp.int32, (count, count), 0) <= lax.broadcasted_iota(
        jnp.int32, (count, count), 1
    )
    order = jnp.dot(
        jnp.where(named, 1.0, 0.0).astype(bf16),
        jnp.where(before, 1.0, 0.0).astype(bf16),
        preferred_element_type=f32,
    )
    table = jnp.where(named, order - 1.0, -1.0)
    own = jnp.sum(jnp.where(ids == expert_id, table, 0.0), axis=0, keepdims=True)
    share = (
        jnp.where(first == expert_id, weight_ref[0:1, :], 0)
        + jnp.where(second == expert_id, weight_ref[1:2, :], 0)
    ).astype(f32) * unit_scale
    slot = lax.broadcasted_iota(jnp.int32, (n_dest * part, count), 0).astype(f32)
    hit = own == slot
    select = jnp.where(hit, 1.0, 0.0).astype(bf16)
    slot_share = jnp.sum(jnp.where(hit, share, 0.0), axis=1, keepdims=True)
    tok = jnp.dot(select, tok_ref[...], preferred_element_type=f32)
    cot = slot_share * jnp.dot(select, cot_ref[...], preferred_element_type=f32)
    for d in range(n_dest):
        rows = tok[d * part : (d + 1) * part]
        tok_out_ref[d] = jnp.concatenate([rows[:, :half], rows[:, half:]], axis=0).astype(bf16)
    sets = [
        jnp.concatenate(
            [cot[d * part : (d + 1) * part] for d in range(side, n_dest, 2)], axis=0
        )
        for side in range(2)
    ]
    mine = jnp.where(core == 0, sets[0], sets[1]).astype(bf16)
    other = jnp.where(core == 0, sets[1], sets[0]).astype(bf16)
    for h in range(2):
        for i in range(2):
            span = slice(i * both, (i + 1) * both)
            keep_ref[2 * h + i] = mine[span, h * half : (h + 1) * half]
            send_ref[2 * h + i] = other[span, h * half : (h + 1) * half]
    padded = jnp.concatenate([table, jnp.zeros((table_rows - window, count), f32)], axis=0)
    table_ref[0] = jnp.concatenate(
        [padded, jnp.zeros((table_rows, half - count), f32)], axis=1
    ).astype(bf16)


def pack_kernel(tok_ref, keep_ref, far_ref, table_ref, out_ref, sems):
    begin, copies = 0, []
    for i, ref in enumerate((tok_ref, keep_ref, far_ref, table_ref)):
        size = ref.shape[0]
        copies.append(pltpu.make_async_copy(ref, out_ref.at[pl.ds(begin, size)], sems.at[i]))
        copies[-1].start()
        begin += size
    for copy in copies:
        copy.wait()


def flip_kernel(in_ref, out_ref):
    out_ref[...] = in_ref[...].T


def source(x_ref, core_ref, n_x, dx, dc):
    x, core = x_ref[0], core_ref[0]
    return lax.rem(x + dx + n_x, n_x) * 2 + (1 - core if dc else core)


def back_kernel(rows_hbm, near_hbm, far_hbm, out_ref, rows_ref, near_ref, far_ref, sems):
    n_x, slots, hidden = out_ref.shape
    n_z, sub, half = rows_ref.shape[1:2] + rows_ref.shape[3:]
    per_z = 2 * sub
    copies = []
    for side, (weight_hbm, weight_ref) in enumerate(((near_hbm, near_ref), (far_hbm, far_ref))):
        at = 8 + 4 * side
        copies.append(
            pltpu.make_async_copy(
                rows_hbm.at[:, pl.ds(at, 4)], rows_ref.at[side], sems.at[2 * side]
            )
        )
        copies.append(pltpu.make_async_copy(weight_hbm, weight_ref, sems.at[2 * side + 1]))
    for copy in copies:
        copy.start()
    total = None
    for side, weight_ref in enumerate((near_ref, far_ref)):
        copies[2 * side].wait()
        copies[2 * side + 1].wait()
        for h in range(2):
            rows = rows_ref[side, :, 2 * h : 2 * h + 2].reshape(n_z * per_z, half)
            term = jnp.dot(
                rows, weight_ref[h * half : (h + 1) * half, :], preferred_element_type=f32
            )
            total = term if total is None else total + term
    total = total.reshape(n_z, n_x, slots // n_z, hidden)
    for i in range(n_x):
        out_ref[i] = total[:, i].reshape(slots, hidden).astype(bf16)


def start_weights(weights_hbm, weights_ref, sems):
    copies = [
        pltpu.make_async_copy(w, weights_ref.at[i // 2, i % 2], sems.at[i])
        for i, w in enumerate(weights_hbm)
    ]
    for copy in copies:
        copy.start()
    return copies


def products_kernel(x_ref, core_ref, *refs):
    n_w = 2 * len(blocks_at)
    rows_hbm, weights_hbm = refs[0], refs[1 : 1 + n_w]
    total_ref, rows_ref, weights_ref, sems = refs[1 + n_w :]
    n_z, n_s, both, half = rows_ref.shape
    part = both // 2
    hidden = weights_ref.shape[-1]
    rows_copy = pltpu.make_async_copy(rows_hbm.at[:, pl.ds(0, n_s)], rows_ref, sems.at[n_w])
    rows_copy.start()
    copies = start_weights(weights_hbm, weights_ref, sems)
    rows_copy.wait()
    for b, (dx, dc) in enumerate(blocks_at):
        copies[2 * b].wait()
        copies[2 * b + 1].wait()
        loaded = rows_ref[:, source(x_ref, core_ref, n_s // 2, dx, dc)].astype(f32)
        low, high = (
            loaded[:, begin : begin + part].reshape(n_z * part, half).astype(bf16)
            for begin in (0, part)
        )
        for m in range(2):
            span = slice(m * hidden, (m + 1) * hidden)
            term = jnp.dot(low, weights_ref[b, m, :half], preferred_element_type=f32)
            term += jnp.dot(high, weights_ref[b, m, half:], preferred_element_type=f32)
            if b == 0:
                total_ref[:, span] = term
            else:
                total_ref[:, span] += term


def result_kernel(x_ref, core_ref, *refs):
    n_w = 2 * len(blocks_at)
    sums_ref, back_ref, weights_hbm = refs[0], refs[1], refs[2 : 2 + n_w]
    out_hbm, weights_ref, out_ref, sems, out_sems = refs[2 + n_w :]
    n_x, slots, hidden = back_ref.shape
    feats = weights_ref.shape[2]
    half = feats // 2
    n_z = slots // 8
    copies = start_weights(weights_hbm, weights_ref, sems)

    back = sum(back_ref[i].astype(f32) for i in range(n_x))
    gate_sum, up_sum, back_sum = (
        jnp.concatenate(
            [
                value.reshape(n_z // 2, 2, 8, hidden)[:, pair].reshape(slots // 2, hidden)
                for pair in range(2)
            ],
            axis=0,
        )
        for value in (sums_ref[:, :hidden], sums_ref[:, hidden:], back)
    )
    sigmoid_gate = jax.nn.sigmoid(gate_sum)
    grad_up = (back_sum * (gate_sum * sigmoid_gate)).astype(bf16)
    grad_gate = (
        back_sum * up_sum * sigmoid_gate * (1.0 + gate_sum * (1.0 - sigmoid_gate))
    ).astype(bf16)

    quarter = feats // window
    sent = []
    for b, (dx, dc) in enumerate(blocks_at):
        s = source(x_ref, core_ref, n_x, dx, dc)
        copies[2 * b].wait()
        copies[2 * b + 1].wait()
        wide = [
            lax.dot_general(
                grad_gate, weights_ref[b, 0, span], contract_last, preferred_element_type=f32
            )
            + lax.dot_general(
                grad_up, weights_ref[b, 1, span], contract_last, preferred_element_type=f32
            )
            for span in (slice(0, half), slice(half, feats))
        ]
        for y in range(window):
            begin = y * quarter % half
            rows = wide[y * quarter // half][:, begin : begin + quarter]
            for pair in range(2):
                mine = rows[pair * slots // 2 : (pair + 1) * slots // 2]
                out_ref[s, y, pair, : slots // 2, :] = mine[:, :128].astype(bf16)
                out_ref[s, y, pair, slots // 2 :, :] = jnp.concatenate(
                    [mine[: slots // 4, 128:], mine[slots // 4 :, 128:]], axis=1
                ).astype(bf16)
        sent.append(pltpu.make_async_copy(out_ref.at[s], out_hbm.at[s], out_sems.at[b]))
        sent[-1].start()
    for copy in sent:
        copy.wait()


def combine_kernel(table_ref, rows_ref, out_ref):
    n_blocks, quarter, count = out_ref.shape
    n_d = rows_ref.shape[0]
    part = 64 // n_d
    slots = n_blocks * part
    rest = quarter - 128
    slot = lax.broadcasted_iota(jnp.int32, (n_d * part, count), 0).astype(f32)
    sources = [(d, e, pair) for pair in range(2) for e in range(window) for d in range(n_d)]
    for p in range(n_blocks // 4):
        begin = 2 * part * p
        tails = [
            rows_ref[(*source, slice(slots + begin, slots + begin + 2 * part))].astype(f32)
            for source in sources
        ]
        for upper in range(2):
            at = upper * slots // 2 + begin
            heads = [
                rows_ref[(*source, slice(at, at + 2 * part))].astype(f32) for source in sources
            ]
            for j in range(2):
                block = upper * n_blocks // 2 + 2 * p + j
                span = slice(j * part, (j + 1) * part)
                values = jnp.concatenate(
                    [
                        jnp.concatenate([v[span] for v in heads], axis=0),
                        jnp.concatenate([v[span] for v in tails], axis=0),
                    ],
                    axis=1,
                ).astype(bf16)
                table = table_ref[block].astype(f32)
                select = jnp.concatenate(
                    [jnp.where(table[e : e + 1] == slot, 1.0, 0.0) for e in range(window)] * 2,
                    axis=0,
                ).astype(bf16)
                dense = lax.dot_general(
                    values, select, contract_first, preferred_element_type=f32
                ).astype(bf16)
                out_ref[block, :128, :] = dense[:128]
                out_ref[block, 128:, :] = dense[128 + upper * rest : 128 + (upper + 1) * rest]


def swap(value):
    return lax.ppermute(value, "c", [(0, 1), (1, 0)])


def gather_weights(gate, up):
    n_x = lax.axis_size("x")
    ahead = [(i, (i + 1) % n_x) for i in range(n_x)]
    behind = [(i, (i - 1) % n_x) for i in range(n_x)]
    gate_before = lax.ppermute(gate, "x", ahead)
    up_after = lax.ppermute(up, "x", behind)
    up_before = lax.ppermute(up, "x", ahead)
    gate_after = lax.ppermute(gate, "x", behind)
    gate_before, up_after, up_before, gate_after = lax.optimization_barrier(
        (gate_before, up_after, up_before, gate_after)
    )
    gate_across = lax.ppermute(gate_before, "x", ahead)
    up_across = lax.ppermute(up_after, "x", behind)
    far = (swap(gate), swap(up))
    near = [(gate_before, up_before), (gate_after, up_after), (gate_across, up_across)]
    swapped = [(swap(a), swap(b)) for a, b in near]
    return [(gate, up), far, near[0], near[1], swapped[0], swapped[1], near[2], swapped[2]]


def per_device(tokens, cotangent, experts, route_weight, gate_weight, up_weight, down_weight):
    n_high = lax.axis_size("zh")
    n_z = n_high * lax.axis_size("zl")
    n_x = lax.axis_size("x")
    n_s = n_x * lax.axis_size("c")
    count, feats = tokens.shape
    quarter = feats // window
    part = count // 2 // n_s
    gate, up, down = gate_weight[0], up_weight[0], down_weight[0]
    hidden = gate.shape[1]
    x, core, expert_id = (
        lax.axis_index(name).reshape(1).astype(jnp.int32) for name in ("x", "c", "y")
    )
    smem, vmem, anywhere = pltpu.SMEM, pltpu.VMEM, pl.ANY
    half = feats // 2
    groups = 2 * n_s + 1

    pieces, keep, send, table = kernel_call(
        prep_kernel,
        (
            jax.ShapeDtypeStruct((n_s, 2 * part, half), bf16),
            jax.ShapeDtypeStruct((n_s // 2, 2 * part, half), bf16),
            jax.ShapeDtypeStruct((n_s // 2, 2 * part, half), bf16),
            jax.ShapeDtypeStruct((1, table_rows, half), bf16),
        ),
        [smem] * 2 + [vmem] * 4,
    )(expert_id, core, experts.T, route_weight.T, tokens, cotangent)
    down, pieces = lax.optimization_barrier((down, pieces))
    pieces = lax.all_to_all(pieces, ("x", "c"), 0, 0, tiled=True)
    down_t = kernel_call(flip_kernel, jax.ShapeDtypeStruct((feats, hidden), bf16), [vmem])(down)
    pieces, down_t = lax.optimization_barrier((pieces, down_t))
    own = kernel_call(
        pack_kernel,
        jax.ShapeDtypeStruct((groups, 2 * part, half), bf16),
        [anywhere] * 4,
        [pltpu.SemaphoreType.DMA((4,))],
        anywhere,
        small_vmem_bytes,
    )(pieces, keep, swap(send), table)
    gate, up, own = lax.optimization_barrier((gate, up, own))
    rows = lax.all_gather(own.reshape(-1, half), ("zh", "zl"), axis=0, tiled=True).reshape(
        n_z, groups, 2 * part, half
    )
    weights = [value for block in gather_weights(gate, up) for value in block]
    down_far = swap(down_t)

    back = kernel_call(
        back_kernel,
        jax.ShapeDtypeStruct((n_x, n_z * part, hidden), bf16),
        [anywhere] * 3,
        [
            pltpu.VMEM((2, n_z, n_s // 2, 2 * part, half), bf16),
            pltpu.VMEM((feats, hidden), bf16),
            pltpu.VMEM((feats, hidden), bf16),
            pltpu.SemaphoreType.DMA((4,)),
        ],
    )(rows, down_t, down_far)
    back = lax.all_to_all(back, "x", 0, 0, tiled=True)
    sums = kernel_call(
        products_kernel,
        jax.ShapeDtypeStruct((n_z * part, 2 * hidden), f32),
        [smem] * 2 + [anywhere] * (1 + len(weights)),
        [
            pltpu.VMEM((n_z, n_s, 2 * part, half), bf16),
            pltpu.VMEM((len(blocks_at), 2, feats, hidden), bf16),
            pltpu.SemaphoreType.DMA((len(weights) + 1,)),
        ],
        vmem_limit=late_vmem_bytes,
    )(x, core, rows, *weights)
    result_shape = (n_s, window, 2, quarter // 2, n_z * part)
    result = kernel_call(
        result_kernel,
        jax.ShapeDtypeStruct(result_shape, bf16),
        [smem] * 2 + [vmem] * 2 + [anywhere] * len(weights),
        [
            pltpu.VMEM((len(blocks_at), 2, feats, hidden), bf16),
            pltpu.VMEM(result_shape, bf16),
            pltpu.SemaphoreType.DMA((len(weights),)),
            pltpu.SemaphoreType.DMA((len(blocks_at),)),
        ],
        anywhere,
        result_vmem_bytes,
    )(x, core, sums, back, *weights)
    tables = lax.dynamic_index_in_dim(
        rows.reshape(n_high, 2, groups, 2 * part, half)[:, :, groups - 1, :, :count],
        lax.axis_index("zl"),
        axis=1,
        keepdims=False,
    )
    shape = result.shape
    result = lax.all_to_all(
        result.reshape(n_s * window * 2, *shape[3:]), ("x", "c", "y", "zl"), 0, 0, tiled=True
    ).reshape(shape)
    dense = kernel_call(
        combine_kernel,
        jax.ShapeDtypeStruct((n_high, quarter, count), bf16),
        [vmem] * 2,
        vmem_limit=small_vmem_bytes,
    )(tables, result)
    dense = lax.all_to_all(dense, "zh", 0, 0, tiled=True)
    return jnp.sum(dense.astype(f32), axis=0).astype(bf16).T


def solution(mesh):
    split = Mesh(
        mesh.devices.reshape(mesh.shape["seq"] // 2, 2, mesh.shape["etp"] // 2, 2, -1),
        ("zh", "zl", "x", "c", "y"),
    )
    seq, etp = ("zh", "zl"), ("x", "c")
    placed = (
        P(seq, etp),
        P(seq, etp),
        P(seq, None),
        P(seq, None),
        P("y", etp, seq),
        P("y", etp, seq),
        P("y", seq, etp),
    )
    return jax.shard_map(
        per_device, mesh=split, in_specs=placed, out_specs=P(seq, ("x", "c", "y")), check_vma=False
    )
```

```python
import jax
import jax.numpy as jnp
from jax import lax
from jax.experimental import pallas as pl
from jax.experimental.pallas import tpu as pltpu
from jax.sharding import Mesh
from jax.sharding import PartitionSpec as P

unit_scale = 1.0 / 65536.0
window = 4
table_rows = 16
bf16 = jnp.bfloat16
f32 = jnp.float32
contract_last = (((1,), (1,)), ((), ()))
contract_first = (((0,), (0,)), ((), ()))
vmem_bytes = 56 * 1024 * 1024
late_vmem_bytes = 52 * 1024 * 1024
result_vmem_bytes = 50 * 1024 * 1024
small_vmem_bytes = 16 * 1024 * 1024
blocks_at = ((0, 0), (0, 1), (-1, 0), (1, 0), (-1, 1), (1, 1), (2, 0), (2, 1))


def kernel_call(
    body, out_shape, spaces, scratch=(), out_space=pltpu.VMEM, vmem_limit=vmem_bytes
):
    return pl.pallas_call(
        body,
        out_shape=out_shape,
        in_specs=[pl.BlockSpec(memory_space=space) for space in spaces],
        out_specs=jax.tree.map(lambda _: pl.BlockSpec(memory_space=out_space), out_shape),
        scratch_shapes=list(scratch),
        compiler_params=pltpu.CompilerParams(vmem_limit_bytes=vmem_limit),
    )


def prep_kernel(
    expert_ref,
    core_ref,
    experts_ref,
    weight_ref,
    tok_hbm,
    cot_hbm,
    tok_out_ref,
    keep_ref,
    send_ref,
    table_ref,
    tok_ref,
    cot_ref,
    sems,
):
    tok_copy = pltpu.make_async_copy(tok_hbm, tok_ref, sems.at[0])
    cot_copy = pltpu.make_async_copy(cot_hbm, cot_ref, sems.at[1])
    tok_copy.start()
    cot_copy.start()
    expert_id, core = expert_ref[0], core_ref[0]
    n_dest, both, half = tok_out_ref.shape
    part = both // 2
    count = tok_ref.shape[0]
    first, second = experts_ref[0:1, :], experts_ref[1:2, :]
    ids = lax.broadcasted_iota(jnp.int32, (window, count), 0)
    named = (first == ids) | (second == ids)
    before = lax.broadcasted_iota(jnp.int32, (count, count), 0) <= lax.broadcasted_iota(
        jnp.int32, (count, count), 1
    )
    order = jnp.dot(
        jnp.where(named, 1.0, 0.0).astype(bf16),
        jnp.where(before, 1.0, 0.0).astype(bf16),
        preferred_element_type=f32,
    )
    table = jnp.where(named, order - 1.0, -1.0)
    own = jnp.sum(jnp.where(ids == expert_id, table, 0.0), axis=0, keepdims=True)
    share = (
        jnp.where(first == expert_id, weight_ref[0:1, :], 0)
        + jnp.where(second == expert_id, weight_ref[1:2, :], 0)
    ).astype(f32) * unit_scale
    slot = lax.broadcasted_iota(jnp.int32, (n_dest * part, count), 0).astype(f32)
    hit = own == slot
    select = jnp.where(hit, 1.0, 0.0).astype(bf16)
    slot_share = jnp.sum(jnp.where(hit, share, 0.0), axis=1, keepdims=True)
    tok_copy.wait()
    cot_copy.wait()
    tok = jnp.dot(select, tok_ref[...], preferred_element_type=f32)
    cot = slot_share * jnp.dot(select, cot_ref[...], preferred_element_type=f32)
    for d in range(n_dest):
        rows = tok[d * part : (d + 1) * part]
        tok_out_ref[d] = jnp.concatenate([rows[:, :half], rows[:, half:]], axis=0).astype(bf16)
    sets = [
        jnp.concatenate(
            [cot[d * part : (d + 1) * part] for d in range(side, n_dest, 2)], axis=0
        )
        for side in range(2)
    ]
    mine = jnp.where(core == 0, sets[0], sets[1]).astype(bf16)
    other = jnp.where(core == 0, sets[1], sets[0]).astype(bf16)
    for h in range(2):
        for i in range(2):
            span = slice(i * both, (i + 1) * both)
            keep_ref[2 * h + i] = mine[span, h * half : (h + 1) * half]
            send_ref[2 * h + i] = other[span, h * half : (h + 1) * half]
    padded = jnp.concatenate([table, jnp.zeros((table_rows - window, count), f32)], axis=0)
    table_ref[0] = jnp.concatenate(
        [padded, jnp.zeros((table_rows, half - count), f32)], axis=1
    ).astype(bf16)


def pack_kernel(tok_ref, keep_ref, far_ref, table_ref, out_ref, sems):
    begin, copies = 0, []
    for i, ref in enumerate((tok_ref, keep_ref, far_ref, table_ref)):
        size = ref.shape[0]
        copies.append(pltpu.make_async_copy(ref, out_ref.at[pl.ds(begin, size)], sems.at[i]))
        copies[-1].start()
        begin += size
    for copy in copies:
        copy.wait()


def flip_kernel(in_ref, out_ref):
    out_ref[...] = in_ref[...].T


def source(x_ref, core_ref, n_x, dx, dc):
    x, core = x_ref[0], core_ref[0]
    return lax.rem(x + dx + n_x, n_x) * 2 + (1 - core if dc else core)


def back_kernel(rows_hbm, near_hbm, far_hbm, out_ref, rows_ref, near_ref, far_ref, sems):
    n_x, slots, hidden = out_ref.shape
    n_z, sub, half = rows_ref.shape[1:2] + rows_ref.shape[3:]
    per_z = 2 * sub
    copies = []
    for side, (weight_hbm, weight_ref) in enumerate(((near_hbm, near_ref), (far_hbm, far_ref))):
        at = 8 + 4 * side
        copies.append(
            pltpu.make_async_copy(
                rows_hbm.at[:, pl.ds(at, 4)], rows_ref.at[side], sems.at[2 * side]
            )
        )
        copies.append(pltpu.make_async_copy(weight_hbm, weight_ref, sems.at[2 * side + 1]))
    for copy in copies:
        copy.start()
    total = None
    for side, weight_ref in enumerate((near_ref, far_ref)):
        copies[2 * side].wait()
        copies[2 * side + 1].wait()
        for h in range(2):
            rows = rows_ref[side, :, 2 * h : 2 * h + 2].reshape(n_z * per_z, half)
            term = jnp.dot(
                rows, weight_ref[h * half : (h + 1) * half, :], preferred_element_type=f32
            )
            total = term if total is None else total + term
    total = total.reshape(n_z, n_x, slots // n_z, hidden)
    for i in range(n_x):
        out_ref[i] = total[:, i].reshape(slots, hidden).astype(bf16)


def start_weights(weights_hbm, weights_ref, sems):
    copies = [
        pltpu.make_async_copy(w, weights_ref.at[i // 2, i % 2], sems.at[i])
        for i, w in enumerate(weights_hbm)
    ]
    for copy in copies:
        copy.start()
    return copies


def products_kernel(x_ref, core_ref, *refs):
    n_w = 2 * len(blocks_at)
    rows_hbm, weights_hbm = refs[0], refs[1 : 1 + n_w]
    total_ref, rows_ref, weights_ref, sems = refs[1 + n_w :]
    n_z, n_s, both, half = rows_ref.shape
    part = both // 2
    hidden = weights_ref.shape[-1]
    rows_copy = pltpu.make_async_copy(rows_hbm.at[:, pl.ds(0, n_s)], rows_ref, sems.at[n_w])
    rows_copy.start()
    copies = start_weights(weights_hbm, weights_ref, sems)
    rows_copy.wait()
    for b, (dx, dc) in enumerate(blocks_at):
        copies[2 * b].wait()
        copies[2 * b + 1].wait()
        loaded = rows_ref[:, source(x_ref, core_ref, n_s // 2, dx, dc)].astype(f32)
        low, high = (
            loaded[:, begin : begin + part].reshape(n_z * part, half).astype(bf16)
            for begin in (0, part)
        )
        for m in range(2):
            span = slice(m * hidden, (m + 1) * hidden)
            term = jnp.dot(low, weights_ref[b, m, :half], preferred_element_type=f32)
            term += jnp.dot(high, weights_ref[b, m, half:], preferred_element_type=f32)
            if b == 0:
                total_ref[:, span] = term
            else:
                total_ref[:, span] += term


def result_kernel(x_ref, core_ref, *refs):
    n_w = 2 * len(blocks_at)
    sums_ref, back_ref, weights_hbm = refs[0], refs[1], refs[2 : 2 + n_w]
    out_hbm, weights_ref, out_ref, sems, out_sems = refs[2 + n_w :]
    n_x, slots, hidden = back_ref.shape
    feats = weights_ref.shape[2]
    half = feats // 2
    n_z = slots // 8
    copies = start_weights(weights_hbm, weights_ref, sems)

    back = sum(back_ref[i].astype(f32) for i in range(n_x))
    gate_sum, up_sum, back_sum = (
        jnp.concatenate(
            [
                value.reshape(n_z // 2, 2, 8, hidden)[:, pair].reshape(slots // 2, hidden)
                for pair in range(2)
            ],
            axis=0,
        )
        for value in (sums_ref[:, :hidden], sums_ref[:, hidden:], back)
    )
    sigmoid_gate = jax.nn.sigmoid(gate_sum)
    grad_up = (back_sum * (gate_sum * sigmoid_gate)).astype(bf16)
    grad_gate = (
        back_sum * up_sum * sigmoid_gate * (1.0 + gate_sum * (1.0 - sigmoid_gate))
    ).astype(bf16)

    quarter = feats // window
    sent = []
    for b, (dx, dc) in enumerate(blocks_at):
        s = source(x_ref, core_ref, n_x, dx, dc)
        copies[2 * b].wait()
        copies[2 * b + 1].wait()
        wide = [
            lax.dot_general(
                grad_gate, weights_ref[b, 0, span], contract_last, preferred_element_type=f32
            )
            + lax.dot_general(
                grad_up, weights_ref[b, 1, span], contract_last, preferred_element_type=f32
            )
            for span in (slice(0, half), slice(half, feats))
        ]
        for y in range(window):
            begin = y * quarter % half
            rows = wide[y * quarter // half][:, begin : begin + quarter]
            for pair in range(2):
                mine = rows[pair * slots // 2 : (pair + 1) * slots // 2]
                out_ref[s, y, pair, : slots // 2, :] = mine[:, :128].astype(bf16)
                out_ref[s, y, pair, slots // 2 :, :] = jnp.concatenate(
                    [mine[: slots // 4, 128:], mine[slots // 4 :, 128:]], axis=1
                ).astype(bf16)
        sent.append(pltpu.make_async_copy(out_ref.at[s], out_hbm.at[s], out_sems.at[b]))
        sent[-1].start()
    for copy in sent:
        copy.wait()


def combine_kernel(table_ref, rows_ref, out_ref):
    n_blocks, quarter, count = out_ref.shape
    n_d = rows_ref.shape[0]
    part = 64 // n_d
    slots = n_blocks * part
    rest = quarter - 128
    slot = lax.broadcasted_iota(jnp.int32, (n_d * part, count), 0).astype(f32)
    sources = [(d, e, pair) for pair in range(2) for e in range(window) for d in range(n_d)]
    for p in range(n_blocks // 4):
        begin = 2 * part * p
        tails = [
            rows_ref[(*source, slice(slots + begin, slots + begin + 2 * part))].astype(f32)
            for source in sources
        ]
        for upper in range(2):
            at = upper * slots // 2 + begin
            heads = [
                rows_ref[(*source, slice(at, at + 2 * part))].astype(f32) for source in sources
            ]
            for j in range(2):
                block = upper * n_blocks // 2 + 2 * p + j
                span = slice(j * part, (j + 1) * part)
                values = jnp.concatenate(
                    [
                        jnp.concatenate([v[span] for v in heads], axis=0),
                        jnp.concatenate([v[span] for v in tails], axis=0),
                    ],
                    axis=1,
                ).astype(bf16)
                table = table_ref[block].astype(f32)
                select = jnp.concatenate(
                    [jnp.where(table[e : e + 1] == slot, 1.0, 0.0) for e in range(window)] * 2,
                    axis=0,
                ).astype(bf16)
                dense = lax.dot_general(
                    values, select, contract_first, preferred_element_type=f32
                ).astype(bf16)
                out_ref[block, :128, :] = dense[:128]
                out_ref[block, 128:, :] = dense[128 + upper * rest : 128 + (upper + 1) * rest]


def swap(value):
    return lax.ppermute(value, "c", [(0, 1), (1, 0)])


def gather_weights(gate, up):
    n_x = lax.axis_size("x")
    ahead = [(i, (i + 1) % n_x) for i in range(n_x)]
    behind = [(i, (i - 1) % n_x) for i in range(n_x)]
    gate_before = lax.ppermute(gate, "x", ahead)
    up_after = lax.ppermute(up, "x", behind)
    up_before = lax.ppermute(up, "x", ahead)
    gate_after = lax.ppermute(gate, "x", behind)
    gate_before, up_after, up_before, gate_after = lax.optimization_barrier(
        (gate_before, up_after, up_before, gate_after)
    )
    gate_across = lax.ppermute(gate_before, "x", ahead)
    up_across = lax.ppermute(up_after, "x", behind)
    far = (swap(gate), swap(up))
    near = [(gate_before, up_before), (gate_after, up_after), (gate_across, up_across)]
    swapped = [(swap(a), swap(b)) for a, b in near]
    return [(gate, up), far, near[0], near[1], swapped[0], swapped[1], near[2], swapped[2]]


def per_device(tokens, cotangent, experts, route_weight, gate_weight, up_weight, down_weight):
    n_high = lax.axis_size("zh")
    n_z = n_high * lax.axis_size("zl")
    n_x = lax.axis_size("x")
    n_s = n_x * lax.axis_size("c")
    count, feats = tokens.shape
    quarter = feats // window
    part = count // 2 // n_s
    gate, up, down = gate_weight[0], up_weight[0], down_weight[0]
    hidden = gate.shape[1]
    x, core, expert_id = (
        lax.axis_index(name).reshape(1).astype(jnp.int32) for name in ("x", "c", "y")
    )
    smem, vmem, anywhere = pltpu.SMEM, pltpu.VMEM, pl.ANY
    half = feats // 2
    groups = 2 * n_s + 1

    pieces, keep, send, table = kernel_call(
        prep_kernel,
        (
            jax.ShapeDtypeStruct((n_s, 2 * part, half), bf16),
            jax.ShapeDtypeStruct((n_s // 2, 2 * part, half), bf16),
            jax.ShapeDtypeStruct((n_s // 2, 2 * part, half), bf16),
            jax.ShapeDtypeStruct((1, table_rows, half), bf16),
        ),
        [smem] * 2 + [vmem] * 2 + [anywhere] * 2,
        [
            pltpu.VMEM((count, feats), bf16),
            pltpu.VMEM((count, feats), bf16),
            pltpu.SemaphoreType.DMA((2,)),
        ],
    )(expert_id, core, experts.T, route_weight.T, tokens, cotangent)
    down, pieces = lax.optimization_barrier((down, pieces))
    pieces = lax.all_to_all(pieces, ("x", "c"), 0, 0, tiled=True)
    down_t = kernel_call(flip_kernel, jax.ShapeDtypeStruct((feats, hidden), bf16), [vmem])(down)
    pieces, down_t = lax.optimization_barrier((pieces, down_t))
    own = kernel_call(
        pack_kernel,
        jax.ShapeDtypeStruct((groups, 2 * part, half), bf16),
        [anywhere] * 4,
        [pltpu.SemaphoreType.DMA((4,))],
        anywhere,
        small_vmem_bytes,
    )(pieces, keep, swap(send), table)
    gate, up, own = lax.optimization_barrier((gate, up, own))
    rows = lax.all_gather(own.reshape(-1, half), ("zh", "zl"), axis=0, tiled=True).reshape(
        n_z, groups, 2 * part, half
    )
    weights = [value for block in gather_weights(gate, up) for value in block]
    down_far = swap(down_t)

    back = kernel_call(
        back_kernel,
        jax.ShapeDtypeStruct((n_x, n_z * part, hidden), bf16),
        [anywhere] * 3,
        [
            pltpu.VMEM((2, n_z, n_s // 2, 2 * part, half), bf16),
            pltpu.VMEM((feats, hidden), bf16),
            pltpu.VMEM((feats, hidden), bf16),
            pltpu.SemaphoreType.DMA((4,)),
        ],
    )(rows, down_t, down_far)
    back = lax.all_to_all(back, "x", 0, 0, tiled=True)
    sums = kernel_call(
        products_kernel,
        jax.ShapeDtypeStruct((n_z * part, 2 * hidden), f32),
        [smem] * 2 + [anywhere] * (1 + len(weights)),
        [
            pltpu.VMEM((n_z, n_s, 2 * part, half), bf16),
            pltpu.VMEM((len(blocks_at), 2, feats, hidden), bf16),
            pltpu.SemaphoreType.DMA((len(weights) + 1,)),
        ],
        vmem_limit=late_vmem_bytes,
    )(x, core, rows, *weights)
    result_shape = (n_s, window, 2, quarter // 2, n_z * part)
    result = kernel_call(
        result_kernel,
        jax.ShapeDtypeStruct(result_shape, bf16),
        [smem] * 2 + [vmem] * 2 + [anywhere] * len(weights),
        [
            pltpu.VMEM((len(blocks_at), 2, feats, hidden), bf16),
            pltpu.VMEM(result_shape, bf16),
            pltpu.SemaphoreType.DMA((len(weights),)),
            pltpu.SemaphoreType.DMA((len(blocks_at),)),
        ],
        anywhere,
        result_vmem_bytes,
    )(x, core, sums, back, *weights)
    tables = lax.dynamic_index_in_dim(
        rows.reshape(n_high, 2, groups, 2 * part, half)[:, :, groups - 1, :, :count],
        lax.axis_index("zl"),
        axis=1,
        keepdims=False,
    )
    shape = result.shape
    result = lax.all_to_all(
        result.reshape(n_s * window * 2, *shape[3:]), ("x", "c", "y", "zl"), 0, 0, tiled=True
    ).reshape(shape)
    dense = kernel_call(
        combine_kernel,
        jax.ShapeDtypeStruct((n_high, quarter, count), bf16),
        [vmem] * 2,
        vmem_limit=small_vmem_bytes,
    )(tables, result)
    dense = lax.all_to_all(dense, "zh", 0, 0, tiled=True)
    return jnp.sum(dense.astype(f32), axis=0).astype(bf16).T


def solution(mesh):
    split = Mesh(
        mesh.devices.reshape(mesh.shape["seq"] // 2, 2, mesh.shape["etp"] // 2, 2, -1),
        ("zh", "zl", "x", "c", "y"),
    )
    seq, etp = ("zh", "zl"), ("x", "c")
    placed = (
        P(seq, etp),
        P(seq, etp),
        P(seq, None),
        P(seq, None),
        P("y", etp, seq),
        P("y", etp, seq),
        P("y", seq, etp),
    )
    return jax.shard_map(
        per_device, mesh=split, in_specs=placed, out_specs=P(seq, ("x", "c", "y")), check_vma=False
    )
```
